32 devices in a mesh: dp: 8 (over z, x), mp: 4 (over y, core).
Axes of the slice: x: 2, y: 2, z: 4, core: 2. Of those that a mesh axis runs over, the one named last changes fastest.
Arguments:
- inputs: bfloat16 [41472, 512], P(('dp', 'mp')), may hold values from -6 to 6
- counts: int32 [128], P('dp'), may hold values from 100 to 324, as said below
- input_norm_gain: float32 [512], replicated, may hold values from 0.5 to 1.5
- shift_in: float32 [512], replicated, may hold values from -1.75 to 1.75
- w_value: float32 [512, 1536], P('dp', 'mp'), may hold values from -0.25 to 0.25
- w_gate: float32 [512, 1536], P('dp', 'mp'), may hold values from -0.25 to 0.25
- bias_value: float32 [1536], P('mp'), may hold values from -1.75 to 1.75
- bias_gate: float32 [1536], P('mp'), may hold values from -1.75 to 1.75
- gate_gain: float32 [1536], P('mp'), may hold values from 0.5 to 1.5
- gate_shift: float32 [1536], P('mp'), may hold values from -1.75 to 1.75
- spatial: float32 [324, 324], replicated, may hold values from -0.3125 to 0.3125
- spatial_bias: float32 [324], replicated, may hold values from 0.5 to 1.5
- w_out: float32 [1536, 512], P('mp', 'dp'), may hold values from -0.3125 to 0.3125
- out_bias: float32 [512], replicated, may hold values from -1.75 to 1.75
- cotangent: bfloat16 [41472, 512], P(('dp', 'mp')), may hold values from -6 to 6
Outputs:
- result: bfloat16 [41472, 512], P(('dp', 'mp'))
- input_grad: float32 [41472, 512], P(('dp', 'mp'))
- grad_gain_in: float32 [512], replicated
- grad_shift_in: float32 [512], replicated
- grad_w_value: float32 [512, 1536], P('dp', 'mp')
- grad_w_gate: float32 [512, 1536], P('dp', 'mp')
- grad_bias_value: float32 [1536], P('mp')
- grad_bias_gate: float32 [1536], P('mp')
- grad_gate_gain: float32 [1536], P('mp')
- grad_gate_shift: float32 [1536], P('mp')
- grad_spatial: float32 [324, 324], replicated
- grad_spatial_bias: float32 [324], replicated
- grad_w_out: float32 [1536, 512], P('mp', 'dp')
- grad_out_bias: float32 [512], replicated
The draws below stay inside these ranges and needn't reach their ends.
Inputs may be any that keep to these rules, and one draw needn't show every extreme that they name: `counts`: each entry is 100, 196 or 324; rows of an image beyond its count are padding slots. Each aligned group of 16 images holds at least one image of 324 patches.
All inputs are finite; a program needn't handle non-finite values.
Results may differ from the reference program's by a relative error of at most 0.0098.
Values may be sent and summed in bfloat16 or wider, within the bound.
No kernel may reach another device: no remote copies, remote signals or barrier semaphores. Data moves between devices by JAX's collectives and lax.ppermute only.
A program may use at most 192 MiB of HBM per device.

```python
import jax
import jax.numpy as jnp
from jax import lax

D = 512
GATE = 1536
MAXP = 324
GROUP = 16
IMAGES = 128
ROWS = 41472
N_MP = 4


def draw_counts(key, part):
    key = jax.random.fold_in(key, 7)
    picks = jax.random.randint(key, (IMAGES,), 0, 3)
    table = jnp.array([MAXP * 25 // 81, MAXP * 49 // 81, MAXP], dtype=jnp.int32)
    chosen = table[picks]
    spots = jax.random.randint(jax.random.fold_in(key, 1), (IMAGES // GROUP,), 0, GROUP)
    within = jnp.arange(IMAGES, dtype=jnp.int32) % GROUP
    largest = within == jnp.repeat(spots, GROUP)
    return jnp.where(largest, MAXP, chosen).astype(jnp.int32)


def level_of(rng, dims, pieces, low, top_value):
    gain, own = 1.0, jax.random.fold_in(rng, 6)
    for position, blocks in pieces:
        heights = jnp.exp(jax.random.uniform(jax.random.fold_in(own, position), (blocks,), jnp.float32, low / len(pieces), top_value / len(pieces)))
        gain = gain * jnp.repeat(heights, dims[position] // blocks).reshape([-1 if axis == position else 1 for axis in range(len(dims))])
    return gain


def noise(own_key, dims, scale, bound, pieces=(), held_as=jnp.bfloat16):
    result = jax.random.normal(own_key, dims, jnp.float32) * scale
    if len(pieces) > 0:
        result = level_of(own_key, dims, pieces, -0.22, 0.18) * result
    return jnp.clip(result, min=-bound, max=bound).astype(held_as)


def setup_inputs(seed: int = 0) -> dict:
    seeds = jax.random.split(jax.random.key(seed), 16)
    inputs = noise(seeds[0], (ROWS, D), 1.0, 6.0, ((0, 32),))
    counts = draw_counts(jax.random.fold_in(seeds[15], 71), 0)
    input_norm_gain = jnp.clip(1.0 + 0.1 * jax.random.normal(seeds[2], (D,), jnp.float32), 0.5, 1.5)
    shift_in = noise(seeds[3], (D,), 0.3, 1.75, (), jnp.float32)
    w_value = noise(seeds[4], (D, GATE), D ** -0.5, 0.25, ((0, 8), (1, 4)), jnp.float32)
    w_gate = noise(seeds[5], (D, GATE), D ** -0.5, 0.25, ((0, 8), (1, 4)), jnp.float32)
    bias_value = noise(seeds[6], (GATE,), 0.3, 1.75, ((0, 4),), jnp.float32)
    bias_gate = noise(seeds[7], (GATE,), 0.3, 1.75, ((0, 4),), jnp.float32)
    gate_gain = jnp.clip(1.0 + 0.1 * jax.random.normal(seeds[8], (GATE,), jnp.float32), 0.5, 1.5)
    gate_shift = noise(seeds[9], (GATE,), 0.3, 1.75, ((0, 4),), jnp.float32)
    spatial = noise(seeds[10], (MAXP, MAXP), MAXP ** -0.5, 0.3125, (), jnp.float32)
    spatial_bias = jnp.clip(jax.random.uniform(seeds[11], (MAXP,), jnp.float32, 0.5, 1.5), 0.5, 1.5)
    w_out = noise(seeds[12], (GATE, D), (GATE // 4) ** -0.5, 0.3125, ((0, 4), (1, 8)), jnp.float32)
    out_bias = noise(seeds[13], (D,), 0.3, 1.75, (), jnp.float32)
    cotangent = noise(seeds[14], (ROWS, D), 1.0, 6.0, ((0, 32),))
    return dict(inputs=inputs, counts=counts, input_norm_gain=input_norm_gain, shift_in=shift_in, w_value=w_value, w_gate=w_gate, bias_value=bias_value, bias_gate=bias_gate, gate_gain=gate_gain, gate_shift=gate_shift, spatial=spatial, spatial_bias=spatial_bias, w_out=w_out, out_bias=out_bias, cotangent=cotangent)


EPS = 1e-05

@jax.custom_vjp
def low(v):
    return lax.optimization_barrier(v.astype(jnp.bfloat16)).astype(jnp.float32)

@jax.custom_vjp
def low_back(v):
    return v

def low_keep(v):
    return (low(v), None)

def low_pass(kept, grad):
    return (grad,)

def back_keep(v):
    return (v, None)

def back_low(kept, grad):
    return (low(grad),)
low.defvjp(low_keep, low_pass)
low_back.defvjp(back_keep, back_low)

def matmul(left, right):
    return jnp.dot(left, right, precision=lax.Precision.HIGHEST, preferred_element_type=jnp.float32)

def normalize(rows_in):
    centre = rows_in - lax.optimization_barrier(jnp.mean(rows_in, -1, keepdims=True))
    return centre * lax.rsqrt(lax.optimization_barrier(jnp.mean(centre * centre, -1, keepdims=True)) + EPS)

def gmlp_layer(params, input_rows, counts):
    input_norm_gain, shift_in, w_value, w_gate, bias_value, bias_gate, gate_gain, gate_shift, spatial, spatial_bias, w_out, out_bias = params
    normed = low(normalize(input_rows) * input_norm_gain + shift_in)
    value_low = low(w_value)
    gate_low = low(w_gate)
    out_low = low(w_out)
    width = GATE // N_MP
    value_pieces = []
    gate_pieces = []
    for block in range(N_MP):
        normed_block = low_back(normed)
        value_pieces.append(matmul(normed_block, value_low[:, block * width:(block + 1) * width]))
        gate_pieces.append(matmul(normed_block, gate_low[:, block * width:(block + 1) * width]))
    pre_value = jnp.concatenate(value_pieces, 1) + bias_value
    pre_gate = jnp.concatenate(gate_pieces, 1) + bias_gate
    value_act = jax.nn.gelu(low_back(pre_value), approximate=False)
    gate_act = jax.nn.gelu(low_back(pre_gate), approximate=False)
    gate_normalized = normalize(gate_act) * gate_gain + gate_shift
    image_count = counts.shape[0]
    positions = jnp.arange(MAXP, dtype=jnp.int32)
    live_mask = (positions[None, :] < counts[:, None]).astype(jnp.float32)[:, :, None]
    gate_rows = low(gate_normalized).reshape(image_count, MAXP, GATE) * live_mask
    mixed_rows = jnp.einsum('rc,bcf->brf', low(spatial), gate_rows, precision=lax.Precision.HIGHEST)
    shifted_output = low_back((mixed_rows + spatial_bias[None, :, None]) * live_mask).reshape(image_count * MAXP, GATE)
    product = low(value_act * shifted_output)
    branch = jnp.zeros_like(input_rows)
    for block in range(N_MP):
        branch = branch + low(matmul(product[:, block * width:(block + 1) * width], out_low[block * width:(block + 1) * width, :]))
    return input_rows + branch + out_bias

def reference(inputs, counts, input_norm_gain, shift_in, w_value, w_gate, bias_value, bias_gate, gate_gain, gate_shift, spatial, spatial_bias, w_out, out_bias, cotangent):
    params = (input_norm_gain, shift_in, w_value, w_gate, bias_value, bias_gate, gate_gain, gate_shift, spatial, spatial_bias, w_out, out_bias)
    blocks = IMAGES // GROUP
    block_rows = GROUP * MAXP
    input_blocks = inputs.astype(jnp.float32).reshape(blocks, block_rows, D)
    count_blocks = counts.reshape(blocks, GROUP)
    tangent_blocks = cotangent.astype(jnp.float32).reshape(blocks, block_rows, D)
    zero_grads = jax.tree.map(jnp.zeros_like, params)

    def visit_block(totals, bundle):
        block_in, block_counts, block_tangent = bundle
        block_out, pullback = jax.vjp(lambda weights, rows_in: gmlp_layer(weights, rows_in, block_counts), params, block_in)
        weight_grads, block_grad = pullback(block_tangent)
        return (jax.tree.map(jnp.add, totals, weight_grads), (block_out.astype(jnp.bfloat16), block_grad))
    totals, (results, input_grads) = lax.scan(visit_block, zero_grads, (input_blocks, count_blocks, tangent_blocks))
    return (results.reshape(ROWS, D), input_grads.reshape(ROWS, D), totals[0], totals[1], totals[2], totals[3], totals[4], totals[5], totals[6], totals[7], totals[8], totals[9], totals[10], totals[11])
```

```python
import jax, jax.numpy as jnp
from jax import lax
from jax.experimental import pallas as pl
from jax.experimental.pallas import tpu as pltpu
EPS=1e-5
BF=jnp.bfloat16; F32=jnp.float32
MAXP=324
WIN=336; STEP=320; CH=16
GELU_C=(7.97882133e-01,3.63449931e-02,-4.51808700e-05,-5.02619616e-05,3.08533547e-06,-6.58149666e-08)
LOG2E_HALF=-0.7213475204444817
INV_SQRT_2PI=0.3989422804014327

def gelu_both(x):
    u=x*x
    um=jnp.minimum(u,30.0)
    p=GELU_C[5]
    for c in GELU_C[4::-1]:
        p=p*um+c
    cdf=0.5+0.5*jnp.tanh(x*p)
    slope=cdf+(x*INV_SQRT_2PI)*jnp.exp2(u*LOG2E_HALF)
    return x*cdf, slope

def dot(a,b): return jnp.dot(a,b,preferred_element_type=F32)
def dot_tn(a,b): return lax.dot_general(a,b,(((0,),(0,)),((),())),preferred_element_type=F32)
def dot_nt(a,b): return lax.dot_general(a,b,(((1,),(1,)),((),())),preferred_element_type=F32)

def norm_kernel(x_ref,g_ref,gain_ref,shift_ref,n_ref,gs_ref):
    x=x_ref[...].astype(F32)
    cen=x-jnp.mean(x,-1,keepdims=True)
    inv=lax.rsqrt(jnp.mean(cen*cen,-1,keepdims=True)+EPS)
    n_ref[...]=(cen*inv*gain_ref[...]+shift_ref[...]).astype(BF)
    @pl.when(pl.program_id(0)==0)
    def _(): gs_ref[...]=jnp.zeros_like(gs_ref)
    gs_ref[...]+=jnp.sum(g_ref[...].astype(F32),0,keepdims=True)

def norm_call(x,g,gain,shift):
    rows,d=x.shape; t=rows//3
    row=pl.BlockSpec((t,d),lambda i:(i,0)); one=pl.BlockSpec((1,d),lambda i:(0,0))
    return pl.pallas_call(norm_kernel,grid=(3,),in_specs=[row,row,one,one],out_specs=[row,one],
        out_shape=[jax.ShapeDtypeStruct((rows,d),BF),jax.ShapeDtypeStruct((1,d),F32)],name="input_norm")(x,g,gain[None],shift[None])

def gate_kernel(n_ref,w_ref,b_ref,gain_ref,shift_ref,s_ref,sb_ref,rows_ref,hat_ref,slope_ref,inv_ref,shifted_ref,pre):
    width=w_ref.shape[1]
    pre[...]=dot(n_ref[...],w_ref[...])
    for r in range(0,WIN,CH):
        act,slope=gelu_both(pre[r:r+CH,:]+b_ref[...])
        slope_ref[0,r:r+CH,:]=slope.astype(BF)
        cen=act-jnp.sum(act,-1,keepdims=True)*(1.0/width)
        inv=lax.rsqrt(jnp.sum(cen*cen,-1,keepdims=True)*(1.0/width)+EPS)
        hat=cen*inv
        inv_ref[0,r:r+CH,:]=inv
        hat_ref[0,r:r+CH,:]=hat.astype(BF)
        rows_ref[0,r:r+CH,:]=(hat*gain_ref[...]+shift_ref[...]).astype(BF)
    shifted_ref[0]=(dot(s_ref[0],rows_ref[0])+sb_ref[0]).astype(BF)

def win_spec(d): return pl.BlockSpec((pl.Element(WIN),pl.Element(d)),lambda b:(b*STEP,0))
def img(*s): return pl.BlockSpec((1,)+s,lambda b:(b,)+(0,)*len(s))
def const(*s): return pl.BlockSpec(s,lambda b:(0,)*len(s))
def params(mb=56): return pltpu.CompilerParams(vmem_limit_bytes=mb*2**20)

def gate_call(normed,w,b,gain,shift,sm,sbias):
    n=sm.shape[0]; d=normed.shape[1]; c=w.shape[1]
    big=jax.ShapeDtypeStruct((n,WIN,c),BF)
    return pl.pallas_call(gate_kernel,grid=(n,),
        in_specs=[win_spec(d),const(d,c),const(1,c),const(1,c),const(1,c),img(WIN,WIN),img(WIN,1)],
        out_specs=[img(WIN,c)]*3+[img(WIN,1),img(WIN,c)],
        out_shape=[big,big,big,jax.ShapeDtypeStruct((n,WIN,1),F32),big],
        scratch_shapes=[pltpu.VMEM((WIN,c),F32)],compiler_params=params(),name="gate_forward")(normed,w,b[None],gain[None],shift[None],sm,sbias)

def value_kernel(n_ref,g_ref,wv_ref,wo_ref,b_ref,shifted_ref,prod_ref,dshift_ref,dpre_ref,ssum_ref,gwv_ref,gwo_ref,gb_ref,pre,dprod):
    @pl.when(pl.program_id(0)==0)
    def _():
        gwv_ref[...]=jnp.zeros_like(gwv_ref); gwo_ref[...]=jnp.zeros_like(gwo_ref); gb_ref[...]=jnp.zeros_like(gb_ref)
    pre[...]=dot(n_ref[...],wv_ref[...])
    dprod[...]=dot(g_ref[...],wo_ref[...])
    for r in range(0,WIN,CH):
        act,slope=gelu_both(pre[r:r+CH,:]+b_ref[...])
        sh=shifted_ref[0,r:r+CH,:].astype(F32)
        dp=dprod[r:r+CH,:]
        prod_ref[0,r:r+CH,:]=(act*sh).astype(BF)
        ds=dp*act
        dshift_ref[0,r:r+CH,:]=ds.astype(BF)
        ssum_ref[0,r:r+CH,:]=jnp.sum(ds,-1,keepdims=True)
        dv=dp*sh*slope
        dpre_ref[0,r:r+CH,:]=dv.astype(BF)
        gb_ref[...]+=dv[0:8]+dv[8:16]
    gwv_ref[...]+=dot_tn(n_ref[...],dpre_ref[0])
    gwo_ref[...]+=dot_tn(g_ref[...],prod_ref[0])

def value_call(normed,g,wv,wo,b,shifted):
    n=shifted.shape[0]; d=normed.shape[1]; c=wv.shape[1]
    big=jax.ShapeDtypeStruct((n,WIN,c),BF)
    gw=jax.ShapeDtypeStruct((d,c),F32)
    return pl.pallas_call(value_kernel,grid=(n,),
        in_specs=[win_spec(d),win_spec(d),const(d,c),const(d,c),const(1,c),img(WIN,c)],
        out_specs=[img(WIN,c)]*3+[img(WIN,1),const(d,c),const(d,c),const(8,c)],
        out_shape=[big,big,big,jax.ShapeDtypeStruct((n,WIN,1),F32),gw,gw,jax.ShapeDtypeStruct((8,c),F32)],
        scratch_shapes=[pltpu.VMEM((WIN,c),F32)]*2,compiler_params=params(),name="value_and_backward")(normed,g,wv,wo,b[None],shifted)

def back_kernel(n_ref,dshift_ref,rows_ref,hat_ref,slope_ref,inv_ref,st_ref,gain_ref,dpre_ref,gsp_ref,gwg_ref,gb_ref,gg_ref,gsh_ref,dgr):
    @pl.when(pl.program_id(0)==0)
    def _():
        for r in (gwg_ref,gb_ref,gg_ref,gsh_ref): r[...]=jnp.zeros_like(r)
    width=gain_ref.shape[1]
    dgr[...]=dot(st_ref[0],dshift_ref[0])
    gsp_ref[0]=dot_nt(dshift_ref[0],rows_ref[0])
    for r in range(0,WIN,CH):
        d=dgr[r:r+CH,:]
        hat=hat_ref[0,r:r+CH,:].astype(F32)
        dh=d*hat
        gg_ref[...]+=dh[0:8]+dh[8:16]
        gsh_ref[...]+=d[0:8]+d[8:16]
        dg=d*gain_ref[...]
        m1=jnp.sum(dg,-1,keepdims=True)*(1.0/width)
        m2=jnp.sum(dg*hat,-1,keepdims=True)*(1.0/width)
        dpg=(dg-m1-hat*m2)*inv_ref[0,r:r+CH,:]*slope_ref[0,r:r+CH,:].astype(F32)
        dpre_ref[0,r:r+CH,:]=dpg.astype(BF)
        gb_ref[...]+=dpg[0:8]+dpg[8:16]
    gwg_ref[...]+=dot_tn(n_ref[...],dpre_ref[0])

def back_call(normed,dshift,rows,hat,slope,inv,st,gain):
    n=dshift.shape[0]; d=normed.shape[1]; c=dshift.shape[2]
    v8=jax.ShapeDtypeStruct((8,c),F32)
    return pl.pallas_call(back_kernel,grid=(n,),
        in_specs=[win_spec(d)]+[img(WIN,c)]*4+[img(WIN,1),img(WIN,WIN),const(1,c)],
        out_specs=[img(WIN,c),img(WIN,WIN),const(d,c)]+[const(8,c)]*3,
        out_shape=[jax.ShapeDtypeStruct((n,WIN,c),BF),jax.ShapeDtypeStruct((n,WIN,WIN),F32),jax.ShapeDtypeStruct((d,c),F32),v8,v8,v8],
        scratch_shapes=[pltpu.VMEM((WIN,c),F32)],compiler_params=params(),name="gate_backward")(normed,dshift,rows,hat,slope,inv,st,gain[None])

def out_kernel(x_ref,g_ref,prod_ref,dpv_ref,dpg_ref,wv_ref,wg_ref,wo_ref,gain_ref,bias_ref,res_ref,ing_ref,gg_ref,gs_ref,carry_a,carry_b):
    i=pl.program_id(0)
    @pl.when(i==0)
    def _():
        carry_a[...]=jnp.zeros_like(carry_a); carry_b[...]=jnp.zeros_like(carry_b)
        gg_ref[...]=jnp.zeros_like(gg_ref); gs_ref[...]=jnp.zeros_like(gs_ref)
    start=pl.multiple_of(i*STEP,16)
    br=dot_nt(prod_ref[0],wo_ref[...])
    dn=dot_nt(dpv_ref[0],wv_ref[...])+dot_nt(dpg_ref[0],wg_ref[...])
    br=jnp.concatenate([br[:16]+carry_a[...],br[16:]],0)
    carry_a[...]=br[STEP:]
    dn=jnp.concatenate([dn[:16]+carry_b[...],dn[16:]],0)
    carry_b[...]=dn[STEP:]
    last=i==pl.num_programs(0)-1
    x=x_ref[...].astype(F32)
    res_ref[pl.ds(start,WIN),:]=(x+br+bias_ref[...]).astype(BF)
    cen=x-jnp.mean(x,-1,keepdims=True)
    inv=lax.rsqrt(jnp.mean(cen*cen,-1,keepdims=True)+EPS)
    hat=cen*inv
    keep=jnp.where(jnp.logical_or(last,lax.broadcasted_iota(jnp.int32,(WIN,1),0)<STEP),1.0,0.0)
    dk=dn*keep
    gg_ref[...]+=jnp.sum(dk*hat,0,keepdims=True)
    gs_ref[...]+=jnp.sum(dk,0,keepdims=True)
    dx=dn*gain_ref[...]
    m1=jnp.mean(dx,-1,keepdims=True); m2=jnp.mean(dx*hat,-1,keepdims=True)
    ing_ref[pl.ds(start,WIN),:]=g_ref[...].astype(F32)+inv*(dx-m1-hat*m2)

def out_call(x,g,prod,dpv,dpg,wv,wg,wo,gain,bias):
    n=prod.shape[0]; rows,d=x.shape; c=wv.shape[1]
    return pl.pallas_call(out_kernel,grid=(n,),
        in_specs=[win_spec(d),win_spec(d)]+[img(WIN,c)]*3+[const(d,c)]*3+[const(1,d)]*2,
        out_specs=[const(rows,d),const(rows,d),const(1,d),const(1,d)],
        out_shape=[jax.ShapeDtypeStruct((rows,d),BF),jax.ShapeDtypeStruct((rows,d),F32)]+[jax.ShapeDtypeStruct((1,d),F32)]*2,
        scratch_shapes=[pltpu.VMEM((16,d),F32)]*2,compiler_params=params(),name="outputs")(x,g,prod,dpv,dpg,wv,wg,wo,gain[None],bias[None])

def spatial_windows(spatial,sbias,counts):
    n=counts.shape[0]; p=spatial.shape[0]
    live=(jnp.arange(p,dtype=jnp.int32)[None]<counts[:,None])
    s=spatial.astype(BF)
    mats=[];cols=[]
    for b in range(n):
        off=b*p-b*STEP
        m=jnp.where(live[b][:,None]&live[b][None,:],s,0)
        mats.append(jnp.pad(m,((off,WIN-p-off),)*2))
        cols.append(jnp.pad(jnp.where(live[b],sbias,0.0),(off,WIN-p-off)))
    return jnp.stack(mats),jnp.stack(cols)[:,:,None]

from jax.sharding import PartitionSpec as P
ORDER=(0,2,1,3)

def swap(x,k):
    n=lax.axis_size("mp")
    return lax.ppermute(x,"mp",[(i,i^k) for i in range(n)])

def gather_dp(x):
    n=lax.axis_size("dp")
    return lax.all_to_all(jnp.broadcast_to(x[None],(n,)+x.shape),"dp",0,0,tiled=True)

def gather_weight(shard):
    t=gather_dp(shard); t=t.reshape(-1,shard.shape[1])
    own=jnp.concatenate([t,swap(t,2)],1)
    return own,swap(own,1)

def scatter_sum(own,other):
    n=lax.axis_size("dp"); c=own.shape[1]//2
    a=own.astype(F32)+swap(other,1).astype(F32)
    s=a[:,:c]+swap(a[:,c:].astype(BF),2).astype(F32)
    s=s.astype(BF).reshape(n,-1,c)
    return lax.all_to_all(s,"dp",0,0,tiled=True).astype(F32).sum(0)

def body(inputs,counts,input_norm_gain,shift_in,w_value,w_gate,bias_value,bias_gate,gate_gain,gate_shift,spatial,spatial_bias,w_out,out_bias,cotangent):
    me=lax.axis_index("mp"); n_mp=lax.axis_size("mp"); ndp=lax.axis_size("dp")
    c=w_value.shape[1]; d=inputs.shape[1]; p=spatial.shape[0]
    n=counts.shape[0]//n_mp
    counts=lax.dynamic_slice(counts,(me*n,),(n,))
    order=jnp.bitwise_xor(jnp.array(ORDER,jnp.int32),me)
    vecs=lax.all_gather(jnp.stack([bias_value,bias_gate,gate_gain,gate_shift]),"mp")
    vecs=jnp.take(vecs,order,axis=0)
    bv,bg,gg,gs=[vecs[:,k].reshape(-1) for k in range(4)]
    g_own,g_oth=gather_weight(w_gate.astype(BF))
    wg=jnp.concatenate([g_own,g_oth],1)
    vo=jnp.concatenate([w_value,w_out.T],1).astype(BF)
    t=gather_dp(vo).reshape(d,2*c)
    y=swap(t,2)
    own=jnp.concatenate([t[:,:c],y[:,:c],t[:,c:],y[:,c:]],1)
    oth=swap(own,1)
    wv=jnp.concatenate([own[:,:2*c],oth[:,:2*c]],1)
    wo=jnp.concatenate([own[:,2*c:],oth[:,2*c:]],1)

    sm,sb=spatial_windows(spatial,spatial_bias,counts)
    normed,gsum=norm_call(inputs,cotangent,input_norm_gain,shift_in)
    rows,hat,slope,inv,shifted=gate_call(normed,wg,bg,gg,gs,sm,sb)
    prod,dshift,dpv,ssum,gwv,gwo,gbv=value_call(normed,cotangent,wv,wo,bv,shifted)
    gwv=gwv.astype(BF); gwo=gwo.astype(BF)
    w=2*c
    def inter(a,b): return jnp.concatenate([a[:,:c],b[:,:c],a[:,c:],b[:,c:]],1)
    vo_sum=scatter_sum(inter(gwv[:,:w],gwo[:,:w]),inter(gwv[:,w:],gwo[:,w:]))
    dpg,gsp,gwg,gbg,ggain,gshift=back_call(normed,dshift,rows,hat,slope,inv,jnp.swapaxes(sm,1,2),gg)
    gwg=gwg.astype(BF)
    live=(jnp.arange(p,dtype=jnp.int32)[None]<counts[:,None]).astype(F32)
    gspat=0; gsb=0
    for b in range(n):
        off=b*p-b*STEP
        gspat+=gsp[b,off:off+p,off:off+p]*live[b][:,None]*live[b][None]
        gsb+=ssum[b,off:off+p,0]*live[b]
    e=-(-p*p//(d*n_mp*8))*8
    sp=jnp.pad(gspat.reshape(-1).astype(BF),(0,d*n_mp*e-p*p)).reshape(n_mp,d,e)
    sp=jnp.take(sp,order,axis=0)
    own=jnp.concatenate([gwg[:,:c],sp[0],gwg[:,c:w],sp[1]],1)
    oth=jnp.concatenate([gwg[:,w:w+c],sp[2],gwg[:,w+c:],sp[3]],1)
    gs_sum=scatter_sum(own,oth)
    res,ing,gin,sin=out_call(inputs,cotangent,prod,dpv,dpg,wv,wg,wo,input_norm_gain,out_bias)
    sums=jnp.concatenate([gbv.sum(0),gbg.sum(0),ggain.sum(0),gshift.sum(0)]).reshape(4,n_mp,c)
    sums=jnp.take(sums,jnp.argsort(order),axis=1).reshape(-1)
    sums=jnp.concatenate([sums,gsb,gin[0],sin[0],gsum[0]])
    part=gs_sum[:,c:].reshape(-1)
    m=sums.shape[0]
    both=gather_dp(jnp.concatenate([sums,part]))
    sums=both[:,:m].sum(0); part=both[:,m:].reshape(1,d,e)
    r=swap(jnp.concatenate([sums,part.reshape(-1)]),2)
    sums=sums+r[:m]; part=jnp.concatenate([part,r[m:].reshape(1,d,e)],0)
    r=swap(jnp.concatenate([sums,part.reshape(-1)]),1)
    sums=sums+r[:m]; part=jnp.concatenate([part,r[m:].reshape(2,d,e)],0)
    part=jnp.take(part,jnp.argsort(order),axis=0).reshape(-1)[:p*p].reshape(p,p)
    four=lax.dynamic_index_in_dim(sums[:4*n_mp*c].reshape(4,n_mp,c),me,1,keepdims=False)
    k=4*n_mp*c
    return (res,ing,sums[k+p:k+p+d],sums[k+p+d:k+p+2*d],vo_sum[:,:c],gs_sum[:,:c],four[0],four[1],four[2],four[3],part,sums[k:k+p],vo_sum[:,c:].T,sums[k+p+2*d:])

def solution(mesh):
    row=P(("dp","mp"),None); wi=P("dp","mp"); mp=P("mp"); al=P()
    return jax.shard_map(body,mesh=mesh,
        in_specs=(row,P("dp"),al,al,wi,wi,mp,mp,mp,mp,al,al,P("mp","dp"),al,row),
        out_specs=(row,row,al,al,wi,wi,mp,mp,mp,mp,al,al,P("mp","dp"),al),check_vma=False)
```

```python
import jax
import jax.numpy as jnp
from jax import lax
from jax.experimental import pallas as pl
from jax.experimental.pallas import tpu as pltpu
from jax.sharding import PartitionSpec as P

EPS = 1e-5
BF = jnp.bfloat16
F32 = jnp.float32
AXES = ("dp", "mp")
WIN = 336
STEP = 320
EXT = 352
CH = 16
PAD = 384
ORDER = (0, 2, 1, 3)
GELU_C = (7.97882133e-01, 3.63449931e-02, -4.51808700e-05, -5.02619616e-05, 3.08533547e-06, -6.58149666e-08)
LOG2E_HALF = -0.7213475204444817
INV_SQRT_2PI = 0.3989422804014327
MB = 2**20


def dot(a, b):
    return jnp.dot(a, b, preferred_element_type=F32)


def dot_tn(a, b):
    return lax.dot_general(a, b, (((0,), (0,)), ((), ())), preferred_element_type=F32)


def dot_nt(a, b):
    return lax.dot_general(a, b, (((1,), (1,)), ((), ())), preferred_element_type=F32)


def gelu_both(x):
    u = x * x
    um = jnp.minimum(u, 30.0)
    p = GELU_C[5]
    for c in GELU_C[4::-1]:
        p = p * um + c
    cdf = 0.5 + 0.5 * jnp.tanh(x * p)
    slope = cdf + (x * INV_SQRT_2PI) * jnp.exp2(u * LOG2E_HALF)
    return x * cdf, slope


def split(v):
    hi = v.astype(BF)
    return hi, (v - hi.astype(F32)).astype(BF)


def fold8(v):
    out = v[0:8]
    for r in range(8, v.shape[0], 8):
        out = out + v[r : r + 8]
    return out


def img(*s):
    return pl.BlockSpec((1,) + s, lambda b, *_: (b,) + (0,) * len(s))


def const(*s):
    return pl.BlockSpec(s, lambda b, *_: (0,) * len(s), pipeline_mode=pl.Buffered(1))


def half(rows, c, h):
    return pl.BlockSpec((1, rows, c), lambda b, *_: (b, 0, h))


def side(d, w, h):
    return pl.BlockSpec((d, w), lambda b, *_: (0, h), pipeline_mode=pl.Buffered(1))


def shape(s, t):
    return jax.ShapeDtypeStruct(s, t)


def fast(s, t):
    return pltpu.VMEM(s, t)


def slow(s, t):
    return pltpu.HBM(s, t)


def in_hbm(*arrays):
    return tuple(pltpu.with_memory_space_constraint(a, pltpu.HBM) for a in arrays)


ANY = pl.BlockSpec(memory_space=pl.ANY)


def call(kernel, info, args, in_specs, outs, out_specs, scratch=(), grid=(1,), name=None, after=(), vmem=8, us=1):
    n_in, n_after = len(args), len(after)

    def ordered(info_ref, *refs):
        kernel(info_ref, *refs[:n_in], *refs[n_in + n_after :])

    return pl.pallas_call(
        ordered,
        grid_spec=pltpu.PrefetchScalarGridSpec(
            num_scalar_prefetch=1, grid=grid, in_specs=list(in_specs) + [ANY] * n_after, out_specs=out_specs, scratch_shapes=list(scratch)
        ),
        out_shape=outs,
        compiler_params=pltpu.CompilerParams(vmem_limit_bytes=vmem * MB),
        cost_estimate=pl.CostEstimate(flops=int(us * 1.1e9), bytes_accessed=int(us * 3.3e6), transcendentals=0),
        name=name,
    )(info, *args, *after)


def whole(a):
    return const(*a.shape)


def simple_call(kernel, info, args, outs, name, scratch=(), after=(), us=1):
    return call(kernel, info, args, [whole(a) for a in args], outs, [whole(o) for o in outs], scratch, name=name, after=after, us=us)


def cast_kernel(info, wg_ref, wv_ref, wo_ref, bv, bg, gg, gs, g_ref, vo_ref, vec_ref):
    c = wg_ref.shape[1]
    g_ref[...] = wg_ref[...].astype(BF)
    vo_ref[:, :c] = wv_ref[...].astype(BF)
    vo_ref[:, c:] = wo_ref[...].astype(BF)
    vec_ref[...] = both(jnp.concatenate([bv[...][None], bg[...][None], gg[...][None], gs[...][None], jnp.zeros((4, bv.shape[0]), F32)], 0))


def run_copies(pairs, sems):
    copies = [pltpu.make_async_copy(src, dst, sems.at[k]) for k, (src, dst) in enumerate(pairs)]
    for c in copies:
        c.start()
    for c in copies:
        c.wait()


def stack_kernel(info, *refs):
    *parts, out, sems = refs
    pairs, at = [], 0
    for ref in parts:
        n = ref.shape[0]
        pairs.append((ref, out.at[at : at + n]))
        at += n
    run_copies(pairs, sems)


def stack_call(info, parts, after, name):
    n = len(parts)
    rows, c = sum(a.shape[0] for a in parts), parts[0].shape[1]
    return call(stack_kernel, info, parts, [ANY] * n, [shape((rows, c), BF)], [ANY], [pltpu.SemaphoreType.DMA((n,))], name=name, after=after)[0]


def assemble_kernel(tensors, extra, info, *refs):
    *pieces, out, sems = refs
    where = ((0, 0), (1, 0), (0, 1), (1, 1))
    d, c = out.shape[0] - extra, out.shape[1] // (2 * tensors)
    n = 4
    r = d // (2 * n)
    pairs = []
    for ref, (xr, slot) in zip(pieces, where):
        for t in range(tensors):
            src, dst = slice(t * c, (t + 1) * c), slice((2 * t + slot) * c, (2 * t + slot + 1) * c)
            for k in range(n):
                row = pl.multiple_of((lax.rem(info[1] + (n - k), n) * 2 + jnp.bitwise_xor(info[2], xr)) * r, r)
                pairs.append((ref.at[k * r : (k + 1) * r, src], out.at[pl.ds(row, r), dst]))
            if xr == 0 and extra:
                pairs.append((ref.at[n * r :, src], out.at[d:, dst]))
    run_copies(pairs, sems)


def assemble_call(info, pieces, tensors, extra, after, name):
    rows, c = pieces[0].shape
    s = (2 * (rows - extra) + extra, 2 * c)
    return call(lambda *a: assemble_kernel(tensors, extra, *a), info, pieces, [ANY] * len(pieces), [shape(s, BF)],
                [const(*s)], [pltpu.SemaphoreType.DMA((18 * tensors,))], name=name, after=after)[0]


def norm_kernel(info, x_ref, g_ref, gain_ref, shift_ref, n_ref, gsum_ref):
    b = pl.program_id(0)

    @pl.when(b == 0)
    def _():
        gsum_ref[...] = jnp.zeros_like(gsum_ref)

    own = jnp.where(b == pl.num_programs(0) - 1, 1.0, 0.0)
    for r in range(0, WIN, 48):
        x = x_ref[r : r + 48, :].astype(F32)
        cen = x - jnp.mean(x, -1, keepdims=True)
        inv = lax.rsqrt(jnp.mean(cen * cen, -1, keepdims=True) + EPS)
        n_ref[0, r : r + 48, :] = (cen * inv * gain_ref[...][None] + shift_ref[...][None]).astype(BF)
    total = fold8(g_ref[STEP:, :].astype(F32)) * own
    for r in range(0, STEP, CH):
        total = total + fold8(g_ref[r : r + CH, :].astype(F32))
    gsum_ref[...] += jnp.sum(total, 0, keepdims=True)


def window_rows(d):
    return pl.BlockSpec((pl.Element(WIN), pl.Element(d)), lambda b, *_: (b * STEP, 0))


def norm_call(info, x, g, gain, shift, n, after):
    d = x.shape[1]
    return call(norm_kernel, info, in_hbm(x, g, gain, shift), [window_rows(d), window_rows(d), const(d), const(d)],
                [slow((n, WIN, d), BF), shape((1, d), F32)], [img(WIN, d), const(1, d)], grid=(n,), name="input_norm", after=after, us=3)


def windows_kernel(info, sp_ref, sb_ref, s_ref, st_ref, sbw_ref, token, pad, tpad, col):
    p = sp_ref.shape[0]
    b = pl.program_id(0)

    @pl.when(b == 0)
    def _():
        pad[...] = jnp.zeros_like(pad)
        pad[0:p, 0:p] = sp_ref[...]
        tpad[...] = pad[...].T
        col[...] = jnp.concatenate([jnp.broadcast_to(sb_ref[...][None], (128, p)), jnp.zeros((128, PAD - p), F32)], 1).T
        token[...] = jnp.zeros_like(token)

    ri = lax.broadcasted_iota(jnp.int32, (WIN, PAD), 0)
    ci = lax.broadcasted_iota(jnp.int32, (WIN, PAD), 1)
    for k in range(4):

        @pl.when(lax.rem(b, 4) == k)
        def _():
            off = k * (p - STEP)
            end = off + count_of(info, b)
            live = (ri >= off) & (ri < end) & (ci >= off) & (ci < end)
            move = lambda v: pltpu.roll(pltpu.roll(v, off, 0), off, 1) if off else v
            s_ref[0] = jnp.where(live, move(pad[...])[:WIN], 0.0).astype(BF)[:, :WIN]
            st_ref[0] = jnp.where(live, move(tpad[...])[:WIN], 0.0).astype(BF)[:, :WIN]
            cb = pltpu.roll(col[...], off, 0) if off else col[...]
            sbw_ref[0] = jnp.where(((ri >= off) & (ri < end))[:, :128], cb[:WIN], 0.0)


def count_of(info, b):
    return info[8 + info[5] + b]


def windows_call(info, spatial, sbias, n, after):
    p = spatial.shape[0]
    win = slow((n, WIN, WIN), BF)
    return call(windows_kernel, info, in_hbm(spatial, sbias), [const(p, p), const(p)], [win, win, slow((n, WIN, 128), F32), shape((8, 128), F32)],
                [img(WIN, WIN), img(WIN, WIN), img(WIN, 128), const(8, 128)], [pltpu.VMEM((PAD, PAD), F32)] * 2 + [pltpu.VMEM((PAD, 128), F32)],
                grid=(n,), name="windows", after=after, us=2)


def gate_kernel(info, wa_ref, wb_ref, n_ref, s_ref, sb_ref, rows_ref, hat_ref, slope_ref, inv_ref, shifted_ref, v_ref, pre):
    w = wa_ref.shape[1]
    d = wa_ref.shape[0] - 16
    width = 2 * w

    @pl.when(pl.program_id(0) == 0)
    def _():
        for k, ref in enumerate((wa_ref, wb_ref)):
            v = ref[d:, :].astype(F32)
            v_ref[:, k * w : (k + 1) * w] = v[:8] + v[8:]

    bias, gain, shift = v_ref[1:2, :], v_ref[2:3, :], v_ref[3:4, :]
    pre[:, :w] = dot(n_ref[0], wa_ref[:d, :])
    pre[:, w:] = dot(n_ref[0], wb_ref[:d, :])
    for r in range(0, WIN, CH):
        act, slope = gelu_both(pre[r : r + CH, :] + bias)
        slope_ref[0, r : r + CH, :] = slope.astype(BF)
        cen = act - jnp.sum(act, -1, keepdims=True) * (1.0 / width)
        inv = lax.rsqrt(jnp.sum(cen * cen, -1, keepdims=True) * (1.0 / width) + EPS)
        hat = cen * inv
        inv_ref[0, r : r + CH, :] = jnp.broadcast_to(inv, (CH, 128))
        hat_ref[0, r : r + CH, :] = hat.astype(BF)
        rows_ref[0, r : r + CH, :] = (hat * gain + shift).astype(BF)
    rows_ref[0, WIN:, :] = jnp.ones((EXT - WIN, width), BF)
    sb = sb_ref[0]
    mixed = dot(s_ref[0], rows_ref[0, :WIN, :])
    for t in range(0, width, 128):
        shifted_ref[0, :, t : t + 128] = (mixed[:, t : t + 128] + sb).astype(BF)


def gate_call(info, halves, normed, s, sb, after):
    n, _, d = normed.shape
    w = 2 * halves[0].shape[1]
    big = slow((n, WIN, w), BF)
    return call(
        gate_kernel, info, (*halves, *in_hbm(normed, s, sb)),
        [whole(a) for a in halves] + [img(WIN, d), img(WIN, WIN), img(WIN, 128)],
        [slow((n, EXT, w), BF), big, big, slow((n, WIN, 128), F32), big, shape((8, w), F32)],
        [img(EXT, w), img(WIN, w), img(WIN, w), img(WIN, 128), img(WIN, w), const(8, w)],
        [pltpu.VMEM((WIN, w), F32)], grid=(n,), name="gate_forward", after=after, us=1, vmem=17,
    )


def value_kernel(info, wv_ref, wo_ref, n_ref, g_ref, v_ref, shifted_ref, rows_ref, gin_ref, prod_ref, dshift_ref, dpre_ref, gw_ref, gb_ref, gsp_ref, small_ref,
                 pre, dprod, prods, dpres, n_all, g_all):
    b = pl.program_id(0)
    n_img = pl.num_programs(0)
    d, _ = wv_ref.shape

    @pl.when(b == 0)
    def _():
        gb_ref[...] = jnp.zeros_like(gb_ref)
        gsp_ref[...] = gin_ref[...]

    pre[...] = dot(n_ref[0], wv_ref[...])
    dprod[...] = dot(g_ref[...], wo_ref[...])
    bias = v_ref[0:1, :]
    for r in range(0, WIN, CH):
        act, slope = gelu_both(pre[r : r + CH, :] + bias)
        sh = shifted_ref[0, r : r + CH, :].astype(F32)
        dp = dprod[r : r + CH, :]
        prod = (act * sh).astype(BF)
        prod_ref[0, r : r + CH, :] = prod
        dshift_ref[0, r : r + CH, :] = (dp * act).astype(BF)
        dv = dp * sh * slope
        dvl = dv.astype(BF)
        dpre_ref[0, r : r + CH, :] = dvl
        gb_ref[...] += fold8(dv)
    row = pl.multiple_of(b * WIN, 16)
    n_all[pl.ds(row, WIN), :] = n_ref[0]
    g_all[pl.ds(row, WIN), :] = g_ref[...]
    prods[pl.ds(row, WIN), :] = prod_ref[0]
    dpres[pl.ds(row, WIN), :] = dpre_ref[0]
    part = dot_nt(dshift_ref[0], rows_ref[0])
    part = jnp.concatenate([jnp.concatenate([part, jnp.zeros((WIN, PAD - EXT), F32)], 1), jnp.zeros((PAD - WIN, PAD), F32)], 0)
    off = b * (MAXP_STEP)
    end = off + count_of(info, b)
    ri = lax.broadcasted_iota(jnp.int32, (PAD, PAD), 0)
    ci = lax.broadcasted_iota(jnp.int32, (PAD, PAD), 1)
    live = (ri >= off) & (ri < end) & (((ci >= off) & (ci < end)) | (ci >= WIN))
    part = jnp.where(live, part, 0.0)
    back = lax.rem(PAD - off, PAD)
    gsp_ref[...] += pltpu.roll(pltpu.roll(part, back, 0), back, 1)

    @pl.when(b == n_img - 1)
    def _():
        gwv = dot_tn(n_all[...], dpres[...])
        gw_ref[:d, :] = gwv.astype(gw_ref.dtype)
        gw_ref[d:, :] = dot_tn(g_all[...], prods[...]).astype(gw_ref.dtype)
        small_ref[...] = jnp.concatenate([row_sums(gwv, wv_ref), back_sum(gb_ref[...], wv_ref), jnp.zeros((6, d), F32)], 0)


def row_sums(gw, w_ref):
    prod = gw * w_ref[...].astype(F32)
    t = prod[:, :128]
    for k in range(128, prod.shape[1], 128):
        t = t + prod[:, k : k + 128]
    return jnp.sum(t.T, 0, keepdims=True)


def back_sum(sums, w_ref):
    hi, lo = split(sums)
    return jnp.sum(dot_nt(hi, w_ref[...]) + dot_nt(lo, w_ref[...]), 0, keepdims=True)


MAXP_STEP = 4


def value_call(info, h, keep, vo, normed, g, vecs, shifted, rows, gsp, after=()):
    n, _, d = normed.shape
    w = vecs.shape[1] // 2
    big, out = shape((n, WIN, w), BF), slow((n, WIN, w), BF)
    return call(
        value_kernel, info, (vo, vo, *in_hbm(normed, g), vecs, *in_hbm(shifted, rows), gsp),
        [side(d, w, 0), side(d, w, 1), img(WIN, d), window_rows(d), pl.BlockSpec((8, w), lambda b, *_: (0, h)), half(WIN, w, h), half(EXT, w, h), const(PAD, PAD)],
        [out, big, out, shape((2 * d, w), F32 if keep else BF), shape((8, w), F32), shape((PAD, PAD), F32), shape((8, d), F32)],
        [img(WIN, w)] * 3 + [const(2 * d, w), const(8, w), const(PAD, PAD), const(8, d)],
        [pltpu.VMEM((WIN, w), F32)] * 2 + [pltpu.VMEM((n * WIN, w), BF)] * 2 + [pltpu.VMEM((n * WIN, d), BF)] * 2,
        grid=(n,), name="value_own" if keep else "value_other", after=after, us=1, vmem=23,
    )


def back_kernel(info, n_ref, dsa_ref, dsb_ref, rows_hat_ref, slope_ref, inv_ref, st_ref, v_ref, wa_ref, wb_ref, gba_ref, gbb_ref, sma_ref, smb_ref, gsum_ref,
                dpre_ref, keep_ref, send_ref, vown_ref, dgr, dpres, n_all, gb, gg, gsh):
    b = pl.program_id(0)
    n_img = pl.num_programs(0)
    d, w = n_ref.shape[2], wa_ref.shape[1]
    width = 2 * w
    wa_ref, wb_ref = wa_ref.at[:d], wb_ref.at[:d]

    @pl.when(b == 0)
    def _():
        for r in (gb, gg, gsh):
            r[...] = jnp.zeros_like(r)

    gain = v_ref[2:3, :]
    dgr[:, :w] = dot(st_ref[0], dsa_ref[0])
    dgr[:, w:] = dot(st_ref[0], dsb_ref[0])
    for r in range(0, WIN, CH):
        dr = dgr[r : r + CH, :]
        hat = rows_hat_ref[0, r : r + CH, :].astype(F32)
        gg[...] += fold8(dr * hat)
        gsh[...] += fold8(dr)
        dg = dr * gain
        m1 = jnp.sum(dg, -1, keepdims=True) * (1.0 / width)
        m2 = jnp.sum(dg * hat, -1, keepdims=True) * (1.0 / width)
        dpg = (dg - m1 - hat * m2) * inv_ref[0, r : r + CH, 0:1] * slope_ref[0, r : r + CH, :].astype(F32)
        dpre_ref[0, r : r + CH, :] = dpg.astype(BF)
        gb[...] += fold8(dpg)
    row = pl.multiple_of(b * WIN, 16)
    dpres[pl.ds(row, WIN), :] = dpre_ref[0]
    n_all[pl.ds(row, WIN), :] = n_ref[0]

    @pl.when(b == n_img - 1)
    def _():
        gw = dot_tn(n_all[...], dpres[...])
        keep_ref[...] = gw[:, :w]
        sums = gb[...]
        send_ref[:d, :] = gw[:, w:].astype(BF)
        t = sma_ref[0:1, :] + smb_ref[0:1, :] + row_sums(gw[:, :w], wa_ref) + row_sums(gw[:, w:], wb_ref)
        s = sma_ref[1:2, :] + smb_ref[1:2, :] + back_sum(sums[:, :w], wa_ref) + back_sum(sums[:, w:], wb_ref)
        one = lambda v: jnp.sum(v, 0, keepdims=True)
        fours = [jnp.concatenate([one(gba_ref[...]), one(gbb_ref[...])], 1), one(gb[...]), one(gg[...]), one(gsh[...])]
        wide = lambda v: jnp.concatenate([v, jnp.zeros((1, w - d), F32)], 1)
        full = jnp.concatenate([wide(t), wide(s), wide(gsum_ref[...]), jnp.zeros((1, w), F32)], 0)
        fours = jnp.concatenate(fours, 0)
        hi, lo = split(jnp.concatenate([fours[:, w:], full], 0))
        send_ref[d:, :] = jnp.concatenate([hi, lo], 0)
        fhi, flo = split(full)
        vown_ref[...] = jnp.concatenate([fours[:, :w], fhi.astype(F32) + flo.astype(F32)], 0)


def back_call(info, normed, ds, hat, slope, inv, st, vecs, wg, gbv, small, gsum, after):
    n, _, d = normed.shape
    width = vecs.shape[1]
    w = width // 2
    return call(
        back_kernel, info, (*in_hbm(normed), *ds, *in_hbm(hat, slope, inv, st), vecs, *wg, *gbv, *small, gsum),
        [img(WIN, d), img(WIN, w), img(WIN, w), img(WIN, width), img(WIN, width), img(WIN, 128), img(WIN, WIN), const(8, width), whole(wg[0]), whole(wg[1]),
         const(8, w), const(8, w), const(8, d), const(8, d), const(1, d)],
        [slow((n, WIN, width), BF), shape((d, w), F32), shape((d + 16, w), BF), shape((8, w), F32)],
        [img(WIN, width), const(d, w), const(d + 16, w), const(8, w)],
        [pltpu.VMEM((WIN, width), F32), pltpu.VMEM((n * WIN, width), BF), pltpu.VMEM((n * WIN, d), BF)] + [pltpu.VMEM((8, width), F32)] * 3,
        grid=(n,), name="gate_backward", after=after, us=1, vmem=23,
    )


def joined(v, carry):
    @pl.when(pl.program_id(0) == 0)
    def _():
        carry[...] = jnp.zeros_like(carry)

    v = jnp.concatenate([v[:16] + carry[...], v[16:]], 0)
    carry[...] = v[STEP:]
    return v


def result_kernel(info, x_ref, pa_ref, pb_ref, woa_ref, wob_ref, bias_ref, res_ref, carry):
    start = pl.multiple_of(pl.program_id(0) * STEP, 16)
    br = joined(dot_nt(pa_ref[0], woa_ref[...]) + dot_nt(pb_ref[0], wob_ref[...]), carry)
    res_ref[pl.ds(start, WIN), :] = (x_ref[pl.ds(start, WIN), :].astype(F32) + br + bias_ref[...][None]).astype(BF)


def grad_kernel(info, x_ref, g_ref, va_ref, vb_ref, dg_ref, wva_ref, wvb_ref, wga_ref, wgb_ref, gain_ref, ing_ref, carry):
    start = pl.multiple_of(pl.program_id(0) * STEP, 16)
    d, w = wva_ref.shape
    dn = dot_nt(va_ref[0], wva_ref[...]) + dot_nt(vb_ref[0], wvb_ref[...])
    dn = joined(dn + dot_nt(dg_ref[0, :, :w], wga_ref[:d, :]) + dot_nt(dg_ref[0, :, w:], wgb_ref[:d, :]), carry)
    x = x_ref[pl.ds(start, WIN), :].astype(F32)
    cen = x - jnp.mean(x, -1, keepdims=True)
    inv = lax.rsqrt(jnp.mean(cen * cen, -1, keepdims=True) + EPS)
    hat = cen * inv
    dx = dn * gain_ref[...][None]
    m1 = jnp.mean(dx, -1, keepdims=True)
    m2 = jnp.mean(dx * hat, -1, keepdims=True)
    ing_ref[pl.ds(start, WIN), :] = g_ref[...].astype(F32) + inv * (dx - m1 - hat * m2)


def result_call(info, x, prod, vo, bias, after):
    n, _, w = prod[0].shape
    rows, d = x.shape
    return call(
        result_kernel, info, (*in_hbm(x, *prod), *vo, *in_hbm(bias)), [const(rows, d), img(WIN, w), img(WIN, w), side(d, w, 1), side(d, w, 1), const(d)],
        [shape((rows, d), BF)], [const(rows, d)], [pltpu.VMEM((16, d), F32)], grid=(n,), name="result", after=after, us=1, vmem=10,
    )[0]


def grad_call(info, x, g, dpv, dpg, vo, wg, gain, after):
    n, _, w = dpv[0].shape
    rows, d = x.shape
    return call(
        grad_kernel, info, (*in_hbm(x, g, *dpv, dpg), *vo, *wg, *in_hbm(gain)),
        [const(rows, d), window_rows(d), img(WIN, w), img(WIN, w), img(WIN, 2 * w)] + [side(d, w, 0)] * 2 + [whole(wg[0]), whole(wg[1]), const(d)],
        [shape((rows, d), F32)], [const(rows, d)], [pltpu.VMEM((16, d), F32)], grid=(n,), name="input_grad", after=after, us=1, vmem=16,
    )[0]


VROWS = 32


def quarter_kernel(tensors, extra, info, *refs):
    if extra == "spatial":
        keep, recv, gsp, *outs = refs
    else:
        keep, recv, vown, *outs = refs
    x, y, core = info[2], info[3], info[4]
    d = keep.shape[0] // tensors
    c = keep.shape[1] // 2
    nz = 4
    r = d // (2 * nz)
    for a, out in enumerate(outs):
        for b in range(2):
            xr, yr = jnp.where(core == 0, b, a), jnp.where(core == 0, a, b)
            cols = pl.ds(pl.multiple_of(yr * c, c), c)
            for t in range(tensors):
                for z in range(nz):
                    row = pl.multiple_of(t * d + (2 * z + jnp.bitwise_xor(x, xr)) * r, r)
                    dst = t * nz * r + z * r
                    out[b, dst : dst + r, :] = (keep[pl.ds(row, r), cols] + recv[pl.ds(row, r), cols].astype(F32)).astype(out.dtype)
            at = tensors * nz * r
            if extra == "spatial":
                q = PAD // 4
                row = pl.multiple_of((2 * jnp.bitwise_xor(x, xr) + jnp.bitwise_xor(y, yr)) * q, q)
                out[b, at:, :] = gsp[pl.ds(row, q), :].astype(BF).astype(out.dtype)
            else:
                got = recv[d:, :].astype(F32)
                v = vown[...] + (got[:8] + got[8:])
                four = jnp.where(yr == 0, v[0:4, :c], v[0:4, c:])
                v = jnp.concatenate([four, v[4:7, :c], jnp.concatenate([v[4:7, c : c + 128], jnp.zeros((3, c - 128), F32)], 1), jnp.zeros((6, c), F32)], 0)
                out[b, at:, :] = both(v).astype(out.dtype)


def both(v):
    hi, lo = split(v)
    return jnp.concatenate([hi, lo], 0)


def rounded(v):
    return both(v[:16] + v[16:]) if v.shape[0] == VROWS else v.astype(BF)


def plane_kernel(extra, info, parts, recv, keep, send):
    m = keep.shape[0] - extra
    for b, out in enumerate((keep, send)):
        out[:m, :] = (parts[b, :m, :] + recv[b, :m, :].astype(F32)).astype(out.dtype)
        out[m:, :] = rounded(parts[b, m:, :] + recv[b, m:, :].astype(F32)).astype(out.dtype)


def line_kernel(tensors, chunks, extra, info, part, recv, keep, send):
    m = part.shape[0] - extra
    r = m // (tensors * chunks)
    h = chunks // 2
    bit = lax.rem(lax.div(info[1], h), 2)
    for out, which in ((keep, bit), (send, 1 - bit)):
        for t in range(tensors):
            rows = pl.ds(pl.multiple_of((t * chunks + which * h) * r, r), h * r)
            out[t * h * r : (t + 1) * h * r, :] = (part[rows, :] + recv[rows, :].astype(F32)).astype(out.dtype)
        out[tensors * h * r :, :] = rounded(part[m:, :] + recv[m:, :].astype(F32)).astype(out.dtype)


def finish_vo_kernel(info, part, recv, gwv, gwo, sp):
    r = gwv.shape[0]
    v = part[...] + recv[...].astype(F32)
    gwv[...] = v[:r]
    gwo[...] = v[r : 2 * r]
    sp[...] = v[2 * r :].astype(BF)


def finish_g_kernel(info, part, recv, gain, shift, gwg, gbv, gbg, ggain, gshift, rows):
    r = gwg.shape[0]
    v = part[...] + recv[...].astype(F32)
    gwg[...] = v[:r]
    v = v[r : r + 16] + v[r + 16 :]
    for k, out in enumerate((gbv, gbg, ggain, gshift)):
        out[...] = v[k]
    full = jnp.concatenate([v[4:7, :], v[7:10, :128]], 1)
    gin = (full[0:1, :] - shift[...][None] * full[1:2, :]) / gain[...][None]
    rows[...] = jnp.concatenate([gin, full[1:], jnp.zeros((5, full.shape[1]), F32)], 0)


def pair_kernel(info, a, b, out):
    out[...] = (a[...].astype(F32) + b[...].astype(F32)).astype(BF)


def spatial_kernel(info, a, rx, ry, rxy, mine, other, out, bias, gin, sin, gout, full):
    q = a.shape[0]
    for ref, k in ((a, 0), (ry, 1), (rx, 2), (rxy, 3)):
        full[pl.ds(pl.multiple_of(jnp.bitwise_xor(2 * info[2] + info[3], k) * q, q), q), :] = ref[...].astype(F32)
    p = out.shape[0]
    out[...] = full[:p, :p]
    bias[...] = full[:, 256:].T[WIN - 256, :p]
    v = jnp.where(info[4] == 0, mine[...], other[...])
    gin[...] = v[0]
    sin[...] = v[1]
    gout[...] = v[2]


def permute(x, to):
    n_dp, n_mp = lax.axis_size("dp"), lax.axis_size("mp")
    pairs = []
    for i in range(n_dp * n_mp):
        dp, mp = to(i // n_mp, i % n_mp)
        pairs.append((i, dp * n_mp + mp))
    return lax.ppermute(x, AXES, pairs)


def core_swap(x):
    return permute(x, lambda dp, mp: (dp, mp ^ 1))


def plane_swaps(a, b, c):
    return (
        permute(a, lambda dp, mp: (dp ^ 1, mp)),
        permute(b, lambda dp, mp: (dp, mp ^ 2)),
        permute(c, lambda dp, mp: (dp ^ 1, mp ^ 2)),
    )


def first_swap(x):
    return permute(x, lambda dp, mp: (dp, mp ^ 2) if mp % 2 == 0 else (dp ^ 1, mp))


def second_swap(x):
    return permute(x, lambda dp, mp: (dp ^ 1, mp) if mp % 2 == 0 else (dp, mp ^ 2))


def z_swap(x, bit):
    return permute(x, lambda dp, mp: (dp ^ (2 * bit), mp))


def line_swaps(arrays):
    n_dp = lax.axis_size("dp")
    return [permute(a, lambda dp, mp, k=k: ((dp + 2 * (k + 1)) % n_dp, mp)) for k, a in enumerate(arrays)]


def gather_dp(copies):
    t = lax.all_to_all(copies, "dp", 0, 0, tiled=True)
    return t.reshape(-1, t.shape[2])


def after(x, y):
    return lax.optimization_barrier((x, y))


def y_swap(x):
    return permute(x, lambda dp, mp: (dp, mp ^ 2))


def scatter_any(keep, recv):
    n = lax.axis_size("dp")
    c = keep.shape[1] // 2
    a = keep + recv.astype(F32)
    s = a[:, :c] + permute(a[:, c:].astype(BF), lambda dp, mp: (dp, mp ^ 2)).astype(F32)
    return lax.all_to_all(s.astype(BF).reshape(n, -1, c), "dp", 0, 0, tiled=True).astype(F32).sum(0)


def body(inputs, counts, input_norm_gain, shift_in, w_value, w_gate, bias_value, bias_gate, gate_gain, gate_shift, spatial, spatial_bias, w_out, out_bias, cotangent):
    n_dp, n_mp = lax.axis_size("dp"), lax.axis_size("mp")
    me, dp = lax.axis_index("mp"), lax.axis_index("dp")
    r, c = w_value.shape
    d = inputs.shape[1]
    p = spatial.shape[0]
    n = counts.shape[0] // n_mp
    quick = n_dp == 8 and r % 16 == 0
    head = jnp.stack([me, dp // 2, dp % 2, me // 2, me % 2, me * n, 0, 0]).astype(jnp.int32)
    info = jnp.concatenate([head, counts])

    args = in_hbm(w_gate, w_value, w_out.T, bias_value, bias_gate, gate_gain, gate_shift)
    pg, vo1, vec = simple_call(cast_kernel, info, args, [shape((r, c), BF), shape((r, 2 * c), BF), shape((16, c), BF)], "casts")
    if quick:
        zg, zvo = line_swaps([pg] * 3), line_swaps([vo1] * 3)
        zg = stack_call(info, (pg, *zg, vec), (), "line_gate")
        pieces = (zg, *plane_swaps(zg, zg, zg))
    else:
        copies = lambda a: gather_dp(jnp.broadcast_to(a[None], (n_dp,) + a.shape))
        g0 = jnp.concatenate([copies(pg), vec])
        zg = wga = jnp.concatenate([g0, y_swap(g0)], 1)
        vo0 = copies(vo1)
        vo2 = y_swap(vo0)
        zvo = ()
        voa = jnp.concatenate([vo0[:, :c], vo2[:, :c], vo0[:, c:], vo2[:, c:]], 1)
    normed, gsum = norm_call(info, inputs, cotangent, input_norm_gain, shift_in, n, (zg,))
    s, st, sb, token = windows_call(info, spatial, spatial_bias, n, (gsum, *zvo))
    if quick:
        wga = assemble_call(info, pieces, 1, 16, (token,), "assemble_gate")
        zvo = stack_call(info, (vo1, *zvo), (wga,), "line_value_out")
        pieces = (zvo, *plane_swaps(zvo, zvo, zvo))
    wgb = core_swap(wga)
    rows, hat, slope, inv, shifted, vec = gate_call(info, (wga, wgb), normed, s, sb, (zvo,) if quick else ())
    if quick:
        voa = assemble_call(info, pieces, 2, 0, (vec,), "assemble_value_out")
    vob = core_swap(voa)
    zero = jnp.zeros((PAD, PAD), F32)
    prod_b, ds_b, dpv_b, gw_b, gb_b, gsp, small_b = value_call(info, 1, False, vob, normed, cotangent, vec, shifted, rows, zero)
    recv_vo = core_swap(gw_b)
    prod_a, ds_a, dpv_a, gw_a, gb_a, gsp, small_a = value_call(info, 0, True, voa, normed, cotangent, vec, shifted, rows, gsp)
    q = PAD // 4
    def quarters(tensors, extra, args, rows, name, after):
        return simple_call(lambda *a: quarter_kernel(tensors, extra, *a), info, args, [shape((2, rows, c), F32), shape((2, rows, c), BF)], name, after=after)

    def plane(parts, recv, extra, name, after):
        s = parts.shape[1:]
        return simple_call(lambda *a: plane_kernel(extra, *a), info, (parts, recv), [shape(s, F32), shape(s, BF)], name, after=after)

    def line(part, recv, tensors, chunks, extra, name, after):
        s = ((part.shape[0] - extra) // 2 + extra, c)
        return simple_call(lambda *a: line_kernel(tensors, chunks, extra, *a), info, (part, recv), [shape(s, F32), shape(s, BF)], name, after=after)

    if quick:
        kvo, snd = quarters(2, "spatial", (gw_a, recv_vo, gsp), 8 * r + q, "quarters_vo", ())
        got_vo = first_swap(snd)
    dpg, keep_g, send_g, vown = back_call(info, normed, (ds_a, ds_b), hat, slope, inv, st, vec, (wga, wgb), (gb_a, gb_b), (small_a, small_b), gsum, (snd,) if quick else ())
    recv_g = core_swap(send_g)
    if quick:
        kvo, snd = plane(kvo, got_vo, q, "plane_vo", (vown,))
        got_vo = second_swap(snd)
    res = result_call(info, inputs, (prod_a, prod_b), (voa, vob), out_bias, (snd if quick else vown,))
    if quick:
        kg, snd = quarters(1, "vectors", (keep_g, recv_g, vown), 4 * r + VROWS, "quarters_g", (res,))
        got_g = first_swap(snd)
        kvo, snd = line(kvo, got_vo, 2, 4, q, "line_vo", (snd,))
        got_vo = z_swap(snd, 2)
        kg, snd = plane(kg, got_g, VROWS, "plane_g", (snd,))
        got_g = second_swap(snd)
        ing = grad_call(info, inputs, cotangent, (dpv_a, dpv_b), dpg, (voa, vob), (wga, wgb), input_norm_gain, (snd,))
        kg, snd = line(kg, got_g, 1, 4, VROWS, "line_g", (ing,))
        got_g = z_swap(snd, 2)
        kvo, snd = line(kvo, got_vo, 2, 2, q, "pair_vo", (snd,))
        got_vo = z_swap(snd, 1)
        kg, snd = line(kg, got_g, 1, 2, VROWS, "pair_g", (snd,))
        got_g = z_swap(snd, 1)
        gwv, gwo, sp = simple_call(finish_vo_kernel, info, (kvo, got_vo), [shape((r, c), F32), shape((r, c), F32), shape((q, c), BF)], "finish_vo", after=(snd,))
        (sp,) = simple_call(pair_kernel, info, (sp, core_swap(sp)), [shape((q, c), BF)], "spatial_pair")
        sps = plane_swaps(sp, sp, sp)
        one = shape((c,), F32)
        gwg, gbv, gbg, ggain, gshift, full = simple_call(
            finish_g_kernel, info, (kg, got_g, *in_hbm(input_norm_gain, shift_in)),
            [shape((r, c), F32)] + [one] * 4 + [shape((8, d), F32)], "finish_g", after=(sp,))
        gspat, gsb, gin, sin, gob = simple_call(spatial_kernel, info, (sp, *sps, full, core_swap(full)), [shape((p, p), F32), shape((p,), F32)] + [shape((d,), F32)] * 3, "spatial_sum", [pltpu.VMEM((PAD, PAD), F32)], after=(gwg,))
    else:
        ing = grad_call(info, inputs, cotangent, (dpv_a, dpv_b), dpg, (voa, vob), (wga, wgb), input_norm_gain, ())
        gwv = scatter_any(gw_a[:d], recv_vo[:d])
        gwo = scatter_any(gw_a[d:], recv_vo[d:])
        gwg = scatter_any(keep_g, recv_g[:d])
        gsp = lax.psum(gsp, AXES)
        gspat, gsb = gsp[:p, :p], gsp[:p, WIN]
        other = send_g[d:].astype(F32)
        other = other[:8] + other[8:]
        back = jnp.argsort(jnp.bitwise_xor(jnp.array(ORDER, jnp.int32), me))
        four = jnp.concatenate([vown[:4], other[:4]], 1).reshape(4, n_mp, c)
        four = lax.psum(jnp.take(four, back, axis=1), AXES)
        gbv, gbg, ggain, gshift = lax.dynamic_index_in_dim(four, me, 1, keepdims=False)
        t, sin, gob = lax.psum(vown[4:7, :d], AXES)
        gin = (t - shift_in * sin) / input_norm_gain
    return (res, ing, gin, sin, gwv, gwg, gbv, gbg, ggain, gshift, gspat, gsb, gwo.T, gob)


def solution(mesh):
    row, wi, mp, al = P(("dp", "mp"), None), P("dp", "mp"), P("mp"), P()
    return jax.shard_map(
        body, mesh=mesh,
        in_specs=(row, P("dp"), al, al, wi, wi, mp, mp, mp, mp, al, al, P("mp", "dp"), al, row),
        out_specs=(row, row, al, al, wi, wi, mp, mp, mp, mp, al, al, P("mp", "dp"), al),
        check_vma=False,
    )
```

```python
import jax
import jax.numpy as jnp
from jax import lax
from jax.experimental import pallas as pl
from jax.experimental.pallas import tpu as pltpu
from jax.sharding import PartitionSpec as P

EPS = 1e-5
BF = jnp.bfloat16
F32 = jnp.float32
AXES = ("dp", "mp")
WIN = 336
STEP = 320
EXT = 352
CH = 16
PAD = 384
ORDER = (0, 2, 1, 3)
GELU_C = (7.97869712e-01, 3.63922863e-02, -8.78266205e-05, -3.66934307e-05, 1.42500480e-06)
LOG2E_HALF = -0.7213475204444817
INV_SQRT_2PI = 0.3989422804014327
MB = 2**20


def dot(a, b):
    return jnp.dot(a, b, preferred_element_type=F32)


def dot_tn(a, b):
    return lax.dot_general(a, b, (((0,), (0,)), ((), ())), preferred_element_type=F32)


def dot_nt(a, b):
    return lax.dot_general(a, b, (((1,), (1,)), ((), ())), preferred_element_type=F32)


def gelu_both(x):
    u = x * x
    p = GELU_C[4]
    for c in GELU_C[3::-1]:
        p = p * u + c
    cdf = 0.5 + 0.5 * jnp.tanh(x * p)
    slope = cdf + (x * INV_SQRT_2PI) * jnp.exp2(u * LOG2E_HALF)
    return x * cdf, slope


def split(v):
    hi = v.astype(BF)
    return hi, (v - hi.astype(F32)).astype(BF)


def fold8(v):
    out = v[0:8]
    for r in range(8, v.shape[0], 8):
        out = out + v[r : r + 8]
    return out


def img(*s):
    return pl.BlockSpec((1,) + s, lambda b, *_: (b,) + (0,) * len(s))


def const(*s):
    return pl.BlockSpec(s, lambda b, *_: (0,) * len(s), pipeline_mode=pl.Buffered(1))


def half(rows, c, h):
    return pl.BlockSpec((1, rows, c), lambda b, *_: (b, 0, h))


def side(d, w, h):
    return pl.BlockSpec((d, w), lambda b, *_: (0, h), pipeline_mode=pl.Buffered(1))


def shape(s, t):
    return jax.ShapeDtypeStruct(s, t)


def fast(s, t):
    return pltpu.VMEM(s, t)


def slow(s, t):
    return pltpu.HBM(s, t)


def in_vmem(*arrays):
    return tuple(pltpu.with_memory_space_constraint(a, pltpu.VMEM) for a in arrays)


def in_hbm(*arrays):
    return tuple(pltpu.with_memory_space_constraint(a, pltpu.HBM) for a in arrays)


ANY = pl.BlockSpec(memory_space=pl.ANY)
VM = pl.BlockSpec(memory_space=pltpu.VMEM)


def call(kernel, info, args, in_specs, outs, out_specs, scratch=(), grid=(1,), name=None, after=(), vmem=8, us=1):
    n_in, n_after = len(args), len(after)

    def ordered(info_ref, *refs):
        kernel(info_ref, *refs[:n_in], *refs[n_in + n_after :])

    return pl.pallas_call(
        ordered,
        grid_spec=pltpu.PrefetchScalarGridSpec(
            num_scalar_prefetch=1, grid=grid, in_specs=list(in_specs) + [ANY] * n_after, out_specs=out_specs, scratch_shapes=list(scratch)
        ),
        out_shape=outs,
        compiler_params=pltpu.CompilerParams(vmem_limit_bytes=vmem * MB),
        cost_estimate=pl.CostEstimate(flops=int(us * 1.1e9), bytes_accessed=int(us * 3.3e6), transcendentals=0),
        name=name,
    )(info, *args, *after)


def whole(a):
    return const(*a.shape)


def simple_call(kernel, info, args, outs, name, scratch=(), after=(), us=1):
    return call(kernel, info, args, [whole(a) for a in args], outs, [whole(o) for o in outs], scratch, name=name, after=after, us=us)


def cast_kernel(info, wg_ref, wv_ref, wo_ref, bv, bg, gg, gs, g_ref, vo_ref, vec_ref):
    c = wg_ref.shape[1]
    g_ref[...] = wg_ref[...].astype(BF)
    vo_ref[:, :c] = wv_ref[...].astype(BF)
    vo_ref[:, c:] = wo_ref[...].astype(BF)
    vec_ref[...] = both(jnp.concatenate([bv[...][None], bg[...][None], gg[...][None], gs[...][None], jnp.zeros((4, bv.shape[0]), F32)], 0))


def run_copies(pairs, sems):
    copies = [pltpu.make_async_copy(src, dst, sems.at[k]) for k, (src, dst) in enumerate(pairs)]
    for c in copies:
        c.start()
    for c in copies:
        c.wait()


def stack_kernel(info, *refs):
    *parts, out, sems = refs
    pairs, at = [], 0
    for ref in parts:
        n = ref.shape[0]
        pairs.append((ref, out.at[at : at + n]))
        at += n
    run_copies(pairs, sems)


def stack_call(info, parts, after, name):
    n = len(parts)
    rows, c = sum(a.shape[0] for a in parts), parts[0].shape[1]
    return call(stack_kernel, info, parts, [ANY] * n, [shape((rows, c), BF)], [ANY], [pltpu.SemaphoreType.DMA((n,))], name=name, after=after)[0]


def assemble_kernel(tensors, extra, info, *refs):
    *pieces, out, sems = refs
    where = ((0, 0), (1, 0), (0, 1), (1, 1))
    d, c = out.shape[0] - extra, out.shape[1] // (2 * tensors)
    n = 4
    r = d // (2 * n)
    pairs = []
    for ref, (xr, slot) in zip(pieces, where):
        for t in range(tensors):
            src, dst = slice(t * c, (t + 1) * c), slice((2 * t + slot) * c, (2 * t + slot + 1) * c)
            for k in range(n):
                row = pl.multiple_of((lax.rem(info[1] + (n - k), n) * 2 + jnp.bitwise_xor(info[2], xr)) * r, r)
                pairs.append((ref.at[k * r : (k + 1) * r, src], out.at[pl.ds(row, r), dst]))
            if xr == 0 and extra:
                pairs.append((ref.at[n * r :, src], out.at[d:, dst]))
    run_copies(pairs, sems)


def assemble_call(info, pieces, tensors, extra, after, name):
    rows, c = pieces[0].shape
    s = (2 * (rows - extra) + extra, 2 * c)
    return call(lambda *a: assemble_kernel(tensors, extra, *a), info, pieces, [ANY] * len(pieces), [shape(s, BF)],
                [const(*s)], [pltpu.SemaphoreType.DMA((18 * tensors,))], name=name, after=after)[0]


def shift_of(b):
    return 4 * b


def norm_kernel(info, x_ref, g_ref, gain_ref, shift_ref, n_ref, gw_ref, gsum_ref, rows):
    b = pl.program_id(0)

    @pl.when(b == 0)
    def _():
        gsum_ref[...] = jnp.zeros_like(gsum_ref)

    own = jnp.where(b == pl.num_programs(0) - 1, 1.0, 0.0)
    up = WIN - shift_of(b)
    for r in range(0, WIN, 48):
        x = x_ref[r : r + 48, :].astype(F32)
        cen = x - jnp.mean(x, -1, keepdims=True)
        inv = lax.rsqrt(jnp.mean(cen * cen, -1, keepdims=True) + EPS)
        rows[r : r + 48, :] = cen * inv * gain_ref[...][None] + shift_ref[...][None]
    n_ref[b] = pltpu.roll(rows[...], up, 0).astype(BF)
    g = g_ref[...].astype(F32)
    gw_ref[b] = pltpu.roll(g, up, 0).astype(BF)
    gsum_ref[...] += jnp.sum(fold8(g[:STEP]) + fold8(g[STEP:]) * own, 0, keepdims=True)


def window_rows(d):
    return pl.BlockSpec((pl.Element(WIN), pl.Element(d)), lambda b, *_: (b * STEP, 0))


def norm_call(info, x, g, gain, shift, n, after):
    d = x.shape[1]
    return call(norm_kernel, info, in_hbm(x, g, gain, shift), [window_rows(d), window_rows(d), const(d), const(d)],
                [fast((n, WIN, d), BF), fast((n, WIN, d), BF), shape((1, d), F32)], [VM, VM, const(1, d)],
                [pltpu.VMEM((WIN, d), F32)], grid=(n,), name="input_norm", after=after, us=3)


def windows_kernel(info, sp_ref, sb_ref, s_ref, st_ref, sbw_ref, token, pad, tpad, col):
    p = sp_ref.shape[0]
    b = pl.program_id(0)

    @pl.when(b == 0)
    def _():
        pad[...] = jnp.zeros_like(pad)
        pad[0:p, 0:p] = sp_ref[...]
        tpad[...] = pad[...].T
        col[...] = jnp.concatenate([jnp.broadcast_to(sb_ref[...][None], (128, p)), jnp.zeros((128, PAD - p), F32)], 1).T
        token[...] = jnp.zeros_like(token)

    ri = lax.broadcasted_iota(jnp.int32, (WIN, WIN), 0)
    ci = lax.broadcasted_iota(jnp.int32, (WIN, WIN), 1)
    end = count_of(info, b)
    live = (ri < end) & (ci < end)
    s_ref[b] = jnp.where(live, pad[:WIN, :WIN], 0.0).astype(BF)
    st_ref[b] = jnp.where(live, tpad[:WIN, :WIN], 0.0).astype(BF)
    sbw_ref[b] = jnp.where((ri < end)[:, :128], col[:WIN], 0.0)


def count_of(info, b):
    return info[8 + info[5] + b]


def windows_call(info, spatial, sbias, n, after):
    p = spatial.shape[0]
    win = fast((n, WIN, WIN), BF)
    return call(windows_kernel, info, in_hbm(spatial, sbias), [const(p, p), const(p)], [win, win, fast((n, WIN, 128), F32), shape((8, 128), F32)],
                [VM, VM, VM, const(8, 128)], [pltpu.VMEM((PAD, PAD), F32)] * 2 + [pltpu.VMEM((PAD, 128), F32)],
                grid=(n,), name="windows", after=after, us=2)


def gate_kernel(info, wa_ref, wb_ref, n_ref, s_ref, sb_ref, rows_ref, hat_ref, slope_ref, inv_ref, shifted_ref, v_ref, pre):
    b = pl.program_id(0)
    w = wa_ref.shape[1]
    d = wa_ref.shape[0] - 16
    width = 2 * w

    @pl.when(b == 0)
    def _():
        for k, ref in enumerate((wa_ref, wb_ref)):
            v = ref[d:, :].astype(F32)
            v_ref[:, k * w : (k + 1) * w] = v[:8] + v[8:]

    bias, gain, shift = v_ref[1:2, :], v_ref[2:3, :], v_ref[3:4, :]
    pre[:, :w] = dot(n_ref[b], wa_ref[:d, :])
    pre[:, w:] = dot(n_ref[b], wb_ref[:d, :])
    for r in range(0, WIN, CH):
        act, slope = gelu_both(pre[r : r + CH, :] + bias)
        slope_ref[b, r : r + CH, :] = slope.astype(BF)
        cen = act - jnp.sum(act, -1, keepdims=True) * (1.0 / width)
        inv = lax.rsqrt(jnp.sum(cen * cen, -1, keepdims=True) * (1.0 / width) + EPS)
        hat = cen * inv
        inv_ref[b, r : r + CH, :] = jnp.broadcast_to(inv, (CH, 128))
        hat_ref[b, r : r + CH, :] = hat.astype(BF)
        rows_ref[b, r : r + CH, :] = (hat * gain + shift).astype(BF)
    rows_ref[b, WIN:, :] = jnp.ones((EXT - WIN, width), BF)
    sb = sb_ref[b]
    mixed = dot(s_ref[b], rows_ref[b, :WIN, :])
    for t in range(0, width, 128):
        shifted_ref[b, :, t : t + 128] = (mixed[:, t : t + 128] + sb).astype(BF)


def gate_call(info, halves, normed, s, sb, after):
    n, _, d = normed.shape
    w = 2 * halves[0].shape[1]
    big = fast((n, WIN, w), BF)
    return call(
        gate_kernel, info, (*halves, *in_vmem(normed, s, sb)), [whole(a) for a in halves] + [VM] * 3,
        [fast((n, EXT, w), BF), big, big, fast((n, WIN, 128), F32), big, shape((8, w), F32)], [VM] * 5 + [const(8, w)],
        [pltpu.VMEM((WIN, w), F32)], grid=(n,), name="gate_forward", after=after, us=1, vmem=8,
    )


def value_kernel(h, info, wv_ref, wo_ref, n_ref, g_ref, v_ref, shifted_ref, rows_ref, gin_ref, prod_ref, dshift_ref, dpre_ref, gw_ref, gb_ref, gsp_ref, small_ref,
                 pre, dprod):
    b = pl.program_id(0)
    n_img = pl.num_programs(0)
    d, w = wv_ref.shape
    cols = slice(h * w, (h + 1) * w)

    @pl.when(b == 0)
    def _():
        gb_ref[...] = jnp.zeros_like(gb_ref)
        gsp_ref[...] = gin_ref[...]

    pre[...] = dot(n_ref[b], wv_ref[...])
    dprod[...] = dot(g_ref[b], wo_ref[...])
    bias = v_ref[0:1, :]
    for r in range(0, WIN, CH):
        act, slope = gelu_both(pre[r : r + CH, :] + bias)
        sh = shifted_ref[b, r : r + CH, cols].astype(F32)
        dp = dprod[r : r + CH, :]
        prod = (act * sh).astype(BF)
        prod_ref[b, r : r + CH, :] = prod
        dshift_ref[b, r : r + CH, :] = (dp * act).astype(BF)
        dv = dp * sh * slope
        dvl = dv.astype(BF)
        dpre_ref[b, r : r + CH, :] = dvl
        gb_ref[...] += fold8(dv)
    part = dot_nt(dshift_ref[b], rows_ref[b, :, cols])
    end = count_of(info, b)
    ri = lax.broadcasted_iota(jnp.int32, (WIN, EXT), 0)
    ci = lax.broadcasted_iota(jnp.int32, (WIN, EXT), 1)
    live = (ri < end) & ((ci < end) | (ci >= WIN))
    gsp_ref[:WIN, :EXT] += jnp.where(live, part, 0.0)

    @pl.when(b == n_img - 1)
    def _():
        gwv = dot_tn(n_ref[...].reshape(-1, d), dpre_ref[...].reshape(-1, w))
        gw_ref[:d, :] = gwv.astype(gw_ref.dtype)
        gw_ref[d:, :] = dot_tn(g_ref[...].reshape(-1, d), prod_ref[...].reshape(-1, w)).astype(gw_ref.dtype)
        small_ref[...] = jnp.concatenate([row_sums(gwv, wv_ref), back_sum(gb_ref[...], wv_ref), jnp.zeros((6, d), F32)], 0)


def row_sums(gw, w_ref):
    prod = gw * w_ref[...].astype(F32)
    t = prod[:, :128]
    for k in range(128, prod.shape[1], 128):
        t = t + prod[:, k : k + 128]
    return jnp.sum(t.T, 0, keepdims=True)


def back_sum(sums, w_ref):
    hi, lo = split(sums)
    return jnp.sum(dot_nt(hi, w_ref[...]) + dot_nt(lo, w_ref[...]), 0, keepdims=True)


def value_call(info, h, keep, vo, normed, g, vecs, shifted, rows, gsp, after=()):
    n, _, d = normed.shape
    w = vecs.shape[1] // 2
    big = fast((n, WIN, w), BF)
    return call(
        lambda *a: value_kernel(h, *a), info, (vo, vo, *in_vmem(normed, g), vecs, *in_vmem(shifted, rows), gsp),
        [side(d, w, 0), side(d, w, 1), VM, VM, pl.BlockSpec((8, w), lambda b, *_: (0, h)), VM, VM, const(PAD, PAD)],
        [big, big, big, shape((2 * d, w), BF), shape((8, w), F32), shape((PAD, PAD), F32), shape((8, d), F32)],
        [VM] * 3 + [const(2 * d, w), const(8, w), const(PAD, PAD), const(8, d)],
        [pltpu.VMEM((WIN, w), F32)] * 2, grid=(n,), name="value_own" if keep else "value_other", after=after, us=1, vmem=12,
    )


def back_kernel(info, n_ref, dsa_ref, dsb_ref, rows_hat_ref, slope_ref, inv_ref, st_ref, v_ref, wa_ref, wb_ref, gba_ref, gbb_ref, sma_ref, smb_ref, gsum_ref,
                dpre_ref, keep_ref, send_ref, vown_ref, dgr, gb, gg, gsh):
    b = pl.program_id(0)
    n_img = pl.num_programs(0)
    d, w = n_ref.shape[2], wa_ref.shape[1]
    width = 2 * w
    wa_ref, wb_ref = wa_ref.at[:d], wb_ref.at[:d]

    @pl.when(b == 0)
    def _():
        for r in (gb, gg, gsh):
            r[...] = jnp.zeros_like(r)

    gain = v_ref[2:3, :]
    dgr[:, :w] = dot(st_ref[b], dsa_ref[b])
    dgr[:, w:] = dot(st_ref[b], dsb_ref[b])
    for r in range(0, WIN, CH):
        dr = dgr[r : r + CH, :]
        hat = rows_hat_ref[b, r : r + CH, :].astype(F32)
        gg[...] += fold8(dr * hat)
        gsh[...] += fold8(dr)
        dg = dr * gain
        m1 = jnp.sum(dg, -1, keepdims=True) * (1.0 / width)
        m2 = jnp.sum(dg * hat, -1, keepdims=True) * (1.0 / width)
        dpg = (dg - m1 - hat * m2) * inv_ref[b, r : r + CH, 0:1] * slope_ref[b, r : r + CH, :].astype(F32)
        dpre_ref[b, r : r + CH, :] = dpg.astype(BF)
        gb[...] += fold8(dpg)

    @pl.when(b == n_img - 1)
    def _():
        gw = dot_tn(n_ref[...].reshape(-1, d), dpre_ref[...].reshape(-1, width))
        keep_ref[...] = gw[:, :w].astype(BF)
        sums = gb[...]
        send_ref[:d, :] = gw[:, w:].astype(BF)
        t = sma_ref[0:1, :] + smb_ref[0:1, :] + row_sums(gw[:, :w], wa_ref) + row_sums(gw[:, w:], wb_ref)
        s = sma_ref[1:2, :] + smb_ref[1:2, :] + back_sum(sums[:, :w], wa_ref) + back_sum(sums[:, w:], wb_ref)
        one = lambda v: jnp.sum(v, 0, keepdims=True)
        fours = [jnp.concatenate([one(gba_ref[...]), one(gbb_ref[...])], 1), one(gb[...]), one(gg[...]), one(gsh[...])]
        wide = lambda v: jnp.concatenate([v, jnp.zeros((1, w - d), F32)], 1)
        full = jnp.concatenate([wide(t), wide(s), wide(gsum_ref[...]), jnp.zeros((1, w), F32)], 0)
        fours = jnp.concatenate(fours, 0)
        hi, lo = split(jnp.concatenate([fours[:, w:], full], 0))
        send_ref[d:, :] = jnp.concatenate([hi, lo], 0)
        fhi, flo = split(full)
        vown_ref[...] = jnp.concatenate([fours[:, :w], fhi.astype(F32) + flo.astype(F32)], 0)


def back_call(info, normed, ds, hat, slope, inv, st, vecs, wg, gbv, small, gsum, after):
    n, _, d = normed.shape
    width = vecs.shape[1]
    w = width // 2
    return call(
        back_kernel, info, (*in_vmem(normed, *ds, hat, slope, inv, st), vecs, *wg, *gbv, *small, gsum),
        [VM] * 7 + [const(8, width), whole(wg[0]), whole(wg[1]), const(8, w), const(8, w), const(8, d), const(8, d), const(1, d)],
        [fast((n, WIN, width), BF), shape((d, w), BF), shape((d + 16, w), BF), shape((8, w), F32)],
        [VM, const(d, w), const(d + 16, w), const(8, w)],
        [pltpu.VMEM((WIN, width), F32)] + [pltpu.VMEM((8, width), F32)] * 3, grid=(n,), name="gate_backward", after=after, us=1, vmem=14,
    )


def joined(v, carry):
    b = pl.program_id(0)

    @pl.when(b == 0)
    def _():
        carry[...] = jnp.zeros_like(carry)

    v = pltpu.roll(v, shift_of(b), 0)
    v = jnp.concatenate([v[:16] + carry[...], v[16:]], 0)
    carry[...] = v[STEP:]
    return v


def result_kernel(info, x_ref, pa_ref, pb_ref, woa_ref, wob_ref, bias_ref, res_ref, token, carry):
    b = pl.program_id(0)
    token[...] = jnp.zeros_like(token)
    finish = lambda x, br: (x.astype(F32) + br + bias_ref[...][None]).astype(BF)

    @pl.when(b < pl.num_programs(0) - 1)
    def _():
        br = joined(dot_nt(pa_ref[b], woa_ref[...]) + dot_nt(pb_ref[b], wob_ref[...]), carry)
        res_ref[...] = finish(x_ref[:STEP, :], br[:STEP])

    @pl.when(b == pl.num_programs(0) - 1)
    def _():
        res_ref[:16, :] = finish(x_ref[STEP:, :], carry[...])


def grad_kernel(info, x_ref, g_ref, va_ref, vb_ref, dg_ref, wva_ref, wvb_ref, wga_ref, wgb_ref, gain_ref, ing_ref, token, carry):
    b = pl.program_id(0)
    token[...] = jnp.zeros_like(token)
    d, w = wva_ref.shape

    def finish(x, g, dn):
        x = x.astype(F32)
        cen = x - jnp.mean(x, -1, keepdims=True)
        inv = lax.rsqrt(jnp.mean(cen * cen, -1, keepdims=True) + EPS)
        hat = cen * inv
        dx = dn * gain_ref[...][None]
        m1 = jnp.mean(dx, -1, keepdims=True)
        m2 = jnp.mean(dx * hat, -1, keepdims=True)
        return g.astype(F32) + inv * (dx - m1 - hat * m2)

    @pl.when(b < pl.num_programs(0) - 1)
    def _():
        dn = dot_nt(va_ref[b], wva_ref[...]) + dot_nt(vb_ref[b], wvb_ref[...])
        dn = joined(dn + dot_nt(dg_ref[b, :, :w], wga_ref[:d, :]) + dot_nt(dg_ref[b, :, w:], wgb_ref[:d, :]), carry)
        ing_ref[...] = finish(x_ref[:STEP, :], g_ref[:STEP, :], dn[:STEP])

    @pl.when(b == pl.num_programs(0) - 1)
    def _():
        ing_ref[:16, :] = finish(x_ref[STEP:, :], g_ref[STEP:, :], carry[...])


def last_rows(n, d):
    return pl.BlockSpec((pl.Element(WIN), pl.Element(d)), lambda b, *_: (jnp.minimum(b, n - 1) * STEP, 0))


def row_block(d):
    return pl.BlockSpec((STEP, d), lambda b, *_: (b, 0))


def result_call(info, x, prod, vo, bias, after):
    n, _, w = prod[0].shape
    rows, d = x.shape
    return call(
        result_kernel, info, (*in_hbm(x), *in_vmem(*prod), *vo, *in_hbm(bias)),
        [last_rows(n, d), VM, VM, side(d, w, 1), side(d, w, 1), const(d)],
        [slow((rows, d), BF), shape((8, 128), F32)], [row_block(d), const(8, 128)], [pltpu.VMEM((16, d), F32)], grid=(n + 1,), name="result", after=after, us=1, vmem=10,
    )


def grad_call(info, x, g, dpv, dpg, vo, wg, gain, after):
    n, _, w = dpv[0].shape
    rows, d = x.shape
    return call(
        grad_kernel, info, (*in_hbm(x, g), *in_vmem(*dpv, dpg), *vo, *wg, *in_hbm(gain)),
        [last_rows(n, d), last_rows(n, d), VM, VM, VM] + [side(d, w, 0)] * 2 + [whole(wg[0]), whole(wg[1]), const(d)],
        [slow((rows, d), F32), shape((8, 128), F32)], [row_block(d), const(8, 128)], [pltpu.VMEM((16, d), F32)], grid=(n + 1,), name="input_grad", after=after, us=1, vmem=16,
    )


VROWS = 32


def quarter_kernel(tensors, extra, info, *refs):
    if extra == "spatial":
        keep, recv, gsp, *outs = refs
    else:
        keep, recv, vown, *outs = refs
    x, y, core = info[2], info[3], info[4]
    d = keep.shape[0] // tensors
    c = keep.shape[1] // 2
    nz = 4
    r = d // (2 * nz)
    for a, out in enumerate(outs):
        for b in range(2):
            xr, yr = jnp.where(core == 0, b, a), jnp.where(core == 0, a, b)
            cols = pl.ds(pl.multiple_of(yr * c, c), c)
            for t in range(tensors):
                for z in range(nz):
                    row = pl.multiple_of(t * d + (2 * z + jnp.bitwise_xor(x, xr)) * r, r)
                    dst = t * nz * r + z * r
                    out[b, dst : dst + r, :] = (keep[pl.ds(row, r), cols].astype(F32) + recv[pl.ds(row, r), cols].astype(F32)).astype(out.dtype)
            at = tensors * nz * r
            if extra == "spatial":
                q = PAD // 4
                row = pl.multiple_of((2 * jnp.bitwise_xor(x, xr) + jnp.bitwise_xor(y, yr)) * q, q)
                out[b, at:, :] = gsp[pl.ds(row, q), :].astype(BF).astype(out.dtype)
            else:
                got = recv[d:, :].astype(F32)
                v = vown[...] + (got[:8] + got[8:])
                four = jnp.where(yr == 0, v[0:4, :c], v[0:4, c:])
                v = jnp.concatenate([four, v[4:7, :c], jnp.concatenate([v[4:7, c : c + 128], jnp.zeros((3, c - 128), F32)], 1), jnp.zeros((6, c), F32)], 0)
                out[b, at:, :] = both(v).astype(out.dtype)


def both(v):
    hi, lo = split(v)
    return jnp.concatenate([hi, lo], 0)


def rounded(v):
    return both(v[:16] + v[16:]) if v.shape[0] == VROWS else v.astype(BF)


def plane_kernel(extra, info, parts, recv, keep, send):
    m = keep.shape[0] - extra
    for b, out in enumerate((keep, send)):
        out[:m, :] = (parts[b, :m, :] + recv[b, :m, :].astype(F32)).astype(out.dtype)
        out[m:, :] = rounded(parts[b, m:, :] + recv[b, m:, :].astype(F32)).astype(out.dtype)


def line_kernel(tensors, chunks, extra, info, part, recv, keep, send):
    m = part.shape[0] - extra
    r = m // (tensors * chunks)
    h = chunks // 2
    bit = lax.rem(lax.div(info[1], h), 2)
    for out, which in ((keep, bit), (send, 1 - bit)):
        for t in range(tensors):
            rows = pl.ds(pl.multiple_of((t * chunks + which * h) * r, r), h * r)
            out[t * h * r : (t + 1) * h * r, :] = (part[rows, :] + recv[rows, :].astype(F32)).astype(out.dtype)
        out[tensors * h * r :, :] = rounded(part[m:, :] + recv[m:, :].astype(F32)).astype(out.dtype)


def finish_vo_kernel(info, part, recv, gwv, gwo, sp):
    r = gwv.shape[0]
    v = part[...] + recv[...].astype(F32)
    gwv[...] = v[:r]
    gwo[...] = v[r : 2 * r]
    sp[...] = v[2 * r :].astype(BF)


def finish_g_kernel(info, part, recv, gain, shift, gwg, gbv, gbg, ggain, gshift, rows):
    r = gwg.shape[0]
    v = part[...] + recv[...].astype(F32)
    gwg[...] = v[:r]
    v = v[r : r + 16] + v[r + 16 :]
    for k, out in enumerate((gbv, gbg, ggain, gshift)):
        out[...] = v[k]
    full = jnp.concatenate([v[4:7, :], v[7:10, :128]], 1)
    gin = (full[0:1, :] - shift[...][None] * full[1:2, :]) / gain[...][None]
    rows[...] = jnp.concatenate([gin, full[1:], jnp.zeros((5, full.shape[1]), F32)], 0)


def pair_kernel(info, a, b, out):
    out[...] = (a[...].astype(F32) + b[...].astype(F32)).astype(BF)


def spatial_kernel(info, a, rx, ry, rxy, mine, other, out, bias, gin, sin, gout, full):
    q = a.shape[0]
    for ref, k in ((a, 0), (ry, 1), (rx, 2), (rxy, 3)):
        full[pl.ds(pl.multiple_of(jnp.bitwise_xor(2 * info[2] + info[3], k) * q, q), q), :] = ref[...].astype(F32)
    p = out.shape[0]
    out[...] = full[:p, :p]
    bias[...] = full[:, 256:].T[WIN - 256, :p]
    v = jnp.where(info[4] == 0, mine[...], other[...])
    gin[...] = v[0]
    sin[...] = v[1]
    gout[...] = v[2]


def permute(x, to):
    n_dp, n_mp = lax.axis_size("dp"), lax.axis_size("mp")
    pairs = []
    for i in range(n_dp * n_mp):
        dp, mp = to(i // n_mp, i % n_mp)
        pairs.append((i, dp * n_mp + mp))
    return lax.ppermute(x, AXES, pairs)


def core_swap(x):
    return permute(x, lambda dp, mp: (dp, mp ^ 1))


def plane_swaps(a, b, c):
    return (
        permute(a, lambda dp, mp: (dp ^ 1, mp)),
        permute(b, lambda dp, mp: (dp, mp ^ 2)),
        permute(c, lambda dp, mp: (dp ^ 1, mp ^ 2)),
    )


def first_swap(x):
    return permute(x, lambda dp, mp: (dp, mp ^ 2) if mp % 2 == 0 else (dp ^ 1, mp))


def second_swap(x):
    return permute(x, lambda dp, mp: (dp ^ 1, mp) if mp % 2 == 0 else (dp, mp ^ 2))


def z_swap(x, bit):
    return permute(x, lambda dp, mp: (dp ^ (2 * bit), mp))


def line_swaps(arrays):
    n_dp = lax.axis_size("dp")
    return [permute(a, lambda dp, mp, k=k: ((dp + 2 * (k + 1)) % n_dp, mp)) for k, a in enumerate(arrays)]


def gather_dp(copies):
    t = lax.all_to_all(copies, "dp", 0, 0, tiled=True)
    return t.reshape(-1, t.shape[2])


def after(x, y):
    return lax.optimization_barrier((x, y))


def y_swap(x):
    return permute(x, lambda dp, mp: (dp, mp ^ 2))


def scatter_any(keep, recv):
    n = lax.axis_size("dp")
    c = keep.shape[1] // 2
    a = keep.astype(F32) + recv.astype(F32)
    s = a[:, :c] + permute(a[:, c:].astype(BF), lambda dp, mp: (dp, mp ^ 2)).astype(F32)
    return lax.all_to_all(s.astype(BF).reshape(n, -1, c), "dp", 0, 0, tiled=True).astype(F32).sum(0)


def body(inputs, counts, input_norm_gain, shift_in, w_value, w_gate, bias_value, bias_gate, gate_gain, gate_shift, spatial, spatial_bias, w_out, out_bias, cotangent):
    n_dp, n_mp = lax.axis_size("dp"), lax.axis_size("mp")
    me, dp = lax.axis_index("mp"), lax.axis_index("dp")
    r, c = w_value.shape
    d = inputs.shape[1]
    p = spatial.shape[0]
    n = counts.shape[0] // n_mp
    quick = n_dp == 8 and r % 16 == 0
    head = jnp.stack([me, dp // 2, dp % 2, me // 2, me % 2, me * n, 0, 0]).astype(jnp.int32)
    info = jnp.concatenate([head, counts])

    args = in_hbm(w_gate, w_value, w_out.T, bias_value, bias_gate, gate_gain, gate_shift)
    pg, vo1, vec = simple_call(cast_kernel, info, args, [shape((r, c), BF), shape((r, 2 * c), BF), shape((16, c), BF)], "casts")
    if quick:
        zg, zvo = line_swaps([pg] * 3), line_swaps([vo1] * 3)
        zg = stack_call(info, (pg, *zg, vec), (), "line_gate")
        pieces = (zg, *plane_swaps(zg, zg, zg))
    else:
        copies = lambda a: gather_dp(jnp.broadcast_to(a[None], (n_dp,) + a.shape))
        g0 = jnp.concatenate([copies(pg), vec])
        zg = wga = jnp.concatenate([g0, y_swap(g0)], 1)
        vo0 = copies(vo1)
        vo2 = y_swap(vo0)
        zvo = ()
        voa = jnp.concatenate([vo0[:, :c], vo2[:, :c], vo0[:, c:], vo2[:, c:]], 1)
    normed, g_win, gsum = norm_call(info, inputs, cotangent, input_norm_gain, shift_in, n, (zg,))
    s, st, sb, token = windows_call(info, spatial, spatial_bias, n, (gsum, *zvo))
    if quick:
        wga = assemble_call(info, pieces, 1, 16, (token,), "assemble_gate")
        zvo = stack_call(info, (vo1, *zvo), (wga,), "line_value_out")
        pieces = (zvo, *plane_swaps(zvo, zvo, zvo))
    wgb = core_swap(wga)
    rows, hat, slope, inv, shifted, vec = gate_call(info, (wga, wgb), normed, s, sb, (zvo,) if quick else ())
    if quick:
        voa = assemble_call(info, pieces, 2, 0, (vec,), "assemble_value_out")
    vob = core_swap(voa)
    zero = jnp.zeros((PAD, PAD), F32)
    prod_b, ds_b, dpv_b, gw_b, gb_b, gsp, small_b = value_call(info, 1, False, vob, normed, g_win, vec, shifted, rows, zero)
    recv_vo = core_swap(gw_b)
    prod_a, ds_a, dpv_a, gw_a, gb_a, gsp, small_a = value_call(info, 0, True, voa, normed, g_win, vec, shifted, rows, gsp)
    q = PAD // 4
    def quarters(tensors, extra, args, rows, name, after):
        return simple_call(lambda *a: quarter_kernel(tensors, extra, *a), info, args, [shape((2, rows, c), F32), shape((2, rows, c), BF)], name, after=after)

    def plane(parts, recv, extra, name, after):
        s = parts.shape[1:]
        return simple_call(lambda *a: plane_kernel(extra, *a), info, (parts, recv), [shape(s, F32), shape(s, BF)], name, after=after)

    def line(part, recv, tensors, chunks, extra, name, after):
        s = ((part.shape[0] - extra) // 2 + extra, c)
        return simple_call(lambda *a: line_kernel(tensors, chunks, extra, *a), info, (part, recv), [shape(s, F32), shape(s, BF)], name, after=after)

    if quick:
        kvo, snd = quarters(2, "spatial", (gw_a, recv_vo, gsp), 8 * r + q, "quarters_vo", ())
        got_vo = first_swap(snd)
    dpg, keep_g, send_g, vown = back_call(info, normed, (ds_a, ds_b), hat, slope, inv, st, vec, (wga, wgb), (gb_a, gb_b), (small_a, small_b), gsum, (snd,) if quick else ())
    recv_g = core_swap(send_g)
    if quick:
        kvo, snd = plane(kvo, got_vo, q, "plane_vo", (vown,))
        got_vo = second_swap(snd)
        kg, snd = quarters(1, "vectors", (keep_g, recv_g, vown), 4 * r + VROWS, "quarters_g", (snd,))
        got_g = first_swap(snd)
    res, token = result_call(info, inputs, (prod_a, prod_b), (voa, vob), out_bias, (snd if quick else vown,))
    if quick:
        kvo, snd = line(kvo, got_vo, 2, 4, q, "line_vo", (token,))
        got_vo = z_swap(snd, 2)
        kg, snd = plane(kg, got_g, VROWS, "plane_g", (snd,))
        got_g = second_swap(snd)
        ing, token = grad_call(info, inputs, cotangent, (dpv_a, dpv_b), dpg, (voa, vob), (wga, wgb), input_norm_gain, (snd,))
        kg, snd = line(kg, got_g, 1, 4, VROWS, "line_g", (token,))
        got_g = z_swap(snd, 2)
        kvo, snd = line(kvo, got_vo, 2, 2, q, "pair_vo", (snd,))
        got_vo = z_swap(snd, 1)
        kg, snd = line(kg, got_g, 1, 2, VROWS, "pair_g", (snd,))
        got_g = z_swap(snd, 1)
        gwv, gwo, sp = simple_call(finish_vo_kernel, info, (kvo, got_vo), [shape((r, c), F32), shape((r, c), F32), shape((q, c), BF)], "finish_vo", after=(snd,))
        (sp,) = simple_call(pair_kernel, info, (sp, core_swap(sp)), [shape((q, c), BF)], "spatial_pair")
        sps = plane_swaps(sp, sp, sp)
        one = shape((c,), F32)
        gwg, gbv, gbg, ggain, gshift, full = simple_call(
            finish_g_kernel, info, (kg, got_g, *in_hbm(input_norm_gain, shift_in)),
            [shape((r, c), F32)] + [one] * 4 + [shape((8, d), F32)], "finish_g", after=(sp,))
        gspat, gsb, gin, sin, gob = simple_call(spatial_kernel, info, (sp, *sps, full, core_swap(full)), [shape((p, p), F32), shape((p,), F32)] + [shape((d,), F32)] * 3, "spatial_sum", [pltpu.VMEM((PAD, PAD), F32)])
    else:
        ing, _ = grad_call(info, inputs, cotangent, (dpv_a, dpv_b), dpg, (voa, vob), (wga, wgb), input_norm_gain, ())
        gwv = scatter_any(gw_a[:d], recv_vo[:d])
        gwo = scatter_any(gw_a[d:], recv_vo[d:])
        gwg = scatter_any(keep_g, recv_g[:d])
        gsp = lax.psum(gsp, AXES)
        gspat, gsb = gsp[:p, :p], gsp[:p, WIN]
        other = send_g[d:].astype(F32)
        other = other[:8] + other[8:]
        back = jnp.argsort(jnp.bitwise_xor(jnp.array(ORDER, jnp.int32), me))
        four = jnp.concatenate([vown[:4], other[:4]], 1).reshape(4, n_mp, c)
        four = lax.psum(jnp.take(four, back, axis=1), AXES)
        gbv, gbg, ggain, gshift = lax.dynamic_index_in_dim(four, me, 1, keepdims=False)
        t, sin, gob = lax.psum(vown[4:7, :d], AXES)
        gin = (t - shift_in * sin) / input_norm_gain
    return (res, ing, gin, sin, gwv, gwg, gbv, gbg, ggain, gshift, gspat, gsb, gwo.T, gob)


def solution(mesh):
    row, wi, mp, al = P(("dp", "mp"), None), P("dp", "mp"), P("mp"), P()
    return jax.shard_map(
        body, mesh=mesh,
        in_specs=(row, P("dp"), al, al, wi, wi, mp, mp, mp, mp, al, al, P("mp", "dp"), al, row),
        out_specs=(row, row, al, al, wi, wi, mp, mp, mp, mp, al, al, P("mp", "dp"), al),
        check_vma=False,
    )
```

```python
import jax
import jax.numpy as jnp
from jax import lax
from jax.experimental import pallas as pl
from jax.experimental.pallas import tpu as pltpu
from jax.sharding import PartitionSpec as P

EPS = 1e-5
BF = jnp.bfloat16
F32 = jnp.float32
AXES = ("dp", "mp")
WIN = 336
STEP = 320
EXT = 352
CH = 16
PAD = 384
ORDER = (0, 2, 1, 3)
GELU_C = (7.97869712e-01, 3.63922863e-02, -8.78266205e-05, -3.66934307e-05, 1.42500480e-06)
LOG2E_HALF = -0.7213475204444817
INV_SQRT_2PI = 0.3989422804014327
MB = 2**20


def dot(a, b):
    return jnp.dot(a, b, preferred_element_type=F32)


def dot_tn(a, b):
    return lax.dot_general(a, b, (((0,), (0,)), ((), ())), preferred_element_type=F32)


def dot_nt(a, b):
    return lax.dot_general(a, b, (((1,), (1,)), ((), ())), preferred_element_type=F32)


def gelu_both(x):
    u = x * x
    p = GELU_C[4]
    for c in GELU_C[3::-1]:
        p = p * u + c
    cdf = 0.5 + 0.5 * jnp.tanh(x * p)
    slope = cdf + (x * INV_SQRT_2PI) * jnp.exp2(u * LOG2E_HALF)
    return x * cdf, slope


def split(v):
    hi = v.astype(BF)
    return hi, (v - hi.astype(F32)).astype(BF)


def fold8(v):
    out = v[0:8]
    for r in range(8, v.shape[0], 8):
        out = out + v[r : r + 8]
    return out


def img(*s):
    return pl.BlockSpec((1,) + s, lambda b, *_: (b,) + (0,) * len(s))


def const(*s):
    return pl.BlockSpec(s, lambda b, *_: (0,) * len(s), pipeline_mode=pl.Buffered(1))


def half(rows, c, h):
    return pl.BlockSpec((1, rows, c), lambda b, *_: (b, 0, h))


def side(d, w, h):
    return pl.BlockSpec((d, w), lambda b, *_: (0, h), pipeline_mode=pl.Buffered(1))


def shape(s, t):
    return jax.ShapeDtypeStruct(s, t)


def fast(s, t):
    return pltpu.VMEM(s, t)


def slow(s, t):
    return pltpu.HBM(s, t)


def in_vmem(*arrays):
    return tuple(pltpu.with_memory_space_constraint(a, pltpu.VMEM) for a in arrays)


def in_hbm(*arrays):
    return tuple(pltpu.with_memory_space_constraint(a, pltpu.HBM) for a in arrays)


ANY = pl.BlockSpec(memory_space=pl.ANY)
VM = pl.BlockSpec(memory_space=pltpu.VMEM)


def call(kernel, info, args, in_specs, outs, out_specs, scratch=(), grid=(1,), name=None, after=(), vmem=8, us=1):
    n_in, n_after = len(args), len(after)

    def ordered(info_ref, *refs):
        kernel(info_ref, *refs[:n_in], *refs[n_in + n_after :])

    return pl.pallas_call(
        ordered,
        grid_spec=pltpu.PrefetchScalarGridSpec(
            num_scalar_prefetch=1, grid=grid, in_specs=list(in_specs) + [ANY] * n_after, out_specs=out_specs, scratch_shapes=list(scratch)
        ),
        out_shape=outs,
        compiler_params=pltpu.CompilerParams(vmem_limit_bytes=vmem * MB),
        cost_estimate=pl.CostEstimate(flops=int(us * 1.1e9), bytes_accessed=int(us * 3.3e6), transcendentals=0),
        name=name,
    )(info, *args, *after)


def whole(a):
    return const(*a.shape)


def simple_call(kernel, info, args, outs, name, scratch=(), after=(), us=1):
    return call(kernel, info, args, [whole(a) for a in args], outs, [whole(o) for o in outs], scratch, name=name, after=after, us=us)


SLOTS = 2
GATE_MB, VALUE_MB, BACK_MB = 11, 14, 16


def pipelined(n, products, arithmetic):
    for b in range(min(n, SLOTS - 1)):
        products(b)
    for b in range(n):
        if b + SLOTS - 1 < n:
            products(b + SLOTS - 1)
        arithmetic(b)


def cast_kernel(info, wg_ref, wv_ref, wo_ref, bv, bg, gg, gs, g_ref, vo_ref, vec_ref):
    c = wg_ref.shape[1]
    g_ref[...] = wg_ref[...].astype(BF)
    vo_ref[:, :c] = wv_ref[...].astype(BF)
    vo_ref[:, c:] = wo_ref[...].astype(BF)
    vec_ref[...] = both(jnp.concatenate([bv[...][None], bg[...][None], gg[...][None], gs[...][None], jnp.zeros((4, bv.shape[0]), F32)], 0))


def run_copies(pairs, sems):
    copies = [pltpu.make_async_copy(src, dst, sems.at[k]) for k, (src, dst) in enumerate(pairs)]
    for c in copies:
        c.start()
    for c in copies:
        c.wait()


def stack_kernel(info, *refs):
    *parts, out, sems = refs
    pairs, at = [], 0
    for ref in parts:
        n = ref.shape[0]
        pairs.append((ref, out.at[at : at + n]))
        at += n
    run_copies(pairs, sems)


def stack_call(info, parts, after, name):
    n = len(parts)
    rows, c = sum(a.shape[0] for a in parts), parts[0].shape[1]
    return call(stack_kernel, info, parts, [ANY] * n, [shape((rows, c), BF)], [ANY], [pltpu.SemaphoreType.DMA((n,))], name=name, after=after)[0]


def assemble_kernel(tensors, extra, info, *refs):
    *pieces, out, sems = refs
    where = ((0, 0), (1, 0), (0, 1), (1, 1))
    d, c = out.shape[0] - extra, out.shape[1] // (2 * tensors)
    n = 4
    r = d // (2 * n)
    pairs = []
    for ref, (xr, slot) in zip(pieces, where):
        for t in range(tensors):
            src, dst = slice(t * c, (t + 1) * c), slice((2 * t + slot) * c, (2 * t + slot + 1) * c)
            for k in range(n):
                row = pl.multiple_of((lax.rem(info[1] + (n - k), n) * 2 + jnp.bitwise_xor(info[2], xr)) * r, r)
                pairs.append((ref.at[k * r : (k + 1) * r, src], out.at[pl.ds(row, r), dst]))
            if xr == 0 and extra:
                pairs.append((ref.at[n * r :, src], out.at[d:, dst]))
    run_copies(pairs, sems)


def assemble_call(info, pieces, tensors, extra, after, name):
    rows, c = pieces[0].shape
    s = (2 * (rows - extra) + extra, 2 * c)
    return call(lambda *a: assemble_kernel(tensors, extra, *a), info, pieces, [ANY] * len(pieces), [shape(s, BF)],
                [const(*s)], [pltpu.SemaphoreType.DMA((18 * tensors,))], name=name, after=after)[0]


def shift_of(b):
    return 4 * b


def norm_kernel(info, x_ref, g_ref, gain_ref, shift_ref, n_ref, gw_ref, gsum_ref, rows):
    b = pl.program_id(0)

    @pl.when(b == 0)
    def _():
        gsum_ref[...] = jnp.zeros_like(gsum_ref)

    own = jnp.where(b == pl.num_programs(0) - 1, 1.0, 0.0)
    up = WIN - shift_of(b)
    for r in range(0, WIN, 48):
        x = x_ref[r : r + 48, :].astype(F32)
        cen = x - jnp.mean(x, -1, keepdims=True)
        inv = lax.rsqrt(jnp.mean(cen * cen, -1, keepdims=True) + EPS)
        rows[r : r + 48, :] = cen * inv * gain_ref[...][None] + shift_ref[...][None]
    n_ref[b] = pltpu.roll(rows[...], up, 0).astype(BF)
    g = g_ref[...].astype(F32)
    gw_ref[b] = pltpu.roll(g, up, 0).astype(BF)
    gsum_ref[...] += jnp.sum(fold8(g[:STEP]) + fold8(g[STEP:]) * own, 0, keepdims=True)


def window_rows(d):
    return pl.BlockSpec((pl.Element(WIN), pl.Element(d)), lambda b, *_: (b * STEP, 0))


def norm_call(info, x, g, gain, shift, n, after):
    d = x.shape[1]
    return call(norm_kernel, info, in_hbm(x, g, gain, shift), [window_rows(d), window_rows(d), const(d), const(d)],
                [fast((n, WIN, d), BF), fast((n, WIN, d), BF), shape((1, d), F32)], [VM, VM, const(1, d)],
                [pltpu.VMEM((WIN, d), F32)], grid=(n,), name="input_norm", after=after, us=3)


def windows_kernel(info, sp_ref, sb_ref, s_ref, st_ref, sbw_ref, token, pad, tpad, col):
    p = sp_ref.shape[0]
    b = pl.program_id(0)

    @pl.when(b == 0)
    def _():
        pad[...] = jnp.zeros_like(pad)
        pad[0:p, 0:p] = sp_ref[...]
        tpad[...] = pad[...].T
        col[...] = jnp.concatenate([jnp.broadcast_to(sb_ref[...][None], (128, p)), jnp.zeros((128, PAD - p), F32)], 1).T
        token[...] = jnp.zeros_like(token)

    ri = lax.broadcasted_iota(jnp.int32, (WIN, WIN), 0)
    ci = lax.broadcasted_iota(jnp.int32, (WIN, WIN), 1)
    end = count_of(info, b)
    live = (ri < end) & (ci < end)
    s_ref[b] = jnp.where(live, pad[:WIN, :WIN], 0.0).astype(BF)
    st_ref[b] = jnp.where(live, tpad[:WIN, :WIN], 0.0).astype(BF)
    sbw_ref[b] = jnp.where((ri < end)[:, :128], col[:WIN], 0.0)


def count_of(info, b):
    return info[8 + info[5] + b]


def windows_call(info, spatial, sbias, n, after):
    p = spatial.shape[0]
    win = fast((n, WIN, WIN), BF)
    return call(windows_kernel, info, in_hbm(spatial, sbias), [const(p, p), const(p)], [win, win, fast((n, WIN, 128), F32), shape((8, 128), F32)],
                [VM, VM, VM, const(8, 128)], [pltpu.VMEM((PAD, PAD), F32)] * 2 + [pltpu.VMEM((PAD, 128), F32)],
                grid=(n,), name="windows", after=after, us=2)


def gate_kernel(info, wa_ref, wb_ref, n_ref, s_ref, sb_ref, rows_ref, hat_ref, slope_ref, inv_ref, shifted_ref, v_ref, pres):
    w = wa_ref.shape[1]
    d = wa_ref.shape[0] - 16
    width = 2 * w
    for k, ref in enumerate((wa_ref, wb_ref)):
        v = ref[d:, :].astype(F32)
        v_ref[:, k * w : (k + 1) * w] = v[:8] + v[8:]
    bias, gain, shift = v_ref[1:2, :], v_ref[2:3, :], v_ref[3:4, :]

    def products(b):
        pre = pres.at[b % SLOTS]
        pre[:, :w] = dot(n_ref[b], wa_ref[:d, :])
        pre[:, w:] = dot(n_ref[b], wb_ref[:d, :])

    def arithmetic(b):
        pre = pres.at[b % SLOTS]
        for r in range(0, WIN, CH):
            act, slope = gelu_both(pre[r : r + CH, :] + bias)
            slope_ref[b, r : r + CH, :] = slope.astype(BF)
            cen = act - jnp.sum(act, -1, keepdims=True) * (1.0 / width)
            inv = lax.rsqrt(jnp.sum(cen * cen, -1, keepdims=True) * (1.0 / width) + EPS)
            hat = cen * inv
            inv_ref[b, r : r + CH, :] = jnp.broadcast_to(inv, (CH, 128))
            hat_ref[b, r : r + CH, :] = hat.astype(BF)
            rows_ref[b, r : r + CH, :] = (hat * gain + shift).astype(BF)
        rows_ref[b, WIN:, :] = jnp.ones((EXT - WIN, width), BF)
        sb = sb_ref[b]
        mixed = dot(s_ref[b], rows_ref[b, :WIN, :])
        for t in range(0, width, 128):
            shifted_ref[b, :, t : t + 128] = (mixed[:, t : t + 128] + sb).astype(BF)

    pipelined(n_ref.shape[0], products, arithmetic)


def gate_call(info, halves, normed, s, sb, after):
    n, _, d = normed.shape
    w = 2 * halves[0].shape[1]
    big = fast((n, WIN, w), BF)
    return call(
        gate_kernel, info, (*halves, *in_vmem(normed, s, sb)), [whole(a) for a in halves] + [VM] * 3,
        [fast((n, EXT, w), BF), big, big, fast((n, WIN, 128), F32), big, shape((8, w), F32)], [VM] * 5 + [const(8, w)],
        [pltpu.VMEM((SLOTS, WIN, w), F32)], name="gate_forward", after=after, us=1, vmem=GATE_MB,
    )


def value_kernel(h, info, wv_ref, wo_ref, n_ref, g_ref, v_ref, shifted_ref, rows_ref, gin_ref, prod_ref, dshift_ref, dpre_ref, gw_ref, gb_ref, gsp_ref, small_ref,
                 pres, dprods):
    d, w = wv_ref.shape
    cols = slice(h * w, (h + 1) * w)
    gb_ref[...] = jnp.zeros_like(gb_ref)
    gsp_ref[...] = gin_ref[...]

    def products(b):
        pre, dprod = pres.at[b % SLOTS], dprods.at[b % SLOTS]
        pre[...] = dot(n_ref[b], wv_ref[...])
        dprod[...] = dot(g_ref[b], wo_ref[...])

    def arithmetic(b):
        pre, dprod = pres.at[b % SLOTS], dprods.at[b % SLOTS]
        bias = v_ref[0:1, :]
        for r in range(0, WIN, CH):
            act, slope = gelu_both(pre[r : r + CH, :] + bias)
            sh = shifted_ref[b, r : r + CH, cols].astype(F32)
            dp = dprod[r : r + CH, :]
            prod = (act * sh).astype(BF)
            prod_ref[b, r : r + CH, :] = prod
            dshift_ref[b, r : r + CH, :] = (dp * act).astype(BF)
            dv = dp * sh * slope
            dvl = dv.astype(BF)
            dpre_ref[b, r : r + CH, :] = dvl
            gb_ref[...] += fold8(dv)
        part = dot_nt(dshift_ref[b], rows_ref[b, :, cols])
        end = count_of(info, b)
        ri = lax.broadcasted_iota(jnp.int32, (WIN, EXT), 0)
        ci = lax.broadcasted_iota(jnp.int32, (WIN, EXT), 1)
        live = (ri < end) & ((ci < end) | (ci >= WIN))
        gsp_ref[:WIN, :EXT] += jnp.where(live, part, 0.0)

    pipelined(n_ref.shape[0], products, arithmetic)
    gwv = dot_tn(n_ref[...].reshape(-1, d), dpre_ref[...].reshape(-1, w))
    gw_ref[:d, :] = gwv.astype(gw_ref.dtype)
    gw_ref[d:, :] = dot_tn(g_ref[...].reshape(-1, d), prod_ref[...].reshape(-1, w)).astype(gw_ref.dtype)
    small_ref[...] = jnp.concatenate([row_sums(gwv, wv_ref), back_sum(gb_ref[...], wv_ref), jnp.zeros((6, d), F32)], 0)


def row_sums(gw, w_ref):
    prod = gw * w_ref[...].astype(F32)
    t = prod[:, :128]
    for k in range(128, prod.shape[1], 128):
        t = t + prod[:, k : k + 128]
    return jnp.sum(t.T, 0, keepdims=True)


def back_sum(sums, w_ref):
    hi, lo = split(sums)
    return jnp.sum(dot_nt(hi, w_ref[...]) + dot_nt(lo, w_ref[...]), 0, keepdims=True)


def value_call(info, h, keep, vo, normed, g, vecs, shifted, rows, gsp, after=()):
    n, _, d = normed.shape
    w = vecs.shape[1] // 2
    big = fast((n, WIN, w), BF)
    return call(
        lambda *a: value_kernel(h, *a), info, (vo, vo, *in_vmem(normed, g), vecs, *in_vmem(shifted, rows), gsp),
        [side(d, w, 0), side(d, w, 1), VM, VM, pl.BlockSpec((8, w), lambda b, *_: (0, h)), VM, VM, const(PAD, PAD)],
        [big, big, big, shape((2 * d, w), BF), shape((8, w), F32), shape((PAD, PAD), F32), shape((8, d), F32)],
        [VM] * 3 + [const(2 * d, w), const(8, w), const(PAD, PAD), const(8, d)],
        [pltpu.VMEM((SLOTS, WIN, w), F32)] * 2, name="value_own" if keep else "value_other", after=after, us=1, vmem=VALUE_MB,
    )


def back_kernel(info, n_ref, dsa_ref, dsb_ref, rows_hat_ref, slope_ref, inv_ref, st_ref, v_ref, wa_ref, wb_ref, gba_ref, gbb_ref, sma_ref, smb_ref, gsum_ref,
                dpre_ref, keep_ref, send_ref, vown_ref, dgrs, gb, gg, gsh):
    d, w = n_ref.shape[2], wa_ref.shape[1]
    width = 2 * w
    wa_ref, wb_ref = wa_ref.at[:d], wb_ref.at[:d]
    for r in (gb, gg, gsh):
        r[...] = jnp.zeros_like(r)
    gain = v_ref[2:3, :]

    def products(b):
        dgr = dgrs.at[b % SLOTS]
        dgr[:, :w] = dot(st_ref[b], dsa_ref[b])
        dgr[:, w:] = dot(st_ref[b], dsb_ref[b])

    def arithmetic(b):
        dgr = dgrs.at[b % SLOTS]
        for r in range(0, WIN, CH):
            dr = dgr[r : r + CH, :]
            hat = rows_hat_ref[b, r : r + CH, :].astype(F32)
            gg[...] += fold8(dr * hat)
            gsh[...] += fold8(dr)
            dg = dr * gain
            m1 = jnp.sum(dg, -1, keepdims=True) * (1.0 / width)
            m2 = jnp.sum(dg * hat, -1, keepdims=True) * (1.0 / width)
            dpg = (dg - m1 - hat * m2) * inv_ref[b, r : r + CH, 0:1] * slope_ref[b, r : r + CH, :].astype(F32)
            dpre_ref[b, r : r + CH, :] = dpg.astype(BF)
            gb[...] += fold8(dpg)

    pipelined(n_ref.shape[0], products, arithmetic)

    gw = dot_tn(n_ref[...].reshape(-1, d), dpre_ref[...].reshape(-1, width))
    keep_ref[...] = gw[:, :w].astype(BF)
    sums = gb[...]
    send_ref[:d, :] = gw[:, w:].astype(BF)
    t = sma_ref[0:1, :] + smb_ref[0:1, :] + row_sums(gw[:, :w], wa_ref) + row_sums(gw[:, w:], wb_ref)
    s = sma_ref[1:2, :] + smb_ref[1:2, :] + back_sum(sums[:, :w], wa_ref) + back_sum(sums[:, w:], wb_ref)
    one = lambda v: jnp.sum(v, 0, keepdims=True)
    fours = [jnp.concatenate([one(gba_ref[...]), one(gbb_ref[...])], 1), one(gb[...]), one(gg[...]), one(gsh[...])]
    wide = lambda v: jnp.concatenate([v, jnp.zeros((1, w - d), F32)], 1)
    full = jnp.concatenate([wide(t), wide(s), wide(gsum_ref[...]), jnp.zeros((1, w), F32)], 0)
    fours = jnp.concatenate(fours, 0)
    hi, lo = split(jnp.concatenate([fours[:, w:], full], 0))
    send_ref[d:, :] = jnp.concatenate([hi, lo], 0)
    fhi, flo = split(full)
    vown_ref[...] = jnp.concatenate([fours[:, :w], fhi.astype(F32) + flo.astype(F32)], 0)


def back_call(info, normed, ds, hat, slope, inv, st, vecs, wg, gbv, small, gsum, after):
    n, _, d = normed.shape
    width = vecs.shape[1]
    w = width // 2
    return call(
        back_kernel, info, (*in_vmem(normed, *ds, hat, slope, inv, st), vecs, *wg, *gbv, *small, gsum),
        [VM] * 7 + [const(8, width), whole(wg[0]), whole(wg[1]), const(8, w), const(8, w), const(8, d), const(8, d), const(1, d)],
        [fast((n, WIN, width), BF), shape((d, w), BF), shape((d + 16, w), BF), shape((8, w), F32)],
        [VM, const(d, w), const(d + 16, w), const(8, w)],
        [pltpu.VMEM((SLOTS, WIN, width), F32)] + [pltpu.VMEM((8, width), F32)] * 3, name="gate_backward", after=after, us=1, vmem=BACK_MB,
    )


def joined(v, carry):
    b = pl.program_id(0)

    @pl.when(b == 0)
    def _():
        carry[...] = jnp.zeros_like(carry)

    v = pltpu.roll(v, shift_of(b), 0)
    v = jnp.concatenate([v[:16] + carry[...], v[16:]], 0)
    carry[...] = v[STEP:]
    return v


def result_kernel(info, x_ref, pa_ref, pb_ref, woa_ref, wob_ref, bias_ref, res_ref, token, carry):
    b = pl.program_id(0)
    token[...] = jnp.zeros_like(token)
    finish = lambda x, br: (x.astype(F32) + br + bias_ref[...][None]).astype(BF)

    @pl.when(b < pl.num_programs(0) - 1)
    def _():
        br = joined(dot_nt(pa_ref[b], woa_ref[...]) + dot_nt(pb_ref[b], wob_ref[...]), carry)
        res_ref[...] = finish(x_ref[:STEP, :], br[:STEP])

    @pl.when(b == pl.num_programs(0) - 1)
    def _():
        res_ref[:16, :] = finish(x_ref[STEP:, :], carry[...])


def value_part_kernel(info, va_ref, vb_ref, wva_ref, wvb_ref, out_ref, token):
    token[...] = jnp.zeros_like(token)
    for b in range(va_ref.shape[0]):
        out_ref[b] = dot_nt(va_ref[b], wva_ref[...]) + dot_nt(vb_ref[b], wvb_ref[...])


def grad_kernel(info, x_ref, g_ref, dv_ref, dg_ref, wga_ref, wgb_ref, gain_ref, ing_ref, token, carry):
    b = pl.program_id(0)
    token[...] = jnp.zeros_like(token)
    d, w = x_ref.shape[1], wga_ref.shape[1]

    def finish(x, g, dn):
        x = x.astype(F32)
        cen = x - jnp.mean(x, -1, keepdims=True)
        inv = lax.rsqrt(jnp.mean(cen * cen, -1, keepdims=True) + EPS)
        hat = cen * inv
        dx = dn * gain_ref[...][None]
        m1 = jnp.mean(dx, -1, keepdims=True)
        m2 = jnp.mean(dx * hat, -1, keepdims=True)
        return g.astype(F32) + inv * (dx - m1 - hat * m2)

    @pl.when(b < pl.num_programs(0) - 1)
    def _():
        dn = joined(dv_ref[b] + dot_nt(dg_ref[b, :, :w], wga_ref[:d, :]) + dot_nt(dg_ref[b, :, w:], wgb_ref[:d, :]), carry)
        ing_ref[...] = finish(x_ref[:STEP, :], g_ref[:STEP, :], dn[:STEP])

    @pl.when(b == pl.num_programs(0) - 1)
    def _():
        ing_ref[:16, :] = finish(x_ref[STEP:, :], g_ref[STEP:, :], carry[...])


def last_rows(n, d):
    return pl.BlockSpec((pl.Element(WIN), pl.Element(d)), lambda b, *_: (jnp.minimum(b, n - 1) * STEP, 0))


def row_block(d):
    return pl.BlockSpec((STEP, d), lambda b, *_: (b, 0))


def result_call(info, x, prod, vo, bias, after):
    n, _, w = prod[0].shape
    rows, d = x.shape
    return call(
        result_kernel, info, (*in_hbm(x), *in_vmem(*prod), *vo, *in_hbm(bias)),
        [last_rows(n, d), VM, VM, side(d, w, 1), side(d, w, 1), const(d)],
        [slow((rows, d), BF), shape((8, 128), F32)], [row_block(d), const(8, 128)], [pltpu.VMEM((16, d), F32)], grid=(n + 1,), name="result", after=after, us=1, vmem=10,
    )


def value_part_call(info, dpv, vo, d, after):
    n, _, w = dpv[0].shape
    return call(
        value_part_kernel, info, (*in_vmem(*dpv), *vo), [VM, VM, side(d, w, 0), side(d, w, 0)],
        [fast((n, WIN, d), F32), shape((8, 128), F32)], [VM, const(8, 128)], name="value_part", after=after, us=1, vmem=4,
    )


def grad_call(info, x, g, dv, dpg, wg, gain, after):
    n = dv.shape[0]
    rows, d = x.shape
    return call(
        grad_kernel, info, (*in_hbm(x, g), *in_vmem(dv, dpg), *wg, *in_hbm(gain)),
        [last_rows(n, d), last_rows(n, d), VM, VM, whole(wg[0]), whole(wg[1]), const(d)],
        [slow((rows, d), F32), shape((8, 128), F32)], [row_block(d), const(8, 128)], [pltpu.VMEM((16, d), F32)], grid=(n + 1,), name="input_grad", after=after, us=1, vmem=12,
    )


VROWS = 32


Z_ORDER = (0, 2, 1, 3)


def quarter_kernel(info, keep, recv, gsp, *outs):
    x, y, core = info[2], info[3], info[4]
    d = keep.shape[0] // 2
    c = keep.shape[1] // 2
    r = d // 8
    q = PAD // 4
    for a, out in enumerate(outs):
        for b in range(2):
            xr, yr = jnp.where(core == 0, b, a), jnp.where(core == 0, a, b)
            cols = pl.ds(pl.multiple_of(yr * c, c), c)
            for t in range(2):
                for at, z in enumerate(Z_ORDER):
                    row = pl.multiple_of(t * d + (2 * z + jnp.bitwise_xor(x, xr)) * r, r)
                    dst = (4 * t + at) * r
                    out[b, dst : dst + r, :] = (keep[pl.ds(row, r), cols].astype(F32) + recv[pl.ds(row, r), cols].astype(F32)).astype(out.dtype)
            row = pl.multiple_of((2 * jnp.bitwise_xor(x, xr) + jnp.bitwise_xor(y, yr)) * q, q)
            out[b, 8 * r :, :] = gsp[pl.ds(row, q), :].astype(BF).astype(out.dtype)


def pair_half_kernel(info, keep, recv, vown, *outs):
    x, core, low = info[2], info[4], lax.rem(info[1], 2)
    d = keep.shape[0]
    c = keep.shape[1] // 2
    r = d // 8
    got = recv[d:, :].astype(F32)
    v = vown[...] + (got[:8] + got[8:])
    tail = jnp.concatenate([v[4:7, :c], jnp.concatenate([v[4:7, c : c + 128], jnp.zeros((3, c - 128), F32)], 1), jnp.zeros((6, c), F32)], 0)
    vecs = [both(jnp.concatenate([v[0:4, k * c : (k + 1) * c], tail], 0)) for k in range(2)]
    for out, bit in zip(outs, (low, 1 - low)):
        for a in range(2):
            for b in range(2):
                xr, yr = jnp.where(core == 0, b, a), jnp.where(core == 0, a, b)
                cols = pl.ds(pl.multiple_of(yr * c, c), c)
                for high in range(2):
                    row = pl.multiple_of((2 * (2 * high + bit) + jnp.bitwise_xor(x, xr)) * r, r)
                    dst = ((2 * a + b) * 2 + high) * r
                    out[dst : dst + r, :] = (keep[pl.ds(row, r), cols].astype(F32) + recv[pl.ds(row, r), cols].astype(F32)).astype(out.dtype)
        for k in range(2):
            at = 8 * r + k * VROWS
            out[at : at + VROWS, :] = vecs[k].astype(out.dtype)


def first_half_kernel(info, part, recv, keep, send):
    m = keep.shape[1] - VROWS
    base = 4 * m
    vec = [rounded(part[base + k * VROWS : base + (k + 1) * VROWS, :] + recv[base + k * VROWS : base + (k + 1) * VROWS, :].astype(F32)) for k in range(2)]
    for a, out in enumerate((keep, send)):
        for b in range(2):
            rows = slice((2 * a + b) * m, (2 * a + b + 1) * m)
            out[b, :m, :] = (part[rows, :] + recv[rows, :].astype(F32)).astype(out.dtype)
            yr = jnp.where(info[4] == 0, a, b)
            out[b, m:, :] = jnp.where(yr == 0, vec[0].astype(F32), vec[1].astype(F32)).astype(out.dtype)


def both(v):
    hi, lo = split(v)
    return jnp.concatenate([hi, lo], 0)


def rounded(v):
    return both(v[:16] + v[16:]) if v.shape[0] == VROWS else v.astype(BF)


def plane_kernel(extra, info, parts, recv, keep, send):
    m = keep.shape[0] - extra
    for b, out in enumerate((keep, send)):
        out[:m, :] = (parts[b, :m, :] + recv[b, :m, :].astype(F32)).astype(out.dtype)
        out[m:, :] = rounded(parts[b, m:, :] + recv[b, m:, :].astype(F32)).astype(out.dtype)


def line_kernel(tensors, chunks, extra, info, part, recv, keep, send):
    m = part.shape[0] - extra
    r = m // (tensors * chunks)
    h = chunks // 2
    bit = lax.rem(info[1], 2) if h == 2 else lax.div(info[1], 2)
    for out, which in ((keep, bit), (send, 1 - bit)):
        for t in range(tensors):
            rows = pl.ds(pl.multiple_of((t * chunks + which * h) * r, r), h * r)
            out[t * h * r : (t + 1) * h * r, :] = (part[rows, :] + recv[rows, :].astype(F32)).astype(out.dtype)
        out[tensors * h * r :, :] = rounded(part[m:, :] + recv[m:, :].astype(F32)).astype(out.dtype)


def finish_vo_kernel(info, part, recv, gwv, gwo, sp):
    r = gwv.shape[0]
    v = part[...] + recv[...].astype(F32)
    gwv[...] = v[:r]
    gwo[...] = v[r : 2 * r]
    sp[...] = v[2 * r :].astype(BF)


def finish_g_kernel(info, part, recv, gain, shift, gwg, gbv, gbg, ggain, gshift, rows):
    r = gwg.shape[0]
    v = part[...] + recv[...].astype(F32)
    gwg[...] = v[:r]
    v = v[r : r + 16] + v[r + 16 :]
    for k, out in enumerate((gbv, gbg, ggain, gshift)):
        out[...] = v[k]
    full = jnp.concatenate([v[4:7, :], v[7:10, :128]], 1)
    gin = (full[0:1, :] - shift[...][None] * full[1:2, :]) / gain[...][None]
    rows[...] = jnp.concatenate([gin, full[1:], jnp.zeros((5, full.shape[1]), F32)], 0)


def pair_kernel(info, a, b, out):
    out[...] = (a[...].astype(F32) + b[...].astype(F32)).astype(BF)


def spatial_kernel(info, a, rx, ry, rxy, mine, other, out, bias, gin, sin, gout, full):
    q = a.shape[0]
    for ref, k in ((a, 0), (ry, 1), (rx, 2), (rxy, 3)):
        full[pl.ds(pl.multiple_of(jnp.bitwise_xor(2 * info[2] + info[3], k) * q, q), q), :] = ref[...].astype(F32)
    p = out.shape[0]
    out[...] = full[:p, :p]
    bias[...] = full[:, 256:].T[WIN - 256, :p]
    v = jnp.where(info[4] == 0, mine[...], other[...])
    gin[...] = v[0]
    sin[...] = v[1]
    gout[...] = v[2]


def permute(x, to):
    n_dp, n_mp = lax.axis_size("dp"), lax.axis_size("mp")
    pairs = []
    for i in range(n_dp * n_mp):
        dp, mp = to(i // n_mp, i % n_mp)
        pairs.append((i, dp * n_mp + mp))
    return lax.ppermute(x, AXES, pairs)


def core_swap(x):
    return permute(x, lambda dp, mp: (dp, mp ^ 1))


def plane_swaps(a, b, c):
    return (
        permute(a, lambda dp, mp: (dp ^ 1, mp)),
        permute(b, lambda dp, mp: (dp, mp ^ 2)),
        permute(c, lambda dp, mp: (dp ^ 1, mp ^ 2)),
    )


def first_swap(x):
    return permute(x, lambda dp, mp: (dp, mp ^ 2) if mp % 2 == 0 else (dp ^ 1, mp))


def second_swap(x):
    return permute(x, lambda dp, mp: (dp ^ 1, mp) if mp % 2 == 0 else (dp, mp ^ 2))


def z_swap(x, bit):
    return permute(x, lambda dp, mp: (dp ^ (2 * bit), mp))


def line_swaps(arrays):
    n_dp = lax.axis_size("dp")
    return [permute(a, lambda dp, mp, k=k: ((dp + 2 * (k + 1)) % n_dp, mp)) for k, a in enumerate(arrays)]


def gather_dp(copies):
    t = lax.all_to_all(copies, "dp", 0, 0, tiled=True)
    return t.reshape(-1, t.shape[2])


def after(x, y):
    return lax.optimization_barrier((x, y))


def y_swap(x):
    return permute(x, lambda dp, mp: (dp, mp ^ 2))


def scatter_any(keep, recv):
    n = lax.axis_size("dp")
    c = keep.shape[1] // 2
    a = keep.astype(F32) + recv.astype(F32)
    s = a[:, :c] + permute(a[:, c:].astype(BF), lambda dp, mp: (dp, mp ^ 2)).astype(F32)
    return lax.all_to_all(s.astype(BF).reshape(n, -1, c), "dp", 0, 0, tiled=True).astype(F32).sum(0)


def body(inputs, counts, input_norm_gain, shift_in, w_value, w_gate, bias_value, bias_gate, gate_gain, gate_shift, spatial, spatial_bias, w_out, out_bias, cotangent):
    n_dp, n_mp = lax.axis_size("dp"), lax.axis_size("mp")
    me, dp = lax.axis_index("mp"), lax.axis_index("dp")
    r, c = w_value.shape
    d = inputs.shape[1]
    p = spatial.shape[0]
    n = counts.shape[0] // n_mp
    quick = n_dp == 8 and r % 16 == 0
    head = jnp.stack([me, dp // 2, dp % 2, me // 2, me % 2, me * n, 0, 0]).astype(jnp.int32)
    info = jnp.concatenate([head, counts])

    args = in_hbm(w_gate, w_value, w_out.T, bias_value, bias_gate, gate_gain, gate_shift)
    pg, vo1, vec = simple_call(cast_kernel, info, args, [shape((r, c), BF), shape((r, 2 * c), BF), shape((16, c), BF)], "casts")
    if quick:
        zg, zvo = line_swaps([pg] * 3), line_swaps([vo1] * 3)
        zg = stack_call(info, (pg, *zg, vec), (), "line_gate")
        pieces = (zg, *plane_swaps(zg, zg, zg))
    else:
        copies = lambda a: gather_dp(jnp.broadcast_to(a[None], (n_dp,) + a.shape))
        g0 = jnp.concatenate([copies(pg), vec])
        zg = wga = jnp.concatenate([g0, y_swap(g0)], 1)
        vo0 = copies(vo1)
        vo2 = y_swap(vo0)
        zvo = ()
        voa = jnp.concatenate([vo0[:, :c], vo2[:, :c], vo0[:, c:], vo2[:, c:]], 1)
    normed, g_win, gsum = norm_call(info, inputs, cotangent, input_norm_gain, shift_in, n, (zg,))
    s, st, sb, token = windows_call(info, spatial, spatial_bias, n, (gsum, *zvo))
    if quick:
        wga = assemble_call(info, pieces, 1, 16, (token,), "assemble_gate")
        zvo = stack_call(info, (vo1, *zvo), (wga,), "line_value_out")
        pieces = (zvo, *plane_swaps(zvo, zvo, zvo))
    wgb = core_swap(wga)
    rows, hat, slope, inv, shifted, vec = gate_call(info, (wga, wgb), normed, s, sb, (zvo,) if quick else ())
    if quick:
        *rest, vec = lax.optimization_barrier((*pieces[1:], vec))
        pieces = (pieces[0], *rest)
        swapped = tuple(core_swap(a) for a in pieces)
        voa = assemble_call(info, pieces, 2, 0, (vec,), "assemble_own")
        vob = assemble_call(info, swapped, 2, 0, (voa,), "assemble_other")
    else:
        vob = core_swap(voa)
    zero = jnp.zeros((PAD, PAD), F32)
    prod_b, ds_b, dpv_b, gw_b, gb_b, gsp, small_b = value_call(info, 1, False, vob, normed, g_win, vec, shifted, rows, zero)
    recv_vo = core_swap(gw_b)
    prod_a, ds_a, dpv_a, gw_a, gb_a, gsp, small_a = value_call(info, 0, True, voa, normed, g_win, vec, shifted, rows, gsp)
    q = PAD // 4
    def plane(parts, recv, extra, name, after):
        s = parts.shape[1:]
        return simple_call(lambda *a: plane_kernel(extra, *a), info, (parts, recv), [shape(s, F32), shape(s, BF)], name, after=after)

    def line(part, recv, tensors, chunks, extra, name, after):
        s = ((part.shape[0] - extra) // 2 + extra, c)
        return simple_call(lambda *a: line_kernel(tensors, chunks, extra, *a), info, (part, recv), [shape(s, F32), shape(s, BF)], name, after=after)

    if quick:
        kvo, snd = simple_call(quarter_kernel, info, (gw_a, recv_vo, gsp), [shape((2, 8 * r + q, c), t) for t in (F32, BF)], "quarters_vo")
        got_vo = first_swap(snd)
    dpg, keep_g, send_g, vown = back_call(info, normed, (ds_a, ds_b), hat, slope, inv, st, vec, (wga, wgb), (gb_a, gb_b), (small_a, small_b), gsum, (snd,) if quick else ())
    recv_g = core_swap(send_g)
    dnv, token = value_part_call(info, (dpv_a, dpv_b), (voa, vob), d, (vown,))
    if quick:
        rows_g = 8 * r + 2 * VROWS
        kg, snd = simple_call(pair_half_kernel, info, (keep_g, recv_g, vown), [shape((rows_g, c), t) for t in (F32, BF)], "halves_g", after=(token,))
        got_g = z_swap(snd, 1)
        kvo, snd = plane(kvo, got_vo, q, "plane_vo", (snd,))
        got_vo = second_swap(snd)
    ing, token = grad_call(info, inputs, cotangent, dnv, dpg, (wga, wgb), input_norm_gain, (snd if quick else token,))
    if quick:
        rows_g = 2 * r + VROWS
        kg, snd = simple_call(first_half_kernel, info, (kg, got_g), [shape((2, rows_g, c), t) for t in (F32, BF)], "quarters_g", after=(token,))
        got_g = first_swap(snd)
        kvo, snd = line(kvo, got_vo, 2, 4, q, "line_vo", (snd,))
        got_vo = z_swap(snd, 1)
    res, token = result_call(info, inputs, (prod_a, prod_b), (voa, vob), out_bias, (snd if quick else token,))
    if quick:
        kg, snd = plane(kg, got_g, VROWS, "plane_g", (token,))
        got_g = second_swap(snd)
        kvo, snd = line(kvo, got_vo, 2, 2, q, "pair_vo", (snd,))
        got_vo = z_swap(snd, 2)
        kg, snd = line(kg, got_g, 1, 2, VROWS, "pair_g", (snd,))
        got_g = z_swap(snd, 2)
        one = shape((c,), F32)
        gwg, gbv, gbg, ggain, gshift, full = simple_call(
            finish_g_kernel, info, (kg, got_g, *in_hbm(input_norm_gain, shift_in)),
            [shape((r, c), F32)] + [one] * 4 + [shape((8, d), F32)], "finish_g")
        gwv, gwo, sp = simple_call(finish_vo_kernel, info, (kvo, got_vo), [shape((r, c), F32), shape((r, c), F32), shape((q, c), BF)], "finish_vo", after=(snd,))
        (sp,) = simple_call(pair_kernel, info, (sp, core_swap(sp)), [shape((q, c), BF)], "spatial_pair")
        sps = plane_swaps(sp, sp, sp)
        gspat, gsb, gin, sin, gob = simple_call(spatial_kernel, info, (sp, *sps, full, core_swap(full)), [shape((p, p), F32), shape((p,), F32)] + [shape((d,), F32)] * 3, "spatial_sum", [pltpu.VMEM((PAD, PAD), F32)])
    else:
        gwv = scatter_any(gw_a[:d], recv_vo[:d])
        gwo = scatter_any(gw_a[d:], recv_vo[d:])
        gwg = scatter_any(keep_g, recv_g[:d])
        gsp = lax.psum(gsp, AXES)
        gspat, gsb = gsp[:p, :p], gsp[:p, WIN]
        other = send_g[d:].astype(F32)
        other = other[:8] + other[8:]
        back = jnp.argsort(jnp.bitwise_xor(jnp.array(ORDER, jnp.int32), me))
        four = jnp.concatenate([vown[:4], other[:4]], 1).reshape(4, n_mp, c)
        four = lax.psum(jnp.take(four, back, axis=1), AXES)
        gbv, gbg, ggain, gshift = lax.dynamic_index_in_dim(four, me, 1, keepdims=False)
        t, sin, gob = lax.psum(vown[4:7, :d], AXES)
        gin = (t - shift_in * sin) / input_norm_gain
    return (res, ing, gin, sin, gwv, gwg, gbv, gbg, ggain, gshift, gspat, gsb, gwo.T, gob)


def solution(mesh):
    row, wi, mp, al = P(("dp", "mp"), None), P("dp", "mp"), P("mp"), P()
    return jax.shard_map(
        body, mesh=mesh,
        in_specs=(row, P("dp"), al, al, wi, wi, mp, mp, mp, mp, al, al, P("mp", "dp"), al, row),
        out_specs=(row, row, al, al, wi, wi, mp, mp, mp, mp, al, al, P("mp", "dp"), al),
        check_vma=False,
    )
```

```python
import jax
import jax.numpy as jnp
from jax import lax
from jax.experimental import pallas as pl
from jax.experimental.pallas import tpu as pltpu
from jax.sharding import PartitionSpec as P

EPS = 1e-5
BF = jnp.bfloat16
F32 = jnp.float32
AXES = ("dp", "mp")
WIN = 336
STEP = 320
EXT = 352
CH = 16
PAD = 384
ORDER = (0, 2, 1, 3)
GELU_C = (7.97869712e-01, 3.63922863e-02, -8.78266205e-05, -3.66934307e-05, 1.42500480e-06)
LOG2E_HALF = -0.7213475204444817
INV_SQRT_2PI = 0.3989422804014327
MB = 2**20


def dot(a, b):
    return jnp.dot(a, b, preferred_element_type=F32)


def dot_tn(a, b):
    return lax.dot_general(a, b, (((0,), (0,)), ((), ())), preferred_element_type=F32)


def dot_nt(a, b):
    return lax.dot_general(a, b, (((1,), (1,)), ((), ())), preferred_element_type=F32)


def gelu_both(x):
    u = x * x
    p = GELU_C[4]
    for c in GELU_C[3::-1]:
        p = p * u + c
    cdf = 0.5 + 0.5 * jnp.tanh(x * p)
    slope = cdf + (x * INV_SQRT_2PI) * jnp.exp2(u * LOG2E_HALF)
    return x * cdf, slope


def split(v):
    hi = v.astype(BF)
    return hi, (v - hi.astype(F32)).astype(BF)


def fold8(v):
    out = v[0:8]
    for r in range(8, v.shape[0], 8):
        out = out + v[r : r + 8]
    return out


def img(*s):
    return pl.BlockSpec((1,) + s, lambda b, *_: (b,) + (0,) * len(s))


def const(*s):
    return pl.BlockSpec(s, lambda b, *_: (0,) * len(s), pipeline_mode=pl.Buffered(1))


def half(rows, c, h):
    return pl.BlockSpec((1, rows, c), lambda b, *_: (b, 0, h))


def side(d, w, h):
    return pl.BlockSpec((d, w), lambda b, *_: (0, h), pipeline_mode=pl.Buffered(1))


def shape(s, t):
    return jax.ShapeDtypeStruct(s, t)


def fast(s, t):
    return pltpu.VMEM(s, t)


def slow(s, t):
    return pltpu.HBM(s, t)


def in_vmem(*arrays):
    return tuple(pltpu.with_memory_space_constraint(a, pltpu.VMEM) for a in arrays)


def in_hbm(*arrays):
    return tuple(pltpu.with_memory_space_constraint(a, pltpu.HBM) for a in arrays)


ANY = pl.BlockSpec(memory_space=pl.ANY)
VM = pl.BlockSpec(memory_space=pltpu.VMEM)


def call(kernel, info, args, in_specs, outs, out_specs, scratch=(), grid=(1,), name=None, after=(), vmem=8, us=1):
    n_in, n_after = len(args), len(after)

    def ordered(info_ref, *refs):
        kernel(info_ref, *refs[:n_in], *refs[n_in + n_after :])

    return pl.pallas_call(
        ordered,
        grid_spec=pltpu.PrefetchScalarGridSpec(
            num_scalar_prefetch=1, grid=grid, in_specs=list(in_specs) + [ANY] * n_after, out_specs=out_specs, scratch_shapes=list(scratch)
        ),
        out_shape=outs,
        compiler_params=pltpu.CompilerParams(vmem_limit_bytes=vmem * MB),
        cost_estimate=pl.CostEstimate(flops=int(us * 1.1e9), bytes_accessed=int(us * 3.3e6), transcendentals=0),
        name=name,
    )(info, *args, *after)


def whole(a):
    return const(*a.shape)


def simple_call(kernel, info, args, outs, name, scratch=(), after=(), us=1):
    return call(kernel, info, args, [whole(a) for a in args], outs, [whole(o) for o in outs], scratch, name=name, after=after, us=us)


SLOTS = 2
GATE_MB, VALUE_MB, BACK_MB = 11, 14, 16


def pipelined(n, products, arithmetic):
    for b in range(min(n, SLOTS - 1)):
        products(b)
    for b in range(n):
        if b + SLOTS - 1 < n:
            products(b + SLOTS - 1)
        arithmetic(b)


def cast_kernel(info, wg_ref, wv_ref, wo_ref, bv, bg, gg, gs, g_ref, vo_ref, vec_ref):
    c = wg_ref.shape[1]
    g_ref[...] = wg_ref[...].astype(BF)
    vo_ref[:, :c] = wv_ref[...].astype(BF)
    vo_ref[:, c:] = wo_ref[...].astype(BF)
    vec_ref[...] = both(jnp.concatenate([bv[...][None], bg[...][None], gg[...][None], gs[...][None], jnp.zeros((4, bv.shape[0]), F32)], 0))


def run_copies(pairs, sems):
    copies = [pltpu.make_async_copy(src, dst, sems.at[k]) for k, (src, dst) in enumerate(pairs)]
    for c in copies:
        c.start()
    for c in copies:
        c.wait()


def stack_kernel(info, *refs):
    *parts, out, sems = refs
    pairs, at = [], 0
    for ref in parts:
        n = ref.shape[0]
        pairs.append((ref, out.at[at : at + n]))
        at += n
    run_copies(pairs, sems)


def stack_call(info, parts, after, name):
    n = len(parts)
    rows, c = sum(a.shape[0] for a in parts), parts[0].shape[1]
    return call(stack_kernel, info, parts, [ANY] * n, [shape((rows, c), BF)], [ANY], [pltpu.SemaphoreType.DMA((n,))], name=name, after=after)[0]


def assemble_kernel(tensors, extra, info, *refs):
    *pieces, out, sems = refs
    where = ((0, 0), (1, 0), (0, 1), (1, 1))
    d, c = out.shape[0] - extra, out.shape[1] // (2 * tensors)
    n = 4
    r = d // (2 * n)
    pairs = []
    for ref, (xr, slot) in zip(pieces, where):
        for t in range(tensors):
            src, dst = slice(t * c, (t + 1) * c), slice((2 * t + slot) * c, (2 * t + slot + 1) * c)
            for k in range(n):
                row = pl.multiple_of((lax.rem(info[1] + (n - k), n) * 2 + jnp.bitwise_xor(info[2], xr)) * r, r)
                pairs.append((ref.at[k * r : (k + 1) * r, src], out.at[pl.ds(row, r), dst]))
            if xr == 0 and extra:
                pairs.append((ref.at[n * r :, src], out.at[d:, dst]))
    run_copies(pairs, sems)


def assemble_call(info, pieces, tensors, extra, after, name):
    rows, c = pieces[0].shape
    s = (2 * (rows - extra) + extra, 2 * c)
    return call(lambda *a: assemble_kernel(tensors, extra, *a), info, pieces, [ANY] * len(pieces), [shape(s, BF)],
                [const(*s)], [pltpu.SemaphoreType.DMA((18 * tensors,))], name=name, after=after)[0]


def shift_of(b):
    return 4 * b


def norm_kernel(info, x_ref, g_ref, gain_ref, shift_ref, n_ref, gw_ref, gsum_ref, rows):
    b = pl.program_id(0)

    @pl.when(b == 0)
    def _():
        gsum_ref[...] = jnp.zeros_like(gsum_ref)

    own = jnp.where(b == pl.num_programs(0) - 1, 1.0, 0.0)
    up = WIN - shift_of(b)
    for r in range(0, WIN, 48):
        x = x_ref[r : r + 48, :].astype(F32)
        cen = x - jnp.mean(x, -1, keepdims=True)
        inv = lax.rsqrt(jnp.mean(cen * cen, -1, keepdims=True) + EPS)
        rows[r : r + 48, :] = cen * inv * gain_ref[...][None] + shift_ref[...][None]
    n_ref[b] = pltpu.roll(rows[...], up, 0).astype(BF)
    g = g_ref[...].astype(F32)
    gw_ref[b] = pltpu.roll(g, up, 0).astype(BF)
    gsum_ref[...] += jnp.sum(fold8(g[:STEP]) + fold8(g[STEP:]) * own, 0, keepdims=True)


def window_rows(d):
    return pl.BlockSpec((pl.Element(WIN), pl.Element(d)), lambda b, *_: (b * STEP, 0))


def norm_call(info, x, g, gain, shift, n, after):
    d = x.shape[1]
    return call(norm_kernel, info, in_hbm(x, g, gain, shift), [window_rows(d), window_rows(d), const(d), const(d)],
                [fast((n, WIN, d), BF), fast((n, WIN, d), BF), shape((1, d), F32)], [VM, VM, const(1, d)],
                [pltpu.VMEM((WIN, d), F32)], grid=(n,), name="input_norm", after=after, us=3)


def windows_kernel(info, sp_ref, sb_ref, s_ref, st_ref, sbw_ref, token, pad, tpad, col):
    p = sp_ref.shape[0]
    b = pl.program_id(0)

    @pl.when(b == 0)
    def _():
        pad[...] = jnp.zeros_like(pad)
        pad[0:p, 0:p] = sp_ref[...]
        tpad[...] = pad[...].T
        col[...] = jnp.concatenate([jnp.broadcast_to(sb_ref[...][None], (128, p)), jnp.zeros((128, PAD - p), F32)], 1).T
        token[...] = jnp.zeros_like(token)

    ri = lax.broadcasted_iota(jnp.int32, (WIN, WIN), 0)
    ci = lax.broadcasted_iota(jnp.int32, (WIN, WIN), 1)
    end = count_of(info, b)
    live = (ri < end) & (ci < end)
    s_ref[b] = jnp.where(live, pad[:WIN, :WIN], 0.0).astype(BF)
    st_ref[b] = jnp.where(live, tpad[:WIN, :WIN], 0.0).astype(BF)
    sbw_ref[b] = jnp.where((ri < end)[:, :128], col[:WIN], 0.0)


def count_of(info, b):
    return info[8 + info[5] + b]


def windows_call(info, spatial, sbias, n, after):
    p = spatial.shape[0]
    win = fast((n, WIN, WIN), BF)
    return call(windows_kernel, info, in_hbm(spatial, sbias), [const(p, p), const(p)], [win, win, fast((n, WIN, 128), F32), shape((8, 128), F32)],
                [VM, VM, VM, const(8, 128)], [pltpu.VMEM((PAD, PAD), F32)] * 2 + [pltpu.VMEM((PAD, 128), F32)],
                grid=(n,), name="windows", after=after, us=2)


def gate_kernel(info, wa_ref, wb_ref, n_ref, s_ref, sb_ref, rows_ref, hat_ref, slope_ref, inv_ref, shifted_ref, v_ref, pres):
    w = wa_ref.shape[1]
    d = wa_ref.shape[0] - 16
    width = 2 * w
    for k, ref in enumerate((wa_ref, wb_ref)):
        v = ref[d:, :].astype(F32)
        v_ref[:, k * w : (k + 1) * w] = v[:8] + v[8:]
    bias, gain, shift = v_ref[1:2, :], v_ref[2:3, :], v_ref[3:4, :]

    def products(b):
        pre = pres.at[b % SLOTS]
        pre[:, :w] = dot(n_ref[b], wa_ref[:d, :])
        pre[:, w:] = dot(n_ref[b], wb_ref[:d, :])

    def arithmetic(b):
        pre = pres.at[b % SLOTS]
        for r in range(0, WIN, CH):
            act, slope = gelu_both(pre[r : r + CH, :] + bias)
            slope_ref[b, r : r + CH, :] = slope.astype(BF)
            cen = act - jnp.sum(act, -1, keepdims=True) * (1.0 / width)
            inv = lax.rsqrt(jnp.sum(cen * cen, -1, keepdims=True) * (1.0 / width) + EPS)
            hat = cen * inv
            inv_ref[b, r : r + CH, :] = jnp.broadcast_to(inv, (CH, 128))
            hat_ref[b, r : r + CH, :] = hat.astype(BF)
            rows_ref[b, r : r + CH, :] = (hat * gain + shift).astype(BF)
        rows_ref[b, WIN:, :] = jnp.ones((EXT - WIN, width), BF)
        sb = sb_ref[b]
        mixed = dot(s_ref[b], rows_ref[b, :WIN, :])
        for t in range(0, width, 128):
            shifted_ref[b, :, t : t + 128] = (mixed[:, t : t + 128] + sb).astype(BF)

    pipelined(n_ref.shape[0], products, arithmetic)


def gate_call(info, halves, normed, s, sb, after):
    n, _, d = normed.shape
    w = 2 * halves[0].shape[1]
    big = fast((n, WIN, w), BF)
    return call(
        gate_kernel, info, (*halves, *in_vmem(normed, s, sb)), [whole(a) for a in halves] + [VM] * 3,
        [fast((n, EXT, w), BF), big, big, fast((n, WIN, 128), F32), big, shape((8, w), F32)], [VM] * 5 + [const(8, w)],
        [pltpu.VMEM((SLOTS, WIN, w), F32)], name="gate_forward", after=after, us=1, vmem=GATE_MB,
    )


def value_kernel(h, info, wv_ref, wo_ref, n_ref, g_ref, v_ref, shifted_ref, rows_ref, gin_ref, prod_ref, dshift_ref, dpre_ref, gw_ref, gb_ref, gsp_ref, small_ref,
                 pres, dprods):
    d, w = wv_ref.shape
    cols = slice(h * w, (h + 1) * w)
    gb_ref[...] = jnp.zeros_like(gb_ref)
    gsp_ref[...] = gin_ref[...]

    def products(b):
        pre, dprod = pres.at[b % SLOTS], dprods.at[b % SLOTS]
        pre[...] = dot(n_ref[b], wv_ref[...])
        dprod[...] = dot(g_ref[b], wo_ref[...])

    def arithmetic(b):
        pre, dprod = pres.at[b % SLOTS], dprods.at[b % SLOTS]
        bias = v_ref[0:1, :]
        for r in range(0, WIN, CH):
            act, slope = gelu_both(pre[r : r + CH, :] + bias)
            sh = shifted_ref[b, r : r + CH, cols].astype(F32)
            dp = dprod[r : r + CH, :]
            prod = (act * sh).astype(BF)
            prod_ref[b, r : r + CH, :] = prod
            dshift_ref[b, r : r + CH, :] = (dp * act).astype(BF)
            dv = dp * sh * slope
            dvl = dv.astype(BF)
            dpre_ref[b, r : r + CH, :] = dvl
            gb_ref[...] += fold8(dv)
        part = dot_nt(dshift_ref[b], rows_ref[b, :, cols])
        end = count_of(info, b)
        ri = lax.broadcasted_iota(jnp.int32, (WIN, EXT), 0)
        ci = lax.broadcasted_iota(jnp.int32, (WIN, EXT), 1)
        live = (ri < end) & ((ci < end) | (ci >= WIN))
        gsp_ref[:WIN, :EXT] += jnp.where(live, part, 0.0)

    pipelined(n_ref.shape[0], products, arithmetic)
    gwv = dot_tn(n_ref[...].reshape(-1, d), dpre_ref[...].reshape(-1, w))
    gw_ref[:d, :] = gwv.astype(gw_ref.dtype)
    gw_ref[d:, :] = dot_tn(g_ref[...].reshape(-1, d), prod_ref[...].reshape(-1, w)).astype(gw_ref.dtype)
    small_ref[...] = jnp.concatenate([row_sums(gwv, wv_ref), back_sum(gb_ref[...], wv_ref), jnp.zeros((6, d), F32)], 0)


def row_sums(gw, w_ref):
    prod = gw * w_ref[...].astype(F32)
    t = prod[:, :128]
    for k in range(128, prod.shape[1], 128):
        t = t + prod[:, k : k + 128]
    return jnp.sum(t.T, 0, keepdims=True)


def back_sum(sums, w_ref):
    hi, lo = split(sums)
    return jnp.sum(dot_nt(hi, w_ref[...]) + dot_nt(lo, w_ref[...]), 0, keepdims=True)


def value_call(info, h, keep, vo, normed, g, vecs, shifted, rows, gsp, after=()):
    n, _, d = normed.shape
    w = vecs.shape[1] // 2
    big = fast((n, WIN, w), BF)
    return call(
        lambda *a: value_kernel(h, *a), info, (vo, vo, *in_vmem(normed, g), vecs, *in_vmem(shifted, rows), gsp),
        [side(d, w, 0), side(d, w, 1), VM, VM, pl.BlockSpec((8, w), lambda b, *_: (0, h)), VM, VM, const(PAD, PAD)],
        [big, big, big, shape((2 * d, w), BF), shape((8, w), F32), shape((PAD, PAD), F32), shape((8, d), F32)],
        [VM] * 3 + [const(2 * d, w), const(8, w), const(PAD, PAD), const(8, d)],
        [pltpu.VMEM((SLOTS, WIN, w), F32)] * 2, name="value_own" if keep else "value_other", after=after, us=1, vmem=VALUE_MB,
    )


def back_kernel(info, n_ref, dsa_ref, dsb_ref, rows_hat_ref, slope_ref, inv_ref, st_ref, v_ref, wa_ref, wb_ref, gba_ref, gbb_ref, sma_ref, smb_ref, gsum_ref,
                dpre_ref, keep_ref, send_ref, vown_ref, dgrs, gb, gg, gsh):
    d, w = n_ref.shape[2], wa_ref.shape[1]
    width = 2 * w
    wa_ref, wb_ref = wa_ref.at[:d], wb_ref.at[:d]
    for r in (gb, gg, gsh):
        r[...] = jnp.zeros_like(r)
    gain = v_ref[2:3, :]

    def products(b):
        dgr = dgrs.at[b % SLOTS]
        dgr[:, :w] = dot(st_ref[b], dsa_ref[b])
        dgr[:, w:] = dot(st_ref[b], dsb_ref[b])

    def arithmetic(b):
        dgr = dgrs.at[b % SLOTS]
        for r in range(0, WIN, CH):
            dr = dgr[r : r + CH, :]
            hat = rows_hat_ref[b, r : r + CH, :].astype(F32)
            gg[...] += fold8(dr * hat)
            gsh[...] += fold8(dr)
            dg = dr * gain
            m1 = jnp.sum(dg, -1, keepdims=True) * (1.0 / width)
            m2 = jnp.sum(dg * hat, -1, keepdims=True) * (1.0 / width)
            dpg = (dg - m1 - hat * m2) * inv_ref[b, r : r + CH, 0:1] * slope_ref[b, r : r + CH, :].astype(F32)
            dpre_ref[b, r : r + CH, :] = dpg.astype(BF)
            gb[...] += fold8(dpg)

    pipelined(n_ref.shape[0], products, arithmetic)

    gw = dot_tn(n_ref[...].reshape(-1, d), dpre_ref[...].reshape(-1, width))
    keep_ref[...] = gw[:, :w].astype(BF)
    sums = gb[...]
    send_ref[:d, :] = gw[:, w:].astype(BF)
    t = sma_ref[0:1, :] + smb_ref[0:1, :] + row_sums(gw[:, :w], wa_ref) + row_sums(gw[:, w:], wb_ref)
    s = sma_ref[1:2, :] + smb_ref[1:2, :] + back_sum(sums[:, :w], wa_ref) + back_sum(sums[:, w:], wb_ref)
    one = lambda v: jnp.sum(v, 0, keepdims=True)
    fours = [jnp.concatenate([one(gba_ref[...]), one(gbb_ref[...])], 1), one(gb[...]), one(gg[...]), one(gsh[...])]
    wide = lambda v: jnp.concatenate([v, jnp.zeros((1, w - d), F32)], 1)
    full = jnp.concatenate([wide(t), wide(s), wide(gsum_ref[...]), jnp.zeros((1, w), F32)], 0)
    fours = jnp.concatenate(fours, 0)
    hi, lo = split(jnp.concatenate([fours[:, w:], full], 0))
    send_ref[d:, :] = jnp.concatenate([hi, lo], 0)
    fhi, flo = split(full)
    vown_ref[...] = jnp.concatenate([fours[:, :w], fhi.astype(F32) + flo.astype(F32)], 0)


def back_call(info, normed, ds, hat, slope, inv, st, vecs, wg, gbv, small, gsum, after):
    n, _, d = normed.shape
    width = vecs.shape[1]
    w = width // 2
    return call(
        back_kernel, info, (*in_vmem(normed, *ds, hat, slope, inv, st), vecs, *wg, *gbv, *small, gsum),
        [VM] * 7 + [const(8, width), whole(wg[0]), whole(wg[1]), const(8, w), const(8, w), const(8, d), const(8, d), const(1, d)],
        [fast((n, WIN, width), BF), shape((d, w), BF), shape((d + 16, w), BF), shape((8, w), F32)],
        [VM, const(d, w), const(d + 16, w), const(8, w)],
        [pltpu.VMEM((SLOTS, WIN, width), F32)] + [pltpu.VMEM((8, width), F32)] * 3, name="gate_backward", after=after, us=1, vmem=BACK_MB,
    )


def rows_of(windows, finish, out_hbm, out, sems):
    n = windows.shape[0]
    copies = []
    carry = None
    for b in range(n):
        v = windows[b]
        if b:
            v = pltpu.roll(v, shift_of(b), 0)
            windows[b] = jnp.concatenate([v[:16] + carry, v[16:]], 0)
        carry = v[STEP:]
        first, count = b * STEP, STEP if b < n - 1 else WIN
        for r in range(0, count, 80):
            e = min(r + 80, count)
            out[first + r : first + e, :] = finish(slice(first + r, first + e), windows[b, r:e, :]).astype(out.dtype)
        copies.append(pltpu.make_async_copy(out.at[first : first + count], out_hbm.at[first : first + count], sems.at[b]))
        copies[-1].start()
    for c in copies:
        c.wait()


def result_kernel(info, x_hbm, pa_ref, pb_ref, woa_ref, wob_ref, bias_ref, res_hbm, token, xs, br, out, sems):
    n = pa_ref.shape[0]
    get = pltpu.make_async_copy(x_hbm, xs, sems.at[n])
    get.start()
    token[...] = jnp.zeros_like(token)
    for b in range(n):
        br[b] = dot_nt(pa_ref[b], woa_ref[...]) + dot_nt(pb_ref[b], wob_ref[...])
    get.wait()
    bias = bias_ref[...][None]
    rows_of(br, lambda at, v: xs[at, :].astype(F32) + v + bias, res_hbm, out, sems)


def value_part_kernel(info, va_ref, vb_ref, wva_ref, wvb_ref, out_ref, token):
    token[...] = jnp.zeros_like(token)
    for b in range(va_ref.shape[0]):
        out_ref[b] = dot_nt(va_ref[b], wva_ref[...]) + dot_nt(vb_ref[b], wvb_ref[...])


def grad_kernel(info, x_hbm, g_hbm, dv_ref, dg_ref, wga_ref, wgb_ref, gain_ref, ing_hbm, token, xs, gs, dn, out, sems):
    n, _, d = dv_ref.shape
    w = wga_ref.shape[1]
    gets = [pltpu.make_async_copy(src, dst, sems.at[n + k]) for k, (src, dst) in enumerate(((x_hbm, xs), (g_hbm, gs)))]
    for get in gets:
        get.start()
    token[...] = jnp.zeros_like(token)
    for b in range(n):
        dn[b] = dv_ref[b] + dot_nt(dg_ref[b, :, :w], wga_ref[:d, :]) + dot_nt(dg_ref[b, :, w:], wgb_ref[:d, :])
    for get in gets:
        get.wait()
    gain = gain_ref[...][None]

    def finish(at, v):
        x = xs[at, :].astype(F32)
        cen = x - jnp.mean(x, -1, keepdims=True)
        inv = lax.rsqrt(jnp.mean(cen * cen, -1, keepdims=True) + EPS)
        hat = cen * inv
        dx = v * gain
        m1 = jnp.mean(dx, -1, keepdims=True)
        m2 = jnp.mean(dx * hat, -1, keepdims=True)
        return gs[at, :].astype(F32) + inv * (dx - m1 - hat * m2)

    rows_of(dn, finish, ing_hbm, out, sems)


def result_call(info, x, prod, vo, bias, after):
    n, _, w = prod[0].shape
    rows, d = x.shape
    return call(
        result_kernel, info, (*in_hbm(x), *in_vmem(*prod), *vo, *in_hbm(bias)), [ANY, VM, VM, side(d, w, 1), side(d, w, 1), const(d)],
        [slow((rows, d), BF), shape((8, 128), F32)], [ANY, const(8, 128)],
        [pltpu.VMEM((rows, d), BF), pltpu.VMEM((n, WIN, d), F32), pltpu.VMEM((rows, d), BF), pltpu.SemaphoreType.DMA((n + 1,))],
        name="result", after=after, us=1, vmem=10,
    )


def value_part_call(info, dpv, vo, d, after):
    n, _, w = dpv[0].shape
    return call(
        value_part_kernel, info, (*in_vmem(*dpv), *vo), [VM, VM, side(d, w, 0), side(d, w, 0)],
        [fast((n, WIN, d), F32), shape((8, 128), F32)], [VM, const(8, 128)], name="value_part", after=after, us=1, vmem=4,
    )


def grad_call(info, x, g, dv, dpg, wg, gain, after):
    n = dv.shape[0]
    rows, d = x.shape
    return call(
        grad_kernel, info, (*in_hbm(x, g), *in_vmem(dv, dpg), *wg, *in_hbm(gain)), [ANY, ANY, VM, VM, whole(wg[0]), whole(wg[1]), const(d)],
        [slow((rows, d), F32), shape((8, 128), F32)], [ANY, const(8, 128)],
        [pltpu.VMEM((rows, d), BF)] * 2 + [pltpu.VMEM((n, WIN, d), F32), pltpu.VMEM((rows, d), F32), pltpu.SemaphoreType.DMA((n + 2,))],
        name="input_grad", after=after, us=1, vmem=13,
    )


VROWS = 32


Z_ORDER = (0, 2, 1, 3)


def quarter_kernel(info, keep, recv, gsp, *outs):
    x, y, core = info[2], info[3], info[4]
    d = keep.shape[0] // 2
    c = keep.shape[1] // 2
    r = d // 8
    q = PAD // 4
    for a, out in enumerate(outs):
        for b in range(2):
            xr, yr = jnp.where(core == 0, b, a), jnp.where(core == 0, a, b)
            cols = pl.ds(pl.multiple_of(yr * c, c), c)
            for t in range(2):
                for at, z in enumerate(Z_ORDER):
                    row = pl.multiple_of(t * d + (2 * z + jnp.bitwise_xor(x, xr)) * r, r)
                    dst = (4 * t + at) * r
                    out[b, dst : dst + r, :] = (keep[pl.ds(row, r), cols].astype(F32) + recv[pl.ds(row, r), cols].astype(F32)).astype(out.dtype)
            row = pl.multiple_of((2 * jnp.bitwise_xor(x, xr) + jnp.bitwise_xor(y, yr)) * q, q)
            out[b, 8 * r :, :] = gsp[pl.ds(row, q), :].astype(BF).astype(out.dtype)


def pair_half_kernel(info, keep, recv, vown, *outs):
    x, core, low = info[2], info[4], lax.rem(info[1], 2)
    d = keep.shape[0]
    c = keep.shape[1] // 2
    r = d // 8
    got = recv[d:, :].astype(F32)
    v = vown[...] + (got[:8] + got[8:])
    tail = jnp.concatenate([v[4:7, :c], jnp.concatenate([v[4:7, c : c + 128], jnp.zeros((3, c - 128), F32)], 1), jnp.zeros((6, c), F32)], 0)
    vecs = [both(jnp.concatenate([v[0:4, k * c : (k + 1) * c], tail], 0)) for k in range(2)]
    for out, bit in zip(outs, (low, 1 - low)):
        for a in range(2):
            for b in range(2):
                xr, yr = jnp.where(core == 0, b, a), jnp.where(core == 0, a, b)
                cols = pl.ds(pl.multiple_of(yr * c, c), c)
                for high in range(2):
                    row = pl.multiple_of((2 * (2 * high + bit) + jnp.bitwise_xor(x, xr)) * r, r)
                    dst = ((2 * a + b) * 2 + high) * r
                    out[dst : dst + r, :] = (keep[pl.ds(row, r), cols].astype(F32) + recv[pl.ds(row, r), cols].astype(F32)).astype(out.dtype)
        for k in range(2):
            at = 8 * r + k * VROWS
            out[at : at + VROWS, :] = vecs[k].astype(out.dtype)


def first_half_kernel(info, part, recv, keep, send):
    m = keep.shape[1] - VROWS
    base = 4 * m
    vec = [rounded(part[base + k * VROWS : base + (k + 1) * VROWS, :] + recv[base + k * VROWS : base + (k + 1) * VROWS, :].astype(F32)) for k in range(2)]
    for a, out in enumerate((keep, send)):
        for b in range(2):
            rows = slice((2 * a + b) * m, (2 * a + b + 1) * m)
            out[b, :m, :] = (part[rows, :] + recv[rows, :].astype(F32)).astype(out.dtype)
            yr = jnp.where(info[4] == 0, a, b)
            out[b, m:, :] = jnp.where(yr == 0, vec[0].astype(F32), vec[1].astype(F32)).astype(out.dtype)


def both(v):
    hi, lo = split(v)
    return jnp.concatenate([hi, lo], 0)


def rounded(v):
    return both(v[:16] + v[16:]) if v.shape[0] == VROWS else v.astype(BF)


def plane_kernel(extra, info, parts, recv, keep, send):
    m = keep.shape[0] - extra
    for b, out in enumerate((keep, send)):
        out[:m, :] = (parts[b, :m, :] + recv[b, :m, :].astype(F32)).astype(out.dtype)
        out[m:, :] = rounded(parts[b, m:, :] + recv[b, m:, :].astype(F32)).astype(out.dtype)


def line_kernel(tensors, chunks, extra, info, part, recv, keep, send):
    m = part.shape[0] - extra
    r = m // (tensors * chunks)
    h = chunks // 2
    bit = lax.rem(info[1], 2) if h == 2 else lax.div(info[1], 2)
    for out, which in ((keep, bit), (send, 1 - bit)):
        for t in range(tensors):
            rows = pl.ds(pl.multiple_of((t * chunks + which * h) * r, r), h * r)
            out[t * h * r : (t + 1) * h * r, :] = (part[rows, :] + recv[rows, :].astype(F32)).astype(out.dtype)
        out[tensors * h * r :, :] = rounded(part[m:, :] + recv[m:, :].astype(F32)).astype(out.dtype)


def finish_vo_kernel(info, part, recv, gwv, gwo, token):
    token[...] = jnp.zeros_like(token)
    r = gwv.shape[0]
    gwv[...] = part[:r, :] + recv[:r, :].astype(F32)
    gwo[...] = part[r : 2 * r, :] + recv[r : 2 * r, :].astype(F32)


def spatial_rows_kernel(info, part, recv, sp):
    m = part.shape[0] - sp.shape[0]
    sp[...] = (part[m:, :] + recv[m:, :].astype(F32)).astype(BF)


def finish_g_kernel(info, part, recv, gain, shift, gwg, gbv, gbg, ggain, gshift, rows):
    r = gwg.shape[0]
    v = part[...] + recv[...].astype(F32)
    gwg[...] = v[:r]
    v = v[r : r + 16] + v[r + 16 :]
    for k, out in enumerate((gbv, gbg, ggain, gshift)):
        out[...] = v[k]
    full = jnp.concatenate([v[4:7, :], v[7:10, :128]], 1)
    gin = (full[0:1, :] - shift[...][None] * full[1:2, :]) / gain[...][None]
    rows[...] = jnp.concatenate([gin, full[1:], jnp.zeros((5, full.shape[1]), F32)], 0)


def pair_kernel(info, a, b, out):
    out[...] = (a[...].astype(F32) + b[...].astype(F32)).astype(BF)


def spatial_kernel(info, a, rx, ry, rxy, mine, other, out, bias, gin, sin, gout, full):
    q = a.shape[0]
    for ref, k in ((a, 0), (ry, 1), (rx, 2), (rxy, 3)):
        full[pl.ds(pl.multiple_of(jnp.bitwise_xor(2 * info[2] + info[3], k) * q, q), q), :] = ref[...].astype(F32)
    p = out.shape[0]
    out[...] = full[:p, :p]
    bias[...] = full[:, 256:].T[WIN - 256, :p]
    v = jnp.where(info[4] == 0, mine[...], other[...])
    gin[...] = v[0]
    sin[...] = v[1]
    gout[...] = v[2]


def permute(x, to):
    n_dp, n_mp = lax.axis_size("dp"), lax.axis_size("mp")
    pairs = []
    for i in range(n_dp * n_mp):
        dp, mp = to(i // n_mp, i % n_mp)
        pairs.append((i, dp * n_mp + mp))
    return lax.ppermute(x, AXES, pairs)


def core_swap(x):
    return permute(x, lambda dp, mp: (dp, mp ^ 1))


def plane_swaps(a, b, c):
    return (
        permute(a, lambda dp, mp: (dp ^ 1, mp)),
        permute(b, lambda dp, mp: (dp, mp ^ 2)),
        permute(c, lambda dp, mp: (dp ^ 1, mp ^ 2)),
    )


def first_swap(x):
    return permute(x, lambda dp, mp: (dp, mp ^ 2) if mp % 2 == 0 else (dp ^ 1, mp))


def second_swap(x):
    return permute(x, lambda dp, mp: (dp ^ 1, mp) if mp % 2 == 0 else (dp, mp ^ 2))


def z_swap(x, bit):
    return permute(x, lambda dp, mp: (dp ^ (2 * bit), mp))


def line_swaps(arrays):
    n_dp = lax.axis_size("dp")
    return [permute(a, lambda dp, mp, k=k: ((dp + 2 * (k + 1)) % n_dp, mp)) for k, a in enumerate(arrays)]


def gather_dp(copies):
    t = lax.all_to_all(copies, "dp", 0, 0, tiled=True)
    return t.reshape(-1, t.shape[2])


def after(x, y):
    return lax.optimization_barrier((x, y))


def y_swap(x):
    return permute(x, lambda dp, mp: (dp, mp ^ 2))


def scatter_any(keep, recv):
    n = lax.axis_size("dp")
    c = keep.shape[1] // 2
    a = keep.astype(F32) + recv.astype(F32)
    s = a[:, :c] + permute(a[:, c:].astype(BF), lambda dp, mp: (dp, mp ^ 2)).astype(F32)
    return lax.all_to_all(s.astype(BF).reshape(n, -1, c), "dp", 0, 0, tiled=True).astype(F32).sum(0)


def body(inputs, counts, input_norm_gain, shift_in, w_value, w_gate, bias_value, bias_gate, gate_gain, gate_shift, spatial, spatial_bias, w_out, out_bias, cotangent):
    n_dp, n_mp = lax.axis_size("dp"), lax.axis_size("mp")
    me, dp = lax.axis_index("mp"), lax.axis_index("dp")
    r, c = w_value.shape
    d = inputs.shape[1]
    p = spatial.shape[0]
    n = counts.shape[0] // n_mp
    quick = n_dp == 8 and r % 16 == 0
    head = jnp.stack([me, dp // 2, dp % 2, me // 2, me % 2, me * n, 0, 0]).astype(jnp.int32)
    info = jnp.concatenate([head, counts])

    args = in_hbm(w_gate, w_value, w_out.T, bias_value, bias_gate, gate_gain, gate_shift)
    pg, vo1, vec = simple_call(cast_kernel, info, args, [shape((r, c), BF), shape((r, 2 * c), BF), shape((16, c), BF)], "casts")
    if quick:
        zg, zvo = line_swaps([pg] * 3), line_swaps([vo1] * 3)
        zg = stack_call(info, (pg, *zg, vec), (), "line_gate")
        pieces = (zg, *plane_swaps(zg, zg, zg))
    else:
        copies = lambda a: gather_dp(jnp.broadcast_to(a[None], (n_dp,) + a.shape))
        g0 = jnp.concatenate([copies(pg), vec])
        zg = wga = jnp.concatenate([g0, y_swap(g0)], 1)
        vo0 = copies(vo1)
        vo2 = y_swap(vo0)
        zvo = ()
        voa = jnp.concatenate([vo0[:, :c], vo2[:, :c], vo0[:, c:], vo2[:, c:]], 1)
    normed, g_win, gsum = norm_call(info, inputs, cotangent, input_norm_gain, shift_in, n, (zg,))
    if quick:
        wga = assemble_call(info, pieces, 1, 16, (gsum, *zvo), "assemble_gate")
        zvo = stack_call(info, (vo1, *zvo), (wga,), "line_value_out")
        pieces = (zvo, *plane_swaps(zvo, zvo, zvo))
    s, st, sb, token = windows_call(info, spatial, spatial_bias, n, (zvo,) if quick else (gsum,))
    wgb = core_swap(wga)
    rows, hat, slope, inv, shifted, vec = gate_call(info, (wga, wgb), normed, s, sb, (token,))
    if quick:
        *rest, vec = lax.optimization_barrier((*pieces[1:], vec))
        pieces = (pieces[0], *rest)
        swapped = tuple(core_swap(a) for a in pieces)
        voa = assemble_call(info, pieces, 2, 0, (vec,), "assemble_own")
        vob = assemble_call(info, swapped, 2, 0, (voa,), "assemble_other")
    else:
        vob = core_swap(voa)
    zero = jnp.zeros((PAD, PAD), F32)
    prod_b, ds_b, dpv_b, gw_b, gb_b, gsp, small_b = value_call(info, 1, False, vob, normed, g_win, vec, shifted, rows, zero)
    recv_vo = core_swap(gw_b)
    prod_a, ds_a, dpv_a, gw_a, gb_a, gsp, small_a = value_call(info, 0, True, voa, normed, g_win, vec, shifted, rows, gsp)
    q = PAD // 4
    def plane(parts, recv, extra, name, after):
        s = parts.shape[1:]
        return simple_call(lambda *a: plane_kernel(extra, *a), info, (parts, recv), [shape(s, F32), shape(s, BF)], name, after=after)

    def line(part, recv, tensors, chunks, extra, name, after):
        s = ((part.shape[0] - extra) // 2 + extra, c)
        return simple_call(lambda *a: line_kernel(tensors, chunks, extra, *a), info, (part, recv), [shape(s, F32), shape(s, BF)], name, after=after)

    if quick:
        kvo, snd = simple_call(quarter_kernel, info, (gw_a, recv_vo, gsp), [shape((2, 8 * r + q, c), t) for t in (F32, BF)], "quarters_vo")
        got_vo = first_swap(snd)
    dpg, keep_g, send_g, vown = back_call(info, normed, (ds_a, ds_b), hat, slope, inv, st, vec, (wga, wgb), (gb_a, gb_b), (small_a, small_b), gsum, (snd,) if quick else ())
    recv_g = core_swap(send_g)
    token = vown
    if quick:
        rows_g = 8 * r + 2 * VROWS
        kg, snd = simple_call(pair_half_kernel, info, (keep_g, recv_g, vown), [shape((rows_g, c), t) for t in (F32, BF)], "halves_g")
        got_g = z_swap(snd, 1)
        kvo, snd = plane(kvo, got_vo, q, "plane_vo", (snd,))
        got_vo = second_swap(snd)
        token = snd
    res, token = result_call(info, inputs, (prod_a, prod_b), (voa, vob), out_bias, (token,))
    if quick:
        kvo, snd = line(kvo, got_vo, 2, 4, q, "line_vo", (token,))
        got_vo = z_swap(snd, 1)
        rows_g = 2 * r + VROWS
        kg, snd = simple_call(first_half_kernel, info, (kg, got_g), [shape((2, rows_g, c), t) for t in (F32, BF)], "quarters_g", after=(snd,))
        got_g = first_swap(snd)
        token = snd
    dnv, token = value_part_call(info, (dpv_a, dpv_b), (voa, vob), d, (token,))
    if quick:
        kg, snd = plane(kg, got_g, VROWS, "plane_g", (token,))
        got_g = second_swap(snd)
        kvo, snd = line(kvo, got_vo, 2, 2, q, "pair_vo", (snd,))
        got_vo = z_swap(snd, 2)
        token = snd
    ing, token = grad_call(info, inputs, cotangent, dnv, dpg, (wga, wgb), input_norm_gain, (token,))
    if quick:
        kg, snd = line(kg, got_g, 1, 2, VROWS, "pair_g", (token,))
        got_g = z_swap(snd, 2)
        (sp,) = simple_call(spatial_rows_kernel, info, (kvo, got_vo), [shape((q, c), BF)], "spatial_rows", after=(snd,))
        gwv, gwo, token = simple_call(finish_vo_kernel, info, (kvo, got_vo), [shape((r, c), F32)] * 2 + [shape((8, 128), F32)], "finish_vo", after=(sp,))
        (sp,) = simple_call(pair_kernel, info, (sp, core_swap(sp)), [shape((q, c), BF)], "spatial_pair", after=(token,))
        sps = plane_swaps(sp, sp, sp)
        one = shape((c,), F32)
        gwg, gbv, gbg, ggain, gshift, full = simple_call(
            finish_g_kernel, info, (kg, got_g, *in_hbm(input_norm_gain, shift_in)),
            [shape((r, c), F32)] + [one] * 4 + [shape((8, d), F32)], "finish_g", after=(sp,))
        gspat, gsb, gin, sin, gob = simple_call(spatial_kernel, info, (sp, *sps, full, core_swap(full)), [shape((p, p), F32), shape((p,), F32)] + [shape((d,), F32)] * 3, "spatial_sum", [pltpu.VMEM((PAD, PAD), F32)])
    else:
        gwv = scatter_any(gw_a[:d], recv_vo[:d])
        gwo = scatter_any(gw_a[d:], recv_vo[d:])
        gwg = scatter_any(keep_g, recv_g[:d])
        gsp = lax.psum(gsp, AXES)
        gspat, gsb = gsp[:p, :p], gsp[:p, WIN]
        other = send_g[d:].astype(F32)
        other = other[:8] + other[8:]
        back = jnp.argsort(jnp.bitwise_xor(jnp.array(ORDER, jnp.int32), me))
        four = jnp.concatenate([vown[:4], other[:4]], 1).reshape(4, n_mp, c)
        four = lax.psum(jnp.take(four, back, axis=1), AXES)
        gbv, gbg, ggain, gshift = lax.dynamic_index_in_dim(four, me, 1, keepdims=False)
        t, sin, gob = lax.psum(vown[4:7, :d], AXES)
        gin = (t - shift_in * sin) / input_norm_gain
    return (res, ing, gin, sin, gwv, gwg, gbv, gbg, ggain, gshift, gspat, gsb, gwo.T, gob)


def solution(mesh):
    row, wi, mp, al = P(("dp", "mp"), None), P("dp", "mp"), P("mp"), P()
    return jax.shard_map(
        body, mesh=mesh,
        in_specs=(row, P("dp"), al, al, wi, wi, mp, mp, mp, mp, al, al, P("mp", "dp"), al, row),
        out_specs=(row, row, al, al, wi, wi, mp, mp, mp, mp, al, al, P("mp", "dp"), al),
        check_vma=False,
    )
```

```python
import jax
import jax.numpy as jnp
from jax import lax
from jax.experimental import pallas as pl
from jax.experimental.pallas import tpu as pltpu
from jax.sharding import PartitionSpec as P

EPS = 1e-5
BF = jnp.bfloat16
F32 = jnp.float32
AXES = ("dp", "mp")
WIN = 336
STEP = 320
EXT = 352
CH = 16
PAD = 384
ORDER = (0, 2, 1, 3)
GELU_C = (7.97869712e-01, 3.63922863e-02, -8.78266205e-05, -3.66934307e-05, 1.42500480e-06)
LOG2E_HALF = -0.7213475204444817
INV_SQRT_2PI = 0.3989422804014327
MB = 2**20


def dot(a, b):
    return jnp.dot(a, b, preferred_element_type=F32)


def dot_tn(a, b):
    return lax.dot_general(a, b, (((0,), (0,)), ((), ())), preferred_element_type=F32)


def dot_nt(a, b):
    return lax.dot_general(a, b, (((1,), (1,)), ((), ())), preferred_element_type=F32)


def gelu_both(x):
    u = x * x
    p = GELU_C[4]
    for c in GELU_C[3::-1]:
        p = p * u + c
    cdf = 0.5 + 0.5 * jnp.tanh(x * p)
    slope = cdf + (x * INV_SQRT_2PI) * jnp.exp2(u * LOG2E_HALF)
    return x * cdf, slope


def split(v):
    hi = v.astype(BF)
    return hi, (v - hi.astype(F32)).astype(BF)


def fold8(v):
    out = v[0:8]
    for r in range(8, v.shape[0], 8):
        out = out + v[r : r + 8]
    return out


def img(*s):
    return pl.BlockSpec((1,) + s, lambda b, *_: (b,) + (0,) * len(s))


def const(*s):
    return pl.BlockSpec(s, lambda b, *_: (0,) * len(s), pipeline_mode=pl.Buffered(1))


def half(rows, c, h):
    return pl.BlockSpec((1, rows, c), lambda b, *_: (b, 0, h))


def side(d, w, h):
    return pl.BlockSpec((d, w), lambda b, *_: (0, h), pipeline_mode=pl.Buffered(1))


def shape(s, t):
    return jax.ShapeDtypeStruct(s, t)


def fast(s, t):
    return pltpu.VMEM(s, t)


def slow(s, t):
    return pltpu.HBM(s, t)


def in_vmem(*arrays):
    return tuple(pltpu.with_memory_space_constraint(a, pltpu.VMEM) for a in arrays)


def in_hbm(*arrays):
    return tuple(pltpu.with_memory_space_constraint(a, pltpu.HBM) for a in arrays)


ANY = pl.BlockSpec(memory_space=pl.ANY)
VM = pl.BlockSpec(memory_space=pltpu.VMEM)


def call(kernel, info, args, in_specs, outs, out_specs, scratch=(), grid=(1,), name=None, after=(), vmem=8, us=1):
    n_in, n_after = len(args), len(after)

    def ordered(info_ref, *refs):
        kernel(info_ref, *refs[:n_in], *refs[n_in + n_after :])

    return pl.pallas_call(
        ordered,
        grid_spec=pltpu.PrefetchScalarGridSpec(
            num_scalar_prefetch=1, grid=grid, in_specs=list(in_specs) + [ANY] * n_after, out_specs=out_specs, scratch_shapes=list(scratch)
        ),
        out_shape=outs,
        compiler_params=pltpu.CompilerParams(vmem_limit_bytes=vmem * MB),
        cost_estimate=pl.CostEstimate(flops=int(us * 1.1e9), bytes_accessed=int(us * 3.3e6), transcendentals=0),
        name=name,
    )(info, *args, *after)


def whole(a):
    return const(*a.shape)


def simple_call(kernel, info, args, outs, name, scratch=(), after=(), us=1):
    return call(kernel, info, args, [whole(a) for a in args], outs, [whole(o) for o in outs], scratch, name=name, after=after, us=us)


SLOTS = 2
GATE_MB, VALUE_MB, BACK_MB = 11, 14, 16


def pipelined(n, products, arithmetic):
    for b in range(min(n, SLOTS - 1)):
        products(b)
    for b in range(n):
        if b + SLOTS - 1 < n:
            products(b + SLOTS - 1)
        arithmetic(b)


def cast_kernel(info, wg_ref, wv_ref, wo_ref, bv, bg, gg, gs, g_ref, vo_ref, vec_ref):
    c = wg_ref.shape[1]
    g_ref[...] = wg_ref[...].astype(BF)
    vo_ref[:, :c] = wv_ref[...].astype(BF)
    vo_ref[:, c:] = wo_ref[...].astype(BF)
    vec_ref[...] = both(jnp.concatenate([bv[...][None], bg[...][None], gg[...][None], gs[...][None], jnp.zeros((4, bv.shape[0]), F32)], 0))


def run_copies(pairs, sems):
    copies = [pltpu.make_async_copy(src, dst, sems.at[k]) for k, (src, dst) in enumerate(pairs)]
    for c in copies:
        c.start()
    for c in copies:
        c.wait()


def stack_kernel(info, *refs):
    *parts, out, sems = refs
    pairs, at = [], 0
    for ref in parts:
        n = ref.shape[0]
        pairs.append((ref, out.at[at : at + n]))
        at += n
    run_copies(pairs, sems)


def stack_call(info, parts, after, name):
    n = len(parts)
    rows, c = sum(a.shape[0] for a in parts), parts[0].shape[1]
    return call(stack_kernel, info, parts, [ANY] * n, [shape((rows, c), BF)], [ANY], [pltpu.SemaphoreType.DMA((n,))], name=name, after=after)[0]


def assemble_kernel(tensors, extra, info, *refs):
    *pieces, out, sems = refs
    where = ((0, 0), (1, 0), (0, 1), (1, 1))
    d, c = out.shape[0] - extra, out.shape[1] // (2 * tensors)
    n = 4
    r = d // (2 * n)
    pairs = []
    for ref, (xr, slot) in zip(pieces, where):
        for t in range(tensors):
            src, dst = slice(t * c, (t + 1) * c), slice((2 * t + slot) * c, (2 * t + slot + 1) * c)
            for k in range(n):
                row = pl.multiple_of((lax.rem(info[1] + (n - k), n) * 2 + jnp.bitwise_xor(info[2], xr)) * r, r)
                pairs.append((ref.at[k * r : (k + 1) * r, src], out.at[pl.ds(row, r), dst]))
            if xr == 0 and extra:
                pairs.append((ref.at[n * r :, src], out.at[d:, dst]))
    run_copies(pairs, sems)


def assemble_call(info, pieces, tensors, extra, after, name):
    rows, c = pieces[0].shape
    s = (2 * (rows - extra) + extra, 2 * c)
    return call(lambda *a: assemble_kernel(tensors, extra, *a), info, pieces, [ANY] * len(pieces), [shape(s, BF)],
                [const(*s)], [pltpu.SemaphoreType.DMA((18 * tensors,))], name=name, after=after)[0]


def shift_of(b):
    return 4 * b


def norm_kernel(info, x_ref, g_ref, gain_ref, shift_ref, n_ref, gw_ref, gsum_ref, rows):
    b = pl.program_id(0)

    @pl.when(b == 0)
    def _():
        gsum_ref[...] = jnp.zeros_like(gsum_ref)

    own = jnp.where(b == pl.num_programs(0) - 1, 1.0, 0.0)
    up = WIN - shift_of(b)
    for r in range(0, WIN, 48):
        x = x_ref[r : r + 48, :].astype(F32)
        cen = x - jnp.mean(x, -1, keepdims=True)
        inv = lax.rsqrt(jnp.mean(cen * cen, -1, keepdims=True) + EPS)
        rows[r : r + 48, :] = cen * inv * gain_ref[...][None] + shift_ref[...][None]
    n_ref[b] = pltpu.roll(rows[...], up, 0).astype(BF)
    g = g_ref[...].astype(F32)
    gw_ref[b] = pltpu.roll(g, up, 0).astype(BF)
    gsum_ref[...] += jnp.sum(fold8(g[:STEP]) + fold8(g[STEP:]) * own, 0, keepdims=True)


def window_rows(d):
    return pl.BlockSpec((pl.Element(WIN), pl.Element(d)), lambda b, *_: (b * STEP, 0))


def norm_call(info, x, g, gain, shift, n, after):
    d = x.shape[1]
    return call(norm_kernel, info, in_hbm(x, g, gain, shift), [window_rows(d), window_rows(d), const(d), const(d)],
                [fast((n, WIN, d), BF), fast((n, WIN, d), BF), shape((1, d), F32)], [VM, VM, const(1, d)],
                [pltpu.VMEM((WIN, d), F32)], grid=(n,), name="input_norm", after=after, us=3)


def windows_kernel(info, sp_ref, sb_ref, s_ref, st_ref, sbw_ref, token, pad, tpad, col):
    p = sp_ref.shape[0]
    b = pl.program_id(0)

    @pl.when(b == 0)
    def _():
        pad[...] = jnp.zeros_like(pad)
        pad[0:p, 0:p] = sp_ref[...]
        tpad[...] = pad[...].T
        col[...] = jnp.concatenate([jnp.broadcast_to(sb_ref[...][None], (128, p)), jnp.zeros((128, PAD - p), F32)], 1).T
        token[...] = jnp.zeros_like(token)

    ri = lax.broadcasted_iota(jnp.int32, (WIN, WIN), 0)
    ci = lax.broadcasted_iota(jnp.int32, (WIN, WIN), 1)
    end = count_of(info, b)
    live = (ri < end) & (ci < end)
    s_ref[b] = jnp.where(live, pad[:WIN, :WIN], 0.0).astype(BF)
    st_ref[b] = jnp.where(live, tpad[:WIN, :WIN], 0.0).astype(BF)
    sbw_ref[b] = jnp.where((ri < end)[:, :128], col[:WIN], 0.0)


def count_of(info, b):
    return info[8 + info[5] + b]


def windows_call(info, spatial, sbias, n, after):
    p = spatial.shape[0]
    win = fast((n, WIN, WIN), BF)
    return call(windows_kernel, info, in_hbm(spatial, sbias), [const(p, p), const(p)], [win, win, fast((n, WIN, 128), F32), shape((8, 128), F32)],
                [VM, VM, VM, const(8, 128)], [pltpu.VMEM((PAD, PAD), F32)] * 2 + [pltpu.VMEM((PAD, 128), F32)],
                grid=(n,), name="windows", after=after, us=2)


def gate_kernel(info, wa_ref, wb_ref, n_ref, s_ref, sb_ref, rows_ref, hat_ref, slope_ref, inv_ref, shifted_ref, v_ref, pres):
    w = wa_ref.shape[1]
    d = wa_ref.shape[0] - 16
    width = 2 * w
    for k, ref in enumerate((wa_ref, wb_ref)):
        v = ref[d:, :].astype(F32)
        v_ref[:, k * w : (k + 1) * w] = v[:8] + v[8:]
    bias, gain, shift = v_ref[1:2, :], v_ref[2:3, :], v_ref[3:4, :]

    def products(b):
        pre = pres.at[b % SLOTS]
        pre[:, :w] = dot(n_ref[b], wa_ref[:d, :])
        pre[:, w:] = dot(n_ref[b], wb_ref[:d, :])

    def arithmetic(b):
        pre = pres.at[b % SLOTS]
        for r in range(0, WIN, CH):
            act, slope = gelu_both(pre[r : r + CH, :] + bias)
            slope_ref[b, r : r + CH, :] = slope.astype(BF)
            cen = act - jnp.sum(act, -1, keepdims=True) * (1.0 / width)
            inv = lax.rsqrt(jnp.sum(cen * cen, -1, keepdims=True) * (1.0 / width) + EPS)
            hat = cen * inv
            inv_ref[b, r : r + CH, :] = jnp.broadcast_to(inv, (CH, 128))
            hat_ref[b, r : r + CH, :] = hat.astype(BF)
            rows_ref[b, r : r + CH, :] = (hat * gain + shift).astype(BF)
        rows_ref[b, WIN:, :] = jnp.ones((EXT - WIN, width), BF)
        sb = sb_ref[b]
        mixed = dot(s_ref[b], rows_ref[b, :WIN, :])
        for t in range(0, width, 128):
            shifted_ref[b, :, t : t + 128] = (mixed[:, t : t + 128] + sb).astype(BF)

    pipelined(n_ref.shape[0], products, arithmetic)


def gate_call(info, halves, normed, s, sb, after):
    n, _, d = normed.shape
    w = 2 * halves[0].shape[1]
    big = fast((n, WIN, w), BF)
    return call(
        gate_kernel, info, (*halves, *in_vmem(normed, s, sb)), [whole(a) for a in halves] + [VM] * 3,
        [fast((n, EXT, w), BF), big, big, fast((n, WIN, 128), F32), big, shape((8, w), F32)], [VM] * 5 + [const(8, w)],
        [pltpu.VMEM((SLOTS, WIN, w), F32)], name="gate_forward", after=after, us=1, vmem=GATE_MB,
    )


def value_kernel(h, info, wv_ref, wo_ref, n_ref, g_ref, v_ref, shifted_ref, rows_ref, gin_ref, prod_ref, dshift_ref, dpre_ref, gw_ref, gb_ref, gsp_ref, small_ref,
                 pres, dprods):
    d, w = wv_ref.shape
    cols = slice(h * w, (h + 1) * w)
    gb_ref[...] = jnp.zeros_like(gb_ref)
    gsp_ref[...] = gin_ref[...]

    def products(b):
        pre, dprod = pres.at[b % SLOTS], dprods.at[b % SLOTS]
        pre[...] = dot(n_ref[b], wv_ref[...])
        dprod[...] = dot(g_ref[b], wo_ref[...])

    def arithmetic(b):
        pre, dprod = pres.at[b % SLOTS], dprods.at[b % SLOTS]
        bias = v_ref[0:1, :]
        for r in range(0, WIN, CH):
            act, slope = gelu_both(pre[r : r + CH, :] + bias)
            sh = shifted_ref[b, r : r + CH, cols].astype(F32)
            dp = dprod[r : r + CH, :]
            prod = (act * sh).astype(BF)
            prod_ref[b, r : r + CH, :] = prod
            dshift_ref[b, r : r + CH, :] = (dp * act).astype(BF)
            dv = dp * sh * slope
            dvl = dv.astype(BF)
            dpre_ref[b, r : r + CH, :] = dvl
            gb_ref[...] += fold8(dv)
        part = dot_nt(dshift_ref[b], rows_ref[b, :, cols])
        end = count_of(info, b)
        ri = lax.broadcasted_iota(jnp.int32, (WIN, EXT), 0)
        ci = lax.broadcasted_iota(jnp.int32, (WIN, EXT), 1)
        live = (ri < end) & ((ci < end) | (ci >= WIN))
        gsp_ref[:WIN, :EXT] += jnp.where(live, part, 0.0)

    pipelined(n_ref.shape[0], products, arithmetic)
    gwv = dot_tn(n_ref[...].reshape(-1, d), dpre_ref[...].reshape(-1, w))
    gw_ref[:d, :] = gwv.astype(gw_ref.dtype)
    gw_ref[d:, :] = dot_tn(g_ref[...].reshape(-1, d), prod_ref[...].reshape(-1, w)).astype(gw_ref.dtype)
    small_ref[...] = jnp.concatenate([row_sums(gwv, wv_ref), back_sum(gb_ref[...], wv_ref), jnp.zeros((6, d), F32)], 0)


def row_sums(gw, w_ref):
    prod = gw * w_ref[...].astype(F32)
    t = prod[:, :128]
    for k in range(128, prod.shape[1], 128):
        t = t + prod[:, k : k + 128]
    return jnp.sum(t.T, 0, keepdims=True)


def back_sum(sums, w_ref):
    hi, lo = split(sums)
    return jnp.sum(dot_nt(hi, w_ref[...]) + dot_nt(lo, w_ref[...]), 0, keepdims=True)


def value_call(info, h, keep, vo, normed, g, vecs, shifted, rows, gsp, after=()):
    n, _, d = normed.shape
    w = vecs.shape[1] // 2
    big = fast((n, WIN, w), BF)
    return call(
        lambda *a: value_kernel(h, *a), info, (vo, vo, *in_vmem(normed, g), vecs, *in_vmem(shifted, rows), gsp),
        [side(d, w, 0), side(d, w, 1), VM, VM, pl.BlockSpec((8, w), lambda b, *_: (0, h)), VM, VM, const(PAD, PAD)],
        [big, big, big, shape((2 * d, w), BF), shape((8, w), F32), shape((PAD, PAD), F32), shape((8, d), F32)],
        [VM] * 3 + [const(2 * d, w), const(8, w), const(PAD, PAD), const(8, d)],
        [pltpu.VMEM((SLOTS, WIN, w), F32)] * 2, name="value_own" if keep else "value_other", after=after, us=1, vmem=VALUE_MB,
    )


def back_kernel(info, n_ref, dsa_ref, dsb_ref, rows_hat_ref, slope_ref, inv_ref, st_ref, v_ref, wa_ref, wb_ref, gba_ref, gbb_ref, sma_ref, smb_ref, gsum_ref,
                dpre_ref, keep_ref, send_ref, vown_ref, dgrs, gb, gg, gsh):
    d, w = n_ref.shape[2], wa_ref.shape[1]
    width = 2 * w
    wa_ref, wb_ref = wa_ref.at[:d], wb_ref.at[:d]
    for r in (gb, gg, gsh):
        r[...] = jnp.zeros_like(r)
    gain = v_ref[2:3, :]

    def products(b):
        dgr = dgrs.at[b % SLOTS]
        dgr[:, :w] = dot(st_ref[b], dsa_ref[b])
        dgr[:, w:] = dot(st_ref[b], dsb_ref[b])

    def arithmetic(b):
        dgr = dgrs.at[b % SLOTS]
        for r in range(0, WIN, CH):
            dr = dgr[r : r + CH, :]
            hat = rows_hat_ref[b, r : r + CH, :].astype(F32)
            gg[...] += fold8(dr * hat)
            gsh[...] += fold8(dr)
            dg = dr * gain
            m1 = jnp.sum(dg, -1, keepdims=True) * (1.0 / width)
            m2 = jnp.sum(dg * hat, -1, keepdims=True) * (1.0 / width)
            dpg = (dg - m1 - hat * m2) * inv_ref[b, r : r + CH, 0:1] * slope_ref[b, r : r + CH, :].astype(F32)
            dpre_ref[b, r : r + CH, :] = dpg.astype(BF)
            gb[...] += fold8(dpg)

    pipelined(n_ref.shape[0], products, arithmetic)

    gw = dot_tn(n_ref[...].reshape(-1, d), dpre_ref[...].reshape(-1, width))
    keep_ref[...] = gw[:, :w].astype(BF)
    sums = gb[...]
    send_ref[:d, :] = gw[:, w:].astype(BF)
    t = sma_ref[0:1, :] + smb_ref[0:1, :] + row_sums(gw[:, :w], wa_ref) + row_sums(gw[:, w:], wb_ref)
    s = sma_ref[1:2, :] + smb_ref[1:2, :] + back_sum(sums[:, :w], wa_ref) + back_sum(sums[:, w:], wb_ref)
    one = lambda v: jnp.sum(v, 0, keepdims=True)
    fours = [jnp.concatenate([one(gba_ref[...]), one(gbb_ref[...])], 1), one(gb[...]), one(gg[...]), one(gsh[...])]
    wide = lambda v: jnp.concatenate([v, jnp.zeros((1, w - d), F32)], 1)
    full = jnp.concatenate([wide(t), wide(s), wide(gsum_ref[...]), jnp.zeros((1, w), F32)], 0)
    fours = jnp.concatenate(fours, 0)
    hi, lo = split(jnp.concatenate([fours[:, w:], full], 0))
    send_ref[d:, :] = jnp.concatenate([hi, lo], 0)
    fhi, flo = split(full)
    vown_ref[...] = jnp.concatenate([fours[:, :w], fhi.astype(F32) + flo.astype(F32)], 0)


def back_call(info, normed, ds, hat, slope, inv, st, vecs, wg, gbv, small, gsum, after):
    n, _, d = normed.shape
    width = vecs.shape[1]
    w = width // 2
    return call(
        back_kernel, info, (*in_vmem(normed, *ds, hat, slope, inv, st), vecs, *wg, *gbv, *small, gsum),
        [VM] * 7 + [const(8, width), whole(wg[0]), whole(wg[1]), const(8, w), const(8, w), const(8, d), const(8, d), const(1, d)],
        [fast((n, WIN, width), BF), shape((d, w), BF), shape((d + 16, w), BF), shape((8, w), F32)],
        [VM, const(d, w), const(d + 16, w), const(8, w)],
        [pltpu.VMEM((SLOTS, WIN, width), F32)] + [pltpu.VMEM((8, width), F32)] * 3, name="gate_backward", after=after, us=1, vmem=BACK_MB,
    )


def rows_of(windows, finish, out_hbm, out, sems):
    n = windows.shape[0]
    copies = []
    carry = None
    for b in range(n):
        v = windows[b]
        if b:
            v = pltpu.roll(v, shift_of(b), 0)
            windows[b] = jnp.concatenate([v[:16] + carry, v[16:]], 0)
        carry = v[STEP:]
        first, count = b * STEP, STEP if b < n - 1 else WIN
        for r in range(0, count, 80):
            e = min(r + 80, count)
            out[first + r : first + e, :] = finish(slice(first + r, first + e), windows[b, r:e, :]).astype(out.dtype)
        copies.append(pltpu.make_async_copy(out.at[first : first + count], out_hbm.at[first : first + count], sems.at[b]))
        copies[-1].start()
    for c in copies:
        c.wait()


def result_kernel(info, x_hbm, pa_ref, pb_ref, woa_ref, wob_ref, bias_ref, res_hbm, token, xs, br, out, sems):
    n = pa_ref.shape[0]
    get = pltpu.make_async_copy(x_hbm, xs, sems.at[n])
    get.start()
    token[...] = jnp.zeros_like(token)
    for b in range(n):
        br[b] = dot_nt(pa_ref[b], woa_ref[...]) + dot_nt(pb_ref[b], wob_ref[...])
    get.wait()
    bias = bias_ref[...][None]
    rows_of(br, lambda at, v: xs[at, :].astype(F32) + v + bias, res_hbm, out, sems)


def value_part_kernel(info, va_ref, vb_ref, wva_ref, wvb_ref, out_ref, token):
    token[...] = jnp.zeros_like(token)
    for b in range(va_ref.shape[0]):
        out_ref[b] = dot_nt(va_ref[b], wva_ref[...]) + dot_nt(vb_ref[b], wvb_ref[...])


def grad_kernel(info, x_hbm, g_hbm, dv_ref, dg_ref, wga_ref, wgb_ref, gain_ref, ing_hbm, token, xs, gs, dn, out, sems):
    n, _, d = dv_ref.shape
    w = wga_ref.shape[1]
    gets = [pltpu.make_async_copy(src, dst, sems.at[n + k]) for k, (src, dst) in enumerate(((x_hbm, xs), (g_hbm, gs)))]
    for get in gets:
        get.start()
    token[...] = jnp.zeros_like(token)
    for b in range(n):
        dn[b] = dv_ref[b] + dot_nt(dg_ref[b, :, :w], wga_ref[:d, :]) + dot_nt(dg_ref[b, :, w:], wgb_ref[:d, :])
    for get in gets:
        get.wait()
    gain = gain_ref[...][None]

    def finish(at, v):
        x = xs[at, :].astype(F32)
        cen = x - jnp.mean(x, -1, keepdims=True)
        inv = lax.rsqrt(jnp.mean(cen * cen, -1, keepdims=True) + EPS)
        hat = cen * inv
        dx = v * gain
        m1 = jnp.mean(dx, -1, keepdims=True)
        m2 = jnp.mean(dx * hat, -1, keepdims=True)
        return gs[at, :].astype(F32) + inv * (dx - m1 - hat * m2)

    rows_of(dn, finish, ing_hbm, out, sems)


def result_call(info, x, prod, vo, bias, after):
    n, _, w = prod[0].shape
    rows, d = x.shape
    return call(
        result_kernel, info, (*in_hbm(x), *in_vmem(*prod), *vo, *in_hbm(bias)), [ANY, VM, VM, side(d, w, 1), side(d, w, 1), const(d)],
        [slow((rows, d), BF), shape((8, 128), F32)], [ANY, const(8, 128)],
        [pltpu.VMEM((rows, d), BF), pltpu.VMEM((n, WIN, d), F32), pltpu.VMEM((rows, d), BF), pltpu.SemaphoreType.DMA((n + 1,))],
        name="result", after=after, us=1, vmem=10,
    )


def value_part_call(info, dpv, vo, d, after):
    n, _, w = dpv[0].shape
    return call(
        value_part_kernel, info, (*in_vmem(*dpv), *vo), [VM, VM, side(d, w, 0), side(d, w, 0)],
        [fast((n, WIN, d), F32), shape((8, 128), F32)], [VM, const(8, 128)], name="value_part", after=after, us=1, vmem=4,
    )


def grad_call(info, x, g, dv, dpg, wg, gain, after):
    n = dv.shape[0]
    rows, d = x.shape
    return call(
        grad_kernel, info, (*in_hbm(x, g), *in_vmem(dv, dpg), *wg, *in_hbm(gain)), [ANY, ANY, VM, VM, whole(wg[0]), whole(wg[1]), const(d)],
        [slow((rows, d), F32), shape((8, 128), F32)], [ANY, const(8, 128)],
        [pltpu.VMEM((rows, d), BF)] * 2 + [pltpu.VMEM((n, WIN, d), F32), pltpu.VMEM((rows, d), F32), pltpu.SemaphoreType.DMA((n + 2,))],
        name="input_grad", after=after, us=1, vmem=13,
    )


VROWS = 32


Z_ORDER = (0, 2, 1, 3)


def quarter_kernel(info, keep, recv, gsp, *outs):
    x, y, core = info[2], info[3], info[4]
    d = keep.shape[0] // 2
    c = keep.shape[1] // 2
    r = d // 8
    q = PAD // 4
    for a, out in enumerate(outs):
        for b in range(2):
            xr, yr = jnp.where(core == 0, b, a), jnp.where(core == 0, a, b)
            cols = pl.ds(pl.multiple_of(yr * c, c), c)
            for t in range(2):
                for at, z in enumerate(Z_ORDER):
                    row = pl.multiple_of(t * d + (2 * z + jnp.bitwise_xor(x, xr)) * r, r)
                    dst = (4 * t + at) * r
                    out[b, dst : dst + r, :] = (keep[pl.ds(row, r), cols].astype(F32) + recv[pl.ds(row, r), cols].astype(F32)).astype(out.dtype)
            row = pl.multiple_of((2 * jnp.bitwise_xor(x, xr) + jnp.bitwise_xor(y, yr)) * q, q)
            out[b, 8 * r :, :] = gsp[pl.ds(row, q), :].astype(BF).astype(out.dtype)


def pair_half_kernel(info, keep, recv, vown, *outs):
    x, core, low = info[2], info[4], lax.rem(info[1], 2)
    d = keep.shape[0]
    c = keep.shape[1] // 2
    r = d // 8
    got = recv[d:, :].astype(F32)
    v = vown[...] + (got[:8] + got[8:])
    tail = jnp.concatenate([v[4:7, :c], jnp.concatenate([v[4:7, c : c + 128], jnp.zeros((3, c - 128), F32)], 1), jnp.zeros((6, c), F32)], 0)
    vecs = [both(jnp.concatenate([v[0:4, k * c : (k + 1) * c], tail], 0)) for k in range(2)]
    for out, bit in zip(outs, (low, 1 - low)):
        for a in range(2):
            for b in range(2):
                xr, yr = jnp.where(core == 0, b, a), jnp.where(core == 0, a, b)
                cols = pl.ds(pl.multiple_of(yr * c, c), c)
                for high in range(2):
                    row = pl.multiple_of((2 * (2 * high + bit) + jnp.bitwise_xor(x, xr)) * r, r)
                    dst = ((2 * a + b) * 2 + high) * r
                    out[dst : dst + r, :] = (keep[pl.ds(row, r), cols].astype(F32) + recv[pl.ds(row, r), cols].astype(F32)).astype(out.dtype)
        for k in range(2):
            at = 8 * r + k * VROWS
            out[at : at + VROWS, :] = vecs[k].astype(out.dtype)


def first_half_kernel(info, part, recv, keep, send):
    m = keep.shape[1] - VROWS
    base = 4 * m
    vec = [rounded(part[base + k * VROWS : base + (k + 1) * VROWS, :] + recv[base + k * VROWS : base + (k + 1) * VROWS, :].astype(F32)) for k in range(2)]
    for a, out in enumerate((keep, send)):
        for b in range(2):
            rows = slice((2 * a + b) * m, (2 * a + b + 1) * m)
            out[b, :m, :] = (part[rows, :] + recv[rows, :].astype(F32)).astype(out.dtype)
            yr = jnp.where(info[4] == 0, a, b)
            out[b, m:, :] = jnp.where(yr == 0, vec[0].astype(F32), vec[1].astype(F32)).astype(out.dtype)


def both(v):
    hi, lo = split(v)
    return jnp.concatenate([hi, lo], 0)


def rounded(v):
    return both(v[:16] + v[16:]) if v.shape[0] == VROWS else v.astype(BF)


def plane_kernel(extra, info, parts, recv, keep, send):
    m = keep.shape[0] - extra
    for b, out in enumerate((keep, send)):
        out[:m, :] = (parts[b, :m, :] + recv[b, :m, :].astype(F32)).astype(out.dtype)
        out[m:, :] = rounded(parts[b, m:, :] + recv[b, m:, :].astype(F32)).astype(out.dtype)


def line_kernel(tensors, chunks, extra, info, part, recv, *refs):
    *cores, keep, send = refs
    m = part.shape[0] - extra
    r = m // (tensors * chunks)
    h = chunks // 2
    if cores:
        rest = rounded(cores[0][...].astype(F32) + cores[1][...].astype(F32))
    else:
        rest = rounded(part[m:, :] + recv[m:, :].astype(F32))
    bit = lax.rem(info[1], 2) if h == 2 else lax.div(info[1], 2)
    for out, which in ((keep, bit), (send, 1 - bit)):
        for t in range(tensors):
            rows = pl.ds(pl.multiple_of((t * chunks + which * h) * r, r), h * r)
            out[t * h * r : (t + 1) * h * r, :] = (part[rows, :] + recv[rows, :].astype(F32)).astype(out.dtype)
        out[tensors * h * r :, :] = rest.astype(out.dtype)


def finish_vo_kernel(info, part, recv, gwv, gwo, token):
    token[...] = jnp.zeros_like(token)
    r = gwv.shape[0]
    gwv[...] = part[:r, :] + recv[:r, :].astype(F32)
    gwo[...] = part[r : 2 * r, :] + recv[r : 2 * r, :].astype(F32)


def spatial_rows_kernel(info, part, recv, sp):
    m = part.shape[0] - sp.shape[0]
    sp[...] = (part[m:, :] + recv[m:, :].astype(F32)).astype(BF)


def vector_rows(part, recv):
    m = part.shape[0] - VROWS
    v = part[m:, :] + recv[m:, :].astype(F32)
    return v[:16] + v[16:]


def finish_g_kernel(info, part, recv, gwg, gbv, gbg, ggain, gshift):
    r = gwg.shape[0]
    gwg[...] = part[:r, :] + recv[:r, :].astype(F32)
    v = vector_rows(part, recv)
    for k, out in enumerate((gbv, gbg, ggain, gshift)):
        out[...] = v[k]


def finish_full_kernel(info, part, recv, gain, shift, rows):
    v = vector_rows(part, recv)
    full = jnp.concatenate([v[4:7, :], v[7:10, :128]], 1)
    gin = (full[0:1, :] - shift[...][None] * full[1:2, :]) / gain[...][None]
    rows[...] = jnp.concatenate([gin, full[1:], jnp.zeros((5, full.shape[1]), F32)], 0)


def spatial_kernel(info, a, rx, ry, rxy, mine, other, out, bias, gin, sin, gout, full):
    q = a.shape[0]
    for ref, k in ((a, 0), (ry, 1), (rx, 2), (rxy, 3)):
        full[pl.ds(pl.multiple_of(jnp.bitwise_xor(2 * info[2] + info[3], k) * q, q), q), :] = ref[...].astype(F32)
    p = out.shape[0]
    out[...] = full[:p, :p]
    bias[...] = full[:, 256:].T[WIN - 256, :p]
    v = jnp.where(info[4] == 0, mine[...], other[...])
    gin[...] = v[0]
    sin[...] = v[1]
    gout[...] = v[2]


def permute(x, to):
    n_dp, n_mp = lax.axis_size("dp"), lax.axis_size("mp")
    pairs = []
    for i in range(n_dp * n_mp):
        dp, mp = to(i // n_mp, i % n_mp)
        pairs.append((i, dp * n_mp + mp))
    return lax.ppermute(x, AXES, pairs)


def core_swap(x):
    return permute(x, lambda dp, mp: (dp, mp ^ 1))


def plane_swaps(a, b, c):
    return (
        permute(a, lambda dp, mp: (dp ^ 1, mp)),
        permute(b, lambda dp, mp: (dp, mp ^ 2)),
        permute(c, lambda dp, mp: (dp ^ 1, mp ^ 2)),
    )


def first_swap(x):
    return permute(x, lambda dp, mp: (dp, mp ^ 2) if mp % 2 == 0 else (dp ^ 1, mp))


def second_swap(x):
    return permute(x, lambda dp, mp: (dp ^ 1, mp) if mp % 2 == 0 else (dp, mp ^ 2))


def z_swap(x, bit):
    return permute(x, lambda dp, mp: (dp ^ (2 * bit), mp))


def line_swaps(arrays):
    n_dp = lax.axis_size("dp")
    return [permute(a, lambda dp, mp, k=k: ((dp + 2 * (k + 1)) % n_dp, mp)) for k, a in enumerate(arrays)]


def gather_dp(copies):
    t = lax.all_to_all(copies, "dp", 0, 0, tiled=True)
    return t.reshape(-1, t.shape[2])


def after(x, y):
    return lax.optimization_barrier((x, y))


def y_swap(x):
    return permute(x, lambda dp, mp: (dp, mp ^ 2))


def scatter_any(keep, recv):
    n = lax.axis_size("dp")
    c = keep.shape[1] // 2
    a = keep.astype(F32) + recv.astype(F32)
    s = a[:, :c] + permute(a[:, c:].astype(BF), lambda dp, mp: (dp, mp ^ 2)).astype(F32)
    return lax.all_to_all(s.astype(BF).reshape(n, -1, c), "dp", 0, 0, tiled=True).astype(F32).sum(0)


def body(inputs, counts, input_norm_gain, shift_in, w_value, w_gate, bias_value, bias_gate, gate_gain, gate_shift, spatial, spatial_bias, w_out, out_bias, cotangent):
    n_dp, n_mp = lax.axis_size("dp"), lax.axis_size("mp")
    me, dp = lax.axis_index("mp"), lax.axis_index("dp")
    r, c = w_value.shape
    d = inputs.shape[1]
    p = spatial.shape[0]
    n = counts.shape[0] // n_mp
    quick = n_dp == 8 and r % 16 == 0
    head = jnp.stack([me, dp // 2, dp % 2, me // 2, me % 2, me * n, 0, 0]).astype(jnp.int32)
    info = jnp.concatenate([head, counts])

    args = in_hbm(w_gate, w_value, w_out.T, bias_value, bias_gate, gate_gain, gate_shift)
    pg, vo1, vec = simple_call(cast_kernel, info, args, [shape((r, c), BF), shape((r, 2 * c), BF), shape((16, c), BF)], "casts")
    if quick:
        zg, zvo = line_swaps([pg] * 3), line_swaps([vo1] * 3)
        zg = stack_call(info, (pg, *zg, vec), (), "line_gate")
        pieces = (zg, *plane_swaps(zg, zg, zg))
    else:
        copies = lambda a: gather_dp(jnp.broadcast_to(a[None], (n_dp,) + a.shape))
        g0 = jnp.concatenate([copies(pg), vec])
        zg = wga = jnp.concatenate([g0, y_swap(g0)], 1)
        vo0 = copies(vo1)
        vo2 = y_swap(vo0)
        zvo = ()
        voa = jnp.concatenate([vo0[:, :c], vo2[:, :c], vo0[:, c:], vo2[:, c:]], 1)
    normed, g_win, gsum = norm_call(info, inputs, cotangent, input_norm_gain, shift_in, n, (zg,))
    if quick:
        wga = assemble_call(info, pieces, 1, 16, (gsum, *zvo), "assemble_gate")
        zvo = stack_call(info, (vo1, *zvo), (wga,), "line_value_out")
        pieces = (zvo, *plane_swaps(zvo, zvo, zvo))
    s, st, sb, token = windows_call(info, spatial, spatial_bias, n, (zvo,) if quick else (gsum,))
    wgb = core_swap(wga)
    rows, hat, slope, inv, shifted, vec = gate_call(info, (wga, wgb), normed, s, sb, (token,))
    if quick:
        *rest, vec = lax.optimization_barrier((*pieces[1:], vec))
        pieces = (pieces[0], *rest)
        swapped = tuple(core_swap(a) for a in pieces)
        voa = assemble_call(info, pieces, 2, 0, (vec,), "assemble_own")
        vob = assemble_call(info, swapped, 2, 0, (voa,), "assemble_other")
    else:
        vob = core_swap(voa)
    zero = jnp.zeros((PAD, PAD), F32)
    prod_b, ds_b, dpv_b, gw_b, gb_b, gsp, small_b = value_call(info, 1, False, vob, normed, g_win, vec, shifted, rows, zero)
    recv_vo = core_swap(gw_b)
    prod_a, ds_a, dpv_a, gw_a, gb_a, gsp, small_a = value_call(info, 0, True, voa, normed, g_win, vec, shifted, rows, gsp)
    q = PAD // 4
    def plane(parts, recv, extra, name, after):
        s = parts.shape[1:]
        return simple_call(lambda *a: plane_kernel(extra, *a), info, (parts, recv), [shape(s, F32), shape(s, BF)], name, after=after)

    def line(part, recv, tensors, chunks, extra, name, after, cores=()):
        s = ((part.shape[0] - extra) // 2 + extra, c)
        return simple_call(lambda *a: line_kernel(tensors, chunks, extra, *a), info, (part, recv, *cores), [shape(s, F32), shape(s, BF)], name, after=after)

    if quick:
        kvo, snd = simple_call(quarter_kernel, info, (gw_a, recv_vo, gsp), [shape((2, 8 * r + q, c), t) for t in (F32, BF)], "quarters_vo")
        got_vo = first_swap(snd)
    dpg, keep_g, send_g, vown = back_call(info, normed, (ds_a, ds_b), hat, slope, inv, st, vec, (wga, wgb), (gb_a, gb_b), (small_a, small_b), gsum, (snd,) if quick else ())
    recv_g = core_swap(send_g)
    token = vown
    if quick:
        rows_g = 8 * r + 2 * VROWS
        kg, snd = simple_call(pair_half_kernel, info, (keep_g, recv_g, vown), [shape((rows_g, c), t) for t in (F32, BF)], "halves_g")
        got_g = z_swap(snd, 1)
        kvo, snd = plane(kvo, got_vo, q, "plane_vo", (snd,))
        got_vo = second_swap(snd)
        token = snd
    res, token = result_call(info, inputs, (prod_a, prod_b), (voa, vob), out_bias, (token,))
    if quick:
        (sp,) = simple_call(spatial_rows_kernel, info, (kvo, got_vo), [shape((q, c), BF)], "spatial_plane", after=(token,))
        kvo, snd = line(kvo, got_vo, 2, 4, q, "line_vo", (), (sp, core_swap(sp)))
        got_vo = z_swap(snd, 1)
        rows_g = 2 * r + VROWS
        kg, snd = simple_call(first_half_kernel, info, (kg, got_g), [shape((2, rows_g, c), t) for t in (F32, BF)], "quarters_g", after=(snd,))
        got_g = first_swap(snd)
        token = snd
    dnv, token = value_part_call(info, (dpv_a, dpv_b), (voa, vob), d, (token,))
    if quick:
        kg, snd = plane(kg, got_g, VROWS, "plane_g", (token,))
        got_g = second_swap(snd)
        kvo, snd = line(kvo, got_vo, 2, 2, q, "pair_vo", (snd,))
        got_vo = z_swap(snd, 2)
        token = snd
    ing, token = grad_call(info, inputs, cotangent, dnv, dpg, (wga, wgb), input_norm_gain, (token,))
    if quick:
        kg, snd = line(kg, got_g, 1, 2, VROWS, "pair_g", (token,))
        got_g = z_swap(snd, 2)
        (sp,) = simple_call(spatial_rows_kernel, info, (kvo, got_vo), [shape((q, c), BF)], "spatial_rows", after=(token,))
        gwv, gwo, token = simple_call(finish_vo_kernel, info, (kvo, got_vo), [shape((r, c), F32)] * 2 + [shape((8, 128), F32)], "finish_vo", after=(sp,))
        sps = plane_swaps(sp, sp, sp)
        one = shape((c,), F32)
        (full,) = simple_call(finish_full_kernel, info, (kg, got_g, input_norm_gain, shift_in), [shape((8, d), F32)], "finish_full", after=(token,))
        gwg, gbv, gbg, ggain, gshift = simple_call(finish_g_kernel, info, (kg, got_g), [shape((r, c), F32)] + [one] * 4, "finish_g", after=(full,))
        gspat, gsb, gin, sin, gob = simple_call(spatial_kernel, info, (sp, *sps, full, core_swap(full)), [shape((p, p), F32), shape((p,), F32)] + [shape((d,), F32)] * 3, "spatial_sum", [pltpu.VMEM((PAD, PAD), F32)])
    else:
        gwv = scatter_any(gw_a[:d], recv_vo[:d])
        gwo = scatter_any(gw_a[d:], recv_vo[d:])
        gwg = scatter_any(keep_g, recv_g[:d])
        gsp = lax.psum(gsp, AXES)
        gspat, gsb = gsp[:p, :p], gsp[:p, WIN]
        other = send_g[d:].astype(F32)
        other = other[:8] + other[8:]
        back = jnp.argsort(jnp.bitwise_xor(jnp.array(ORDER, jnp.int32), me))
        four = jnp.concatenate([vown[:4], other[:4]], 1).reshape(4, n_mp, c)
        four = lax.psum(jnp.take(four, back, axis=1), AXES)
        gbv, gbg, ggain, gshift = lax.dynamic_index_in_dim(four, me, 1, keepdims=False)
        t, sin, gob = lax.psum(vown[4:7, :d], AXES)
        gin = (t - shift_in * sin) / input_norm_gain
    return (res, ing, gin, sin, gwv, gwg, gbv, gbg, ggain, gshift, gspat, gsb, gwo.T, gob)


def solution(mesh):
    row, wi, mp, al = P(("dp", "mp"), None), P("dp", "mp"), P("mp"), P()
    return jax.shard_map(
        body, mesh=mesh,
        in_specs=(row, P("dp"), al, al, wi, wi, mp, mp, mp, mp, al, al, P("mp", "dp"), al, row),
        out_specs=(row, row, al, al, wi, wi, mp, mp, mp, mp, al, al, P("mp", "dp"), al),
        check_vma=False,
    )
```

```python
import jax
import jax.numpy as jnp
from jax import lax
from jax.experimental import pallas as pl
from jax.experimental.pallas import tpu as pltpu
from jax.sharding import PartitionSpec as P

EPS = 1e-5
BF = jnp.bfloat16
F32 = jnp.float32
AXES = ("dp", "mp")
WIN = 336
STEP = 320
EXT = 352
CH = 16
PAD = 384
ORDER = (0, 2, 1, 3)
GELU_C = (7.97869712e-01, 3.63922863e-02, -8.78266205e-05, -3.66934307e-05, 1.42500480e-06)
LOG2E_HALF = -0.7213475204444817
INV_SQRT_2PI = 0.3989422804014327
MB = 2**20


def dot(a, b):
    return jnp.dot(a, b, preferred_element_type=F32)


def dot_tn(a, b):
    return lax.dot_general(a, b, (((0,), (0,)), ((), ())), preferred_element_type=F32)


def dot_nt(a, b):
    return lax.dot_general(a, b, (((1,), (1,)), ((), ())), preferred_element_type=F32)


def gelu_both(x):
    u = x * x
    p = GELU_C[4]
    for c in GELU_C[3::-1]:
        p = p * u + c
    cdf = 0.5 + 0.5 * jnp.tanh(x * p)
    slope = cdf + (x * INV_SQRT_2PI) * jnp.exp2(u * LOG2E_HALF)
    return x * cdf, slope


def split(v):
    hi = v.astype(BF)
    return hi, (v - hi.astype(F32)).astype(BF)


def fold8(v):
    out = v[0:8]
    for r in range(8, v.shape[0], 8):
        out = out + v[r : r + 8]
    return out


def img(*s):
    return pl.BlockSpec((1,) + s, lambda b, *_: (b,) + (0,) * len(s))


def const(*s):
    return pl.BlockSpec(s, lambda b, *_: (0,) * len(s), pipeline_mode=pl.Buffered(1))


def half(rows, c, h):
    return pl.BlockSpec((1, rows, c), lambda b, *_: (b, 0, h))


def side(d, w, h):
    return pl.BlockSpec((d, w), lambda b, *_: (0, h), pipeline_mode=pl.Buffered(1))


def shape(s, t):
    return jax.ShapeDtypeStruct(s, t)


def fast(s, t):
    return pltpu.VMEM(s, t)


def slow(s, t):
    return pltpu.HBM(s, t)


def in_vmem(*arrays):
    return tuple(pltpu.with_memory_space_constraint(a, pltpu.VMEM) for a in arrays)


def in_hbm(*arrays):
    return tuple(pltpu.with_memory_space_constraint(a, pltpu.HBM) for a in arrays)


ANY = pl.BlockSpec(memory_space=pl.ANY)
VM = pl.BlockSpec(memory_space=pltpu.VMEM)


class Place:
    def __init__(self, counts):
        self.counts = counts

    def __getitem__(self, k):
        if not isinstance(k, int):
            return self.counts[k - 8]
        me, dp = lax.axis_index("mp"), lax.axis_index("dp")
        images = self.counts.shape[0] // lax.axis_size("mp")
        return (me, lax.div(dp, 2), lax.rem(dp, 2), lax.div(me, 2), lax.rem(me, 2), me * images)[k]


def call(kernel, info, args, in_specs, outs, out_specs, scratch=(), grid=(1,), name=None, after=(), vmem=8, us=1):
    n_in, n_after = len(args), len(after)

    def ordered(counts_ref, *refs):
        kernel(Place(counts_ref), *refs[:n_in], *refs[n_in + n_after :])

    return pl.pallas_call(
        ordered,
        grid_spec=pltpu.PrefetchScalarGridSpec(
            num_scalar_prefetch=1, grid=grid, in_specs=list(in_specs) + [ANY] * n_after, out_specs=out_specs, scratch_shapes=list(scratch)
        ),
        out_shape=outs,
        compiler_params=pltpu.CompilerParams(vmem_limit_bytes=vmem * MB),
        cost_estimate=pl.CostEstimate(flops=int(us * 1.1e9), bytes_accessed=int(us * 3.3e6), transcendentals=0),
        name=name,
    )(info, *args, *after)


def whole(a):
    return const(*a.shape)


def simple_call(kernel, info, args, outs, name, scratch=(), after=(), us=1):
    return call(kernel, info, args, [whole(a) for a in args], outs, [whole(o) for o in outs], scratch, name=name, after=after, us=us)


SLOTS = 2
GATE_MB, VALUE_MB, BACK_MB = 11, 14, 16


def pipelined(n, products, arithmetic):
    for b in range(min(n, SLOTS - 1)):
        products(b)
    for b in range(n):
        if b + SLOTS - 1 < n:
            products(b + SLOTS - 1)
        arithmetic(b)


def cast_kernel(info, wg_ref, wv_ref, wo_ref, bv, bg, gg, gs, g_ref, vo_ref, vec_ref):
    c = wg_ref.shape[1]
    g_ref[...] = wg_ref[...].astype(BF)
    vo_ref[:, :c] = wv_ref[...].astype(BF)
    vo_ref[:, c:] = wo_ref[...].astype(BF)
    vec_ref[...] = both(jnp.concatenate([bv[...][None], bg[...][None], gg[...][None], gs[...][None], jnp.zeros((4, bv.shape[0]), F32)], 0))


def run_copies(pairs, sems):
    copies = [pltpu.make_async_copy(src, dst, sems.at[k]) for k, (src, dst) in enumerate(pairs)]
    for c in copies:
        c.start()
    for c in copies:
        c.wait()


def stack_kernel(info, *refs):
    *parts, out, sems = refs
    pairs, at = [], 0
    for ref in parts:
        n = ref.shape[0]
        pairs.append((ref, out.at[at : at + n]))
        at += n
    run_copies(pairs, sems)


def stack_call(info, parts, after, name):
    n = len(parts)
    rows, c = sum(a.shape[0] for a in parts), parts[0].shape[1]
    return call(stack_kernel, info, parts, [ANY] * n, [shape((rows, c), BF)], [ANY], [pltpu.SemaphoreType.DMA((n,))], name=name, after=after)[0]


def assemble_kernel(tensors, extra, info, *refs):
    *pieces, out, sems = refs
    if len(pieces) == 1:
        return run_copies([(pieces[0], out)], sems)
    where = ((0, 0), (1, 0), (0, 1), (1, 1))
    d, c = out.shape[0] - extra, out.shape[1] // (2 * tensors)
    n = 4
    r = d // (2 * n)
    pairs = []
    for ref, (xr, slot) in zip(pieces, where):
        for t in range(tensors):
            src, dst = slice(t * c, (t + 1) * c), slice((2 * t + slot) * c, (2 * t + slot + 1) * c)
            for k in range(n):
                row = pl.multiple_of((lax.rem(info[1] + (n - k), n) * 2 + jnp.bitwise_xor(info[2], xr)) * r, r)
                pairs.append((ref.at[k * r : (k + 1) * r, src], out.at[pl.ds(row, r), dst]))
            if xr == 0 and extra:
                pairs.append((ref.at[n * r :, src], out.at[d:, dst]))
    run_copies(pairs, sems)


def assemble_call(info, pieces, tensors, extra, after, name):
    rows, c = pieces[0].shape
    s = (2 * (rows - extra) + extra, 2 * c)
    return call(lambda *a: assemble_kernel(tensors, extra, *a), info, pieces, [ANY] * len(pieces), [shape(s, BF)],
                [const(*s)], [pltpu.SemaphoreType.DMA((18 * tensors,))], name=name, after=after)[0]


def shift_of(b):
    return 4 * b


def norm_kernel(info, x_ref, g_ref, gain_ref, shift_ref, n_ref, gw_ref, gsum_ref, rows):
    b = pl.program_id(0)

    @pl.when(b == 0)
    def _():
        gsum_ref[...] = jnp.zeros_like(gsum_ref)

    own = jnp.where(b == pl.num_programs(0) - 1, 1.0, 0.0)
    up = WIN - shift_of(b)
    for r in range(0, WIN, 48):
        x = x_ref[r : r + 48, :].astype(F32)
        cen = x - jnp.mean(x, -1, keepdims=True)
        inv = lax.rsqrt(jnp.mean(cen * cen, -1, keepdims=True) + EPS)
        rows[r : r + 48, :] = cen * inv * gain_ref[...][None] + shift_ref[...][None]
    n_ref[b] = pltpu.roll(rows[...], up, 0).astype(BF)
    g = g_ref[...].astype(F32)
    gw_ref[b] = pltpu.roll(g, up, 0).astype(BF)
    gsum_ref[...] += jnp.sum(fold8(g[:STEP]) + fold8(g[STEP:]) * own, 0, keepdims=True)


def window_rows(d):
    return pl.BlockSpec((pl.Element(WIN), pl.Element(d)), lambda b, *_: (b * STEP, 0))


def norm_call(info, x, g, gain, shift, n, after):
    d = x.shape[1]
    return call(norm_kernel, info, in_hbm(x, g, gain, shift), [window_rows(d), window_rows(d), const(d), const(d)],
                [fast((n, WIN, d), BF), fast((n, WIN, d), BF), shape((1, d), F32)], [VM, VM, const(1, d)],
                [pltpu.VMEM((WIN, d), F32)], grid=(n,), name="input_norm", after=after, us=3)


def windows_kernel(info, sp_ref, sb_ref, s_ref, st_ref, sbw_ref, token, pad, tpad, col):
    p = sp_ref.shape[0]
    b = pl.program_id(0)

    @pl.when(b == 0)
    def _():
        pad[...] = jnp.zeros_like(pad)
        pad[0:p, 0:p] = sp_ref[...]
        tpad[...] = pad[...].T
        col[...] = jnp.concatenate([jnp.broadcast_to(sb_ref[...][None], (128, p)), jnp.zeros((128, PAD - p), F32)], 1).T
        token[...] = jnp.zeros_like(token)

    ri = lax.broadcasted_iota(jnp.int32, (WIN, WIN), 0)
    ci = lax.broadcasted_iota(jnp.int32, (WIN, WIN), 1)
    end = count_of(info, b)
    live = (ri < end) & (ci < end)
    s_ref[b] = jnp.where(live, pad[:WIN, :WIN], 0.0).astype(BF)
    st_ref[b] = jnp.where(live, tpad[:WIN, :WIN], 0.0).astype(BF)
    sbw_ref[b] = jnp.where((ri < end)[:, :128], col[:WIN], 0.0)


def count_of(info, b):
    return info[8 + info[5] + b]


def windows_call(info, spatial, sbias, n, after):
    p = spatial.shape[0]
    win = fast((n, WIN, WIN), BF)
    return call(windows_kernel, info, in_hbm(spatial, sbias), [const(p, p), const(p)], [win, win, fast((n, WIN, 128), F32), shape((8, 128), F32)],
                [VM, VM, VM, const(8, 128)], [pltpu.VMEM((PAD, PAD), F32)] * 2 + [pltpu.VMEM((PAD, 128), F32)],
                grid=(n,), name="windows", after=after, us=2)


def gate_kernel(info, wa_ref, wb_ref, n_ref, s_ref, sb_ref, rows_ref, hat_ref, slope_ref, inv_ref, shifted_ref, v_ref, pres):
    w = wa_ref.shape[1]
    d = wa_ref.shape[0] - 16
    width = 2 * w
    for k, ref in enumerate((wa_ref, wb_ref)):
        v = ref[d:, :].astype(F32)
        v_ref[:, k * w : (k + 1) * w] = v[:8] + v[8:]
    bias, gain, shift = v_ref[1:2, :], v_ref[2:3, :], v_ref[3:4, :]

    def products(b):
        pre = pres.at[b % SLOTS]
        pre[:, :w] = dot(n_ref[b], wa_ref[:d, :])
        pre[:, w:] = dot(n_ref[b], wb_ref[:d, :])

    def arithmetic(b):
        pre = pres.at[b % SLOTS]
        for r in range(0, WIN, CH):
            act, slope = gelu_both(pre[r : r + CH, :] + bias)
            slope_ref[b, r : r + CH, :] = slope.astype(BF)
            cen = act - jnp.sum(act, -1, keepdims=True) * (1.0 / width)
            inv = lax.rsqrt(jnp.sum(cen * cen, -1, keepdims=True) * (1.0 / width) + EPS)
            hat = cen * inv
            inv_ref[b, r : r + CH, :] = jnp.broadcast_to(inv, (CH, 128))
            hat_ref[b, r : r + CH, :] = hat.astype(BF)
            rows_ref[b, r : r + CH, :] = (hat * gain + shift).astype(BF)
        rows_ref[b, WIN:, :] = jnp.ones((EXT - WIN, width), BF)
        sb = sb_ref[b]
        mixed = dot(s_ref[b], rows_ref[b, :WIN, :])
        for t in range(0, width, 128):
            shifted_ref[b, :, t : t + 128] = (mixed[:, t : t + 128] + sb).astype(BF)

    pipelined(n_ref.shape[0], products, arithmetic)


def gate_call(info, halves, normed, s, sb, after):
    n, _, d = normed.shape
    w = 2 * halves[0].shape[1]
    big = fast((n, WIN, w), BF)
    return call(
        gate_kernel, info, (*halves, *in_vmem(normed, s, sb)), [whole(a) for a in halves] + [VM] * 3,
        [fast((n, EXT, w), BF), big, big, fast((n, WIN, 128), F32), big, shape((8, w), F32)], [VM] * 5 + [const(8, w)],
        [pltpu.VMEM((SLOTS, WIN, w), F32)], name="gate_forward", after=after, us=1, vmem=GATE_MB,
    )


def value_kernel(h, info, wv_ref, wo_ref, n_ref, g_ref, v_ref, shifted_ref, rows_ref, gin_ref, prod_ref, dshift_ref, dpre_ref, gw_ref, gb_ref, gsp_ref, small_ref,
                 pres, dprods):
    d, w = wv_ref.shape
    cols = slice(h * w, (h + 1) * w)
    gb_ref[...] = jnp.zeros_like(gb_ref)
    gsp_ref[...] = gin_ref[...]

    def products(b):
        pre, dprod = pres.at[b % SLOTS], dprods.at[b % SLOTS]
        pre[...] = dot(n_ref[b], wv_ref[...])
        dprod[...] = dot(g_ref[b], wo_ref[...])

    def arithmetic(b):
        pre, dprod = pres.at[b % SLOTS], dprods.at[b % SLOTS]
        bias = v_ref[0:1, :]
        for r in range(0, WIN, CH):
            act, slope = gelu_both(pre[r : r + CH, :] + bias)
            sh = shifted_ref[b, r : r + CH, cols].astype(F32)
            dp = dprod[r : r + CH, :]
            prod = (act * sh).astype(BF)
            prod_ref[b, r : r + CH, :] = prod
            dshift_ref[b, r : r + CH, :] = (dp * act).astype(BF)
            dv = dp * sh * slope
            dvl = dv.astype(BF)
            dpre_ref[b, r : r + CH, :] = dvl
            gb_ref[...] += fold8(dv)
        part = dot_nt(dshift_ref[b], rows_ref[b, :, cols])
        end = count_of(info, b)
        ri = lax.broadcasted_iota(jnp.int32, (WIN, EXT), 0)
        ci = lax.broadcasted_iota(jnp.int32, (WIN, EXT), 1)
        live = (ri < end) & ((ci < end) | (ci >= WIN))
        gsp_ref[:WIN, :EXT] += jnp.where(live, part, 0.0)

    pipelined(n_ref.shape[0], products, arithmetic)
    gwv = dot_tn(n_ref[...].reshape(-1, d), dpre_ref[...].reshape(-1, w))
    gw_ref[:d, :] = gwv.astype(gw_ref.dtype)
    gw_ref[d:, :] = dot_tn(g_ref[...].reshape(-1, d), prod_ref[...].reshape(-1, w)).astype(gw_ref.dtype)
    small_ref[...] = jnp.concatenate([row_sums(gwv, wv_ref), back_sum(gb_ref[...], wv_ref), jnp.zeros((6, d), F32)], 0)


def row_sums(gw, w_ref):
    prod = gw * w_ref[...].astype(F32)
    t = prod[:, :128]
    for k in range(128, prod.shape[1], 128):
        t = t + prod[:, k : k + 128]
    return jnp.sum(t.T, 0, keepdims=True)


def back_sum(sums, w_ref):
    hi, lo = split(sums)
    return jnp.sum(dot_nt(hi, w_ref[...]) + dot_nt(lo, w_ref[...]), 0, keepdims=True)


def value_call(info, h, keep, vo, normed, g, vecs, shifted, rows, gsp, after=()):
    n, _, d = normed.shape
    w = vecs.shape[1] // 2
    big = fast((n, WIN, w), BF)
    return call(
        lambda *a: value_kernel(h, *a), info, (vo, vo, *in_vmem(normed, g), vecs, *in_vmem(shifted, rows), gsp),
        [side(d, w, 0), side(d, w, 1), VM, VM, pl.BlockSpec((8, w), lambda b, *_: (0, h)), VM, VM, const(PAD, PAD)],
        [big, big, big, shape((2 * d, w), BF), shape((8, w), F32), shape((PAD, PAD), F32), shape((8, d), F32)],
        [VM] * 3 + [const(2 * d, w), const(8, w), const(PAD, PAD), const(8, d)],
        [pltpu.VMEM((SLOTS, WIN, w), F32)] * 2, name="value_own" if keep else "value_other", after=after, us=1, vmem=VALUE_MB,
    )


def back_kernel(info, n_ref, dsa_ref, dsb_ref, rows_hat_ref, slope_ref, inv_ref, st_ref, v_ref, wa_ref, wb_ref, gba_ref, gbb_ref, sma_ref, smb_ref, gsum_ref,
                dpre_ref, keep_ref, send_ref, vown_ref, dgrs, gb, gg, gsh):
    d, w = n_ref.shape[2], wa_ref.shape[1]
    width = 2 * w
    wa_ref, wb_ref = wa_ref.at[:d], wb_ref.at[:d]
    for r in (gb, gg, gsh):
        r[...] = jnp.zeros_like(r)
    gain = v_ref[2:3, :]

    def products(b):
        dgr = dgrs.at[b % SLOTS]
        dgr[:, :w] = dot(st_ref[b], dsa_ref[b])
        dgr[:, w:] = dot(st_ref[b], dsb_ref[b])

    def arithmetic(b):
        dgr = dgrs.at[b % SLOTS]
        for r in range(0, WIN, CH):
            dr = dgr[r : r + CH, :]
            hat = rows_hat_ref[b, r : r + CH, :].astype(F32)
            gg[...] += fold8(dr * hat)
            gsh[...] += fold8(dr)
            dg = dr * gain
            m1 = jnp.sum(dg, -1, keepdims=True) * (1.0 / width)
            m2 = jnp.sum(dg * hat, -1, keepdims=True) * (1.0 / width)
            dpg = (dg - m1 - hat * m2) * inv_ref[b, r : r + CH, 0:1] * slope_ref[b, r : r + CH, :].astype(F32)
            dpre_ref[b, r : r + CH, :] = dpg.astype(BF)
            gb[...] += fold8(dpg)

    pipelined(n_ref.shape[0], products, arithmetic)

    gw = dot_tn(n_ref[...].reshape(-1, d), dpre_ref[...].reshape(-1, width))
    keep_ref[...] = gw[:, :w].astype(BF)
    sums = gb[...]
    send_ref[:d, :] = gw[:, w:].astype(BF)
    t = sma_ref[0:1, :] + smb_ref[0:1, :] + row_sums(gw[:, :w], wa_ref) + row_sums(gw[:, w:], wb_ref)
    s = sma_ref[1:2, :] + smb_ref[1:2, :] + back_sum(sums[:, :w], wa_ref) + back_sum(sums[:, w:], wb_ref)
    one = lambda v: jnp.sum(v, 0, keepdims=True)
    fours = [jnp.concatenate([one(gba_ref[...]), one(gbb_ref[...])], 1), one(gb[...]), one(gg[...]), one(gsh[...])]
    wide = lambda v: jnp.concatenate([v, jnp.zeros((1, w - d), F32)], 1)
    full = jnp.concatenate([wide(t), wide(s), wide(gsum_ref[...]), jnp.zeros((1, w), F32)], 0)
    fours = jnp.concatenate(fours, 0)
    hi, lo = split(jnp.concatenate([fours[:, w:], full], 0))
    send_ref[d:, :] = jnp.concatenate([hi, lo], 0)
    fhi, flo = split(full)
    vown_ref[...] = jnp.concatenate([fours[:, :w], fhi.astype(F32) + flo.astype(F32)], 0)


def back_call(info, normed, ds, hat, slope, inv, st, vecs, wg, gbv, small, gsum, after):
    n, _, d = normed.shape
    width = vecs.shape[1]
    w = width // 2
    return call(
        back_kernel, info, (*in_vmem(normed, *ds, hat, slope, inv, st), vecs, *wg, *gbv, *small, gsum),
        [VM] * 7 + [const(8, width), whole(wg[0]), whole(wg[1]), const(8, w), const(8, w), const(8, d), const(8, d), const(1, d)],
        [fast((n, WIN, width), BF), shape((d, w), BF), shape((d + 16, w), BF), shape((8, w), F32)],
        [VM, const(d, w), const(d + 16, w), const(8, w)],
        [pltpu.VMEM((SLOTS, WIN, width), F32)] + [pltpu.VMEM((8, width), F32)] * 3, name="gate_backward", after=after, us=1, vmem=BACK_MB,
    )


def rows_of(windows, finish, out_hbm, out, sems):
    n = windows.shape[0]
    copies = []
    carry = None
    for b in range(n):
        v = windows[b]
        if b:
            v = pltpu.roll(v, shift_of(b), 0)
            windows[b] = jnp.concatenate([v[:16] + carry, v[16:]], 0)
        carry = v[STEP:]
        first, count = b * STEP, STEP if b < n - 1 else WIN
        for r in range(0, count, 320):
            e = min(r + 320, count)
            out[first + r : first + e, :] = finish(slice(first + r, first + e), windows[b, r:e, :]).astype(out.dtype)
        copies.append(pltpu.make_async_copy(out.at[first : first + count], out_hbm.at[first : first + count], sems.at[b]))
        copies[-1].start()
    for c in copies:
        c.wait()


def result_kernel(info, x_hbm, pa_ref, pb_ref, woa_ref, wob_ref, bias_ref, res_hbm, token, xs, br, out, sems):
    n = pa_ref.shape[0]
    get = pltpu.make_async_copy(x_hbm, xs, sems.at[n])
    get.start()
    token[...] = jnp.zeros_like(token)
    for b in range(n):
        br[b] = dot_nt(pa_ref[b], woa_ref[...]) + dot_nt(pb_ref[b], wob_ref[...])
    get.wait()
    bias = bias_ref[...][None]
    rows_of(br, lambda at, v: xs[at, :].astype(F32) + v + bias, res_hbm, out, sems)


def value_part_kernel(info, va_ref, vb_ref, wva_ref, wvb_ref, out_ref, token):
    token[...] = jnp.zeros_like(token)
    for b in range(va_ref.shape[0]):
        out_ref[b] = dot_nt(va_ref[b], wva_ref[...]) + dot_nt(vb_ref[b], wvb_ref[...])


def grad_kernel(info, x_hbm, g_hbm, dv_ref, dg_ref, wga_ref, wgb_ref, gain_ref, ing_hbm, token, xs, gs, dn, out, sems):
    n, _, d = dv_ref.shape
    w = wga_ref.shape[1]
    gets = [pltpu.make_async_copy(src, dst, sems.at[n + k]) for k, (src, dst) in enumerate(((x_hbm, xs), (g_hbm, gs)))]
    for get in gets:
        get.start()
    token[...] = jnp.zeros_like(token)
    for b in range(n):
        dn[b] = dv_ref[b] + dot_nt(dg_ref[b, :, :w], wga_ref[:d, :]) + dot_nt(dg_ref[b, :, w:], wgb_ref[:d, :])
    for get in gets:
        get.wait()
    gain = gain_ref[...][None]

    def finish(at, v):
        x = xs[at, :].astype(F32)
        cen = x - jnp.mean(x, -1, keepdims=True)
        inv = lax.rsqrt(jnp.mean(cen * cen, -1, keepdims=True) + EPS)
        hat = cen * inv
        dx = v * gain
        m1 = jnp.mean(dx, -1, keepdims=True)
        m2 = jnp.mean(dx * hat, -1, keepdims=True)
        return gs[at, :].astype(F32) + inv * (dx - m1 - hat * m2)

    rows_of(dn, finish, ing_hbm, out, sems)


def result_call(info, x, prod, vo, bias, after):
    n, _, w = prod[0].shape
    rows, d = x.shape
    return call(
        result_kernel, info, (*in_hbm(x), *in_vmem(*prod), *vo, *in_hbm(bias)), [ANY, VM, VM, side(d, w, 1), side(d, w, 1), const(d)],
        [slow((rows, d), BF), shape((8, 128), F32)], [ANY, const(8, 128)],
        [pltpu.VMEM((rows, d), BF), pltpu.VMEM((n, WIN, d), F32), pltpu.VMEM((rows, d), BF), pltpu.SemaphoreType.DMA((n + 1,))],
        name="result", after=after, us=1, vmem=10,
    )


def value_part_call(info, dpv, vo, d, after):
    n, _, w = dpv[0].shape
    return call(
        value_part_kernel, info, (*in_vmem(*dpv), *vo), [VM, VM, side(d, w, 0), side(d, w, 0)],
        [fast((n, WIN, d), F32), shape((8, 128), F32)], [VM, const(8, 128)], name="value_part", after=after, us=1, vmem=4,
    )


def grad_call(info, x, g, dv, dpg, wg, gain, after):
    n = dv.shape[0]
    rows, d = x.shape
    return call(
        grad_kernel, info, (*in_hbm(x, g), *in_vmem(dv, dpg), *wg, *in_hbm(gain)), [ANY, ANY, VM, VM, whole(wg[0]), whole(wg[1]), const(d)],
        [slow((rows, d), F32), shape((8, 128), F32)], [ANY, const(8, 128)],
        [pltpu.VMEM((rows, d), BF)] * 2 + [pltpu.VMEM((n, WIN, d), F32), pltpu.VMEM((rows, d), F32), pltpu.SemaphoreType.DMA((n + 2,))],
        name="input_grad", after=after, us=1, vmem=13,
    )


VROWS = 32


Z_ORDER = (0, 2, 1, 3)


def quarter_kernel(info, keep, recv, gsp, *outs):
    x, y, core = info[2], info[3], info[4]
    d = keep.shape[0] // 2
    c = keep.shape[1] // 2
    r = d // 8
    q = PAD // 4
    for a, out in enumerate(outs):
        for b in range(2):
            xr, yr = jnp.where(core == 0, b, a), jnp.where(core == 0, a, b)
            cols = pl.ds(pl.multiple_of(yr * c, c), c)
            for t in range(2):
                for at, z in enumerate(Z_ORDER):
                    row = pl.multiple_of(t * d + (2 * z + jnp.bitwise_xor(x, xr)) * r, r)
                    dst = (4 * t + at) * r
                    out[b, dst : dst + r, :] = (keep[pl.ds(row, r), cols].astype(F32) + recv[pl.ds(row, r), cols].astype(F32)).astype(out.dtype)
            row = pl.multiple_of((2 * jnp.bitwise_xor(x, xr) + jnp.bitwise_xor(y, yr)) * q, q)
            out[b, 8 * r :, :] = gsp[pl.ds(row, q), :].astype(BF).astype(out.dtype)


def pair_half_kernel(info, keep, recv, vown, *outs):
    x, core, low = info[2], info[4], lax.rem(info[1], 2)
    d = keep.shape[0]
    c = keep.shape[1] // 2
    r = d // 8
    got = recv[d:, :].astype(F32)
    v = vown[...] + (got[:8] + got[8:])
    tail = jnp.concatenate([v[4:7, :c], jnp.concatenate([v[4:7, c : c + 128], jnp.zeros((3, c - 128), F32)], 1), jnp.zeros((6, c), F32)], 0)
    vecs = [both(jnp.concatenate([v[0:4, k * c : (k + 1) * c], tail], 0)) for k in range(2)]
    for out, bit in zip(outs, (low, 1 - low)):
        for a in range(2):
            for b in range(2):
                xr, yr = jnp.where(core == 0, b, a), jnp.where(core == 0, a, b)
                cols = pl.ds(pl.multiple_of(yr * c, c), c)
                for high in range(2):
                    row = pl.multiple_of((2 * (2 * high + bit) + jnp.bitwise_xor(x, xr)) * r, r)
                    dst = ((2 * a + b) * 2 + high) * r
                    out[dst : dst + r, :] = (keep[pl.ds(row, r), cols].astype(F32) + recv[pl.ds(row, r), cols].astype(F32)).astype(out.dtype)
        for k in range(2):
            at = 8 * r + k * VROWS
            out[at : at + VROWS, :] = vecs[k].astype(out.dtype)


def first_half_kernel(info, part, recv, keep, send):
    m = keep.shape[1] - VROWS
    base = 4 * m
    vec = [rounded(part[base + k * VROWS : base + (k + 1) * VROWS, :] + recv[base + k * VROWS : base + (k + 1) * VROWS, :].astype(F32)) for k in range(2)]
    for a, out in enumerate((keep, send)):
        for b in range(2):
            rows = slice((2 * a + b) * m, (2 * a + b + 1) * m)
            out[b, :m, :] = (part[rows, :] + recv[rows, :].astype(F32)).astype(out.dtype)
            yr = jnp.where(info[4] == 0, a, b)
            out[b, m:, :] = jnp.where(yr == 0, vec[0].astype(F32), vec[1].astype(F32)).astype(out.dtype)


def both(v):
    hi, lo = split(v)
    return jnp.concatenate([hi, lo], 0)


def rounded(v):
    return both(v[:16] + v[16:]) if v.shape[0] == VROWS else v.astype(BF)


def plane_kernel(extra, info, parts, recv, keep, send):
    m = keep.shape[0] - extra
    for b, out in enumerate((keep, send)):
        out[:m, :] = (parts[b, :m, :] + recv[b, :m, :].astype(F32)).astype(out.dtype)
        out[m:, :] = rounded(parts[b, m:, :] + recv[b, m:, :].astype(F32)).astype(out.dtype)


def line_kernel(tensors, chunks, extra, info, part, recv, *refs):
    *cores, keep, send = refs
    m = part.shape[0] - extra
    r = m // (tensors * chunks)
    h = chunks // 2
    if cores:
        rest = rounded(cores[0][...].astype(F32) + cores[1][...].astype(F32))
    else:
        rest = rounded(part[m:, :] + recv[m:, :].astype(F32))
    bit = lax.rem(info[1], 2) if h == 2 else lax.div(info[1], 2)
    for out, which in ((keep, bit), (send, 1 - bit)):
        for t in range(tensors):
            rows = pl.ds(pl.multiple_of((t * chunks + which * h) * r, r), h * r)
            out[t * h * r : (t + 1) * h * r, :] = (part[rows, :] + recv[rows, :].astype(F32)).astype(out.dtype)
        out[tensors * h * r :, :] = rest.astype(out.dtype)


def finish_vo_kernel(info, part, recv, gwv, gwo, token):
    token[...] = jnp.zeros_like(token)
    r = gwv.shape[0]
    gwv[...] = part[:r, :] + recv[:r, :].astype(F32)
    gwo[...] = part[r : 2 * r, :] + recv[r : 2 * r, :].astype(F32)


def spatial_rows_kernel(info, part, recv, sp):
    m = part.shape[0] - sp.shape[0]
    sp[...] = (part[m:, :] + recv[m:, :].astype(F32)).astype(BF)


def vector_rows(part, recv):
    m = part.shape[0] - VROWS
    v = part[m:, :] + recv[m:, :].astype(F32)
    return v[:16] + v[16:]


def finish_g_kernel(info, part, recv, gwg, gbv, gbg, ggain, gshift):
    r = gwg.shape[0]
    gwg[...] = part[:r, :] + recv[:r, :].astype(F32)
    v = vector_rows(part, recv)
    for k, out in enumerate((gbv, gbg, ggain, gshift)):
        out[...] = v[k]


def finish_full_kernel(info, part, recv, gain, shift, rows):
    v = vector_rows(part, recv)
    full = jnp.concatenate([v[4:7, :], v[7:10, :128]], 1)
    gin = (full[0:1, :] - shift[...][None] * full[1:2, :]) / gain[...][None]
    rows[...] = jnp.concatenate([gin, full[1:], jnp.zeros((5, full.shape[1]), F32)], 0)


def spatial_kernel(info, a, rx, ry, rxy, mine, other, out, bias, gin, sin, gout, full):
    q = a.shape[0]
    for ref, k in ((a, 0), (ry, 1), (rx, 2), (rxy, 3)):
        full[pl.ds(pl.multiple_of(jnp.bitwise_xor(2 * info[2] + info[3], k) * q, q), q), :] = ref[...].astype(F32)
    p = out.shape[0]
    out[...] = full[:p, :p]
    bias[...] = full[:, 256:].T[WIN - 256, :p]
    v = jnp.where(info[4] == 0, mine[...], other[...])
    gin[...] = v[0]
    sin[...] = v[1]
    gout[...] = v[2]


def permute(x, to):
    n_dp, n_mp = lax.axis_size("dp"), lax.axis_size("mp")
    pairs = []
    for i in range(n_dp * n_mp):
        dp, mp = to(i // n_mp, i % n_mp)
        pairs.append((i, dp * n_mp + mp))
    return lax.ppermute(x, AXES, pairs)


def core_swap(x):
    return permute(x, lambda dp, mp: (dp, mp ^ 1))


def plane_swaps(a, b, c):
    return (
        permute(a, lambda dp, mp: (dp ^ 1, mp)),
        permute(b, lambda dp, mp: (dp, mp ^ 2)),
        permute(c, lambda dp, mp: (dp ^ 1, mp ^ 2)),
    )


def first_swap(x):
    return permute(x, lambda dp, mp: (dp, mp ^ 2) if mp % 2 == 0 else (dp ^ 1, mp))


def second_swap(x):
    return permute(x, lambda dp, mp: (dp ^ 1, mp) if mp % 2 == 0 else (dp, mp ^ 2))


def z_swap(x, bit):
    return permute(x, lambda dp, mp: (dp ^ (2 * bit), mp))


def line_swaps(arrays):
    n_dp = lax.axis_size("dp")
    return [permute(a, lambda dp, mp, k=k: ((dp + 2 * (k + 1)) % n_dp, mp)) for k, a in enumerate(arrays)]


def gather_dp(copies):
    t = lax.all_to_all(copies, "dp", 0, 0, tiled=True)
    return t.reshape(-1, t.shape[2])


def after(x, y):
    return lax.optimization_barrier((x, y))


def y_swap(x):
    return permute(x, lambda dp, mp: (dp, mp ^ 2))


def scatter_any(keep, recv):
    n = lax.axis_size("dp")
    c = keep.shape[1] // 2
    a = keep.astype(F32) + recv.astype(F32)
    s = a[:, :c] + permute(a[:, c:].astype(BF), lambda dp, mp: (dp, mp ^ 2)).astype(F32)
    return lax.all_to_all(s.astype(BF).reshape(n, -1, c), "dp", 0, 0, tiled=True).astype(F32).sum(0)


def body(inputs, counts, input_norm_gain, shift_in, w_value, w_gate, bias_value, bias_gate, gate_gain, gate_shift, spatial, spatial_bias, w_out, out_bias, cotangent):
    n_dp, n_mp = lax.axis_size("dp"), lax.axis_size("mp")
    me, dp = lax.axis_index("mp"), lax.axis_index("dp")
    r, c = w_value.shape
    d = inputs.shape[1]
    p = spatial.shape[0]
    n = counts.shape[0] // n_mp
    quick = n_dp == 8 and r % 16 == 0
    info = counts

    args = in_hbm(w_gate, w_value, w_out.T, bias_value, bias_gate, gate_gain, gate_shift)
    pg, vo1, vec = simple_call(cast_kernel, info, args, [shape((r, c), BF), shape((r, 2 * c), BF), shape((16, c), BF)], "casts")
    if quick:
        zg, zvo = line_swaps([pg] * 3), line_swaps([vo1] * 3)
        zg = stack_call(info, (pg, *zg, vec), (), "line_gate")
        pieces = (zg, *plane_swaps(zg, zg, zg))
    else:
        copies = lambda a: gather_dp(jnp.broadcast_to(a[None], (n_dp,) + a.shape))
        g0 = jnp.concatenate([copies(pg), vec])
        zg = wga = jnp.concatenate([g0, y_swap(g0)], 1)
        vo0 = copies(vo1)
        vo2 = y_swap(vo0)
        zvo = ()
        voa = jnp.concatenate([vo0[:, :c], vo2[:, :c], vo0[:, c:], vo2[:, c:]], 1)
    normed, g_win, gsum = norm_call(info, inputs, cotangent, input_norm_gain, shift_in, n, (zg,))
    if quick:
        wga = assemble_call(info, pieces, 1, 16, (gsum, *zvo), "assemble_gate")
        zvo = stack_call(info, (vo1, *zvo), (wga,), "line_value_out")
        pieces = (zvo, *plane_swaps(zvo, zvo, zvo))
    s, st, sb, token = windows_call(info, spatial, spatial_bias, n, (zvo,) if quick else (gsum,))
    wgb = core_swap(wga)
    rows, hat, slope, inv, shifted, vec = gate_call(info, (wga, wgb), normed, s, sb, (token,))
    if quick:
        *rest, vec = lax.optimization_barrier((*pieces[1:], vec))
        pieces = (pieces[0], *rest)
        swapped = tuple(core_swap(a) for a in pieces)
        voa = assemble_call(info, pieces, 2, 0, (vec,), "assemble_own")
        vob = assemble_call(info, swapped, 2, 0, (voa,), "assemble_other")
    else:
        vob = core_swap(voa)
    zero = jnp.zeros((PAD, PAD), F32)
    prod_b, ds_b, dpv_b, gw_b, gb_b, gsp, small_b = value_call(info, 1, False, vob, normed, g_win, vec, shifted, rows, zero)
    recv_vo = core_swap(gw_b)
    prod_a, ds_a, dpv_a, gw_a, gb_a, gsp, small_a = value_call(info, 0, True, voa, normed, g_win, vec, shifted, rows, gsp)
    q = PAD // 4
    def plane(parts, recv, extra, name, after):
        s = parts.shape[1:]
        return simple_call(lambda *a: plane_kernel(extra, *a), info, (parts, recv), [shape(s, F32), shape(s, BF)], name, after=after)

    def line(part, recv, tensors, chunks, extra, name, after, cores=()):
        s = ((part.shape[0] - extra) // 2 + extra, c)
        return simple_call(lambda *a: line_kernel(tensors, chunks, extra, *a), info, (part, recv, *cores), [shape(s, F32), shape(s, BF)], name, after=after)

    if quick:
        kvo, snd = simple_call(quarter_kernel, info, (gw_a, recv_vo, gsp), [shape((2, 8 * r + q, c), t) for t in (F32, BF)], "quarters_vo")
        got_vo = first_swap(snd)
    dpg, keep_g, send_g, vown = back_call(info, normed, (ds_a, ds_b), hat, slope, inv, st, vec, (wga, wgb), (gb_a, gb_b), (small_a, small_b), gsum, (snd,) if quick else ())
    recv_g = core_swap(send_g)
    token = vown
    if quick:
        rows_g = 8 * r + 2 * VROWS
        kg, snd = simple_call(pair_half_kernel, info, (keep_g, recv_g, vown), [shape((rows_g, c), t) for t in (F32, BF)], "halves_g")
        got_g = z_swap(snd, 1)
        kvo, snd = plane(kvo, got_vo, q, "plane_vo", (snd,))
        got_vo = second_swap(snd)
        token = snd
    res, token = result_call(info, inputs, (prod_a, prod_b), (voa, vob), out_bias, (token,))
    if quick:
        (sp,) = simple_call(spatial_rows_kernel, info, (kvo, got_vo), [shape((q, c), BF)], "spatial_plane", after=(token,))
        kvo, snd = line(kvo, got_vo, 2, 4, q, "line_vo", (), (sp, core_swap(sp)))
        got_vo = z_swap(snd, 1)
        rows_g = 2 * r + VROWS
        kg, snd = simple_call(first_half_kernel, info, (kg, got_g), [shape((2, rows_g, c), t) for t in (F32, BF)], "quarters_g", after=(snd,))
        got_g = first_swap(snd)
        token = snd
    dnv, token = value_part_call(info, (dpv_a, dpv_b), (voa, vob), d, (token,))
    if quick:
        kg, snd = plane(kg, got_g, VROWS, "plane_g", (token,))
        got_g = second_swap(snd)
        kvo, snd = line(kvo, got_vo, 2, 2, q, "pair_vo", (snd,))
        got_vo = z_swap(snd, 2)
        token = snd
    ing, token = grad_call(info, inputs, cotangent, dnv, dpg, (wga, wgb), input_norm_gain, (token,))
    if quick:
        kg, snd = line(kg, got_g, 1, 2, VROWS, "pair_g", (token,))
        got_g = z_swap(snd, 2)
        (sp,) = simple_call(spatial_rows_kernel, info, (kvo, got_vo), [shape((q, c), BF)], "spatial_rows", after=(token,))
        gwv, gwo, token = simple_call(finish_vo_kernel, info, (kvo, got_vo), [shape((r, c), F32)] * 2 + [shape((8, 128), F32)], "finish_vo", after=(sp,))
        sps = plane_swaps(sp, sp, sp)
        one = shape((c,), F32)
        (full,) = simple_call(finish_full_kernel, info, (kg, got_g, input_norm_gain, shift_in), [shape((8, d), F32)], "finish_full", after=(token,))
        gwg, gbv, gbg, ggain, gshift = simple_call(finish_g_kernel, info, (kg, got_g), [shape((r, c), F32)] + [one] * 4, "finish_g", after=(full,))
        gspat, gsb, gin, sin, gob = simple_call(spatial_kernel, info, (sp, *sps, full, core_swap(full)), [shape((p, p), F32), shape((p,), F32)] + [shape((d,), F32)] * 3, "spatial_sum", [pltpu.VMEM((PAD, PAD), F32)])
    else:
        gwv = scatter_any(gw_a[:d], recv_vo[:d])
        gwo = scatter_any(gw_a[d:], recv_vo[d:])
        gwg = scatter_any(keep_g, recv_g[:d])
        gsp = lax.psum(gsp, AXES)
        gspat, gsb = gsp[:p, :p], gsp[:p, WIN]
        other = send_g[d:].astype(F32)
        other = other[:8] + other[8:]
        back = jnp.argsort(jnp.bitwise_xor(jnp.array(ORDER, jnp.int32), me))
        four = jnp.concatenate([vown[:4], other[:4]], 1).reshape(4, n_mp, c)
        four = lax.psum(jnp.take(four, back, axis=1), AXES)
        gbv, gbg, ggain, gshift = lax.dynamic_index_in_dim(four, me, 1, keepdims=False)
        t, sin, gob = lax.psum(vown[4:7, :d], AXES)
        gin = (t - shift_in * sin) / input_norm_gain
    return (res, ing, gin, sin, gwv, gwg, gbv, gbg, ggain, gshift, gspat, gsb, gwo.T, gob)


def solution(mesh):
    row, wi, mp, al = P(("dp", "mp"), None), P("dp", "mp"), P("mp"), P()
    return jax.shard_map(
        body, mesh=mesh,
        in_specs=(row, P("dp"), al, al, wi, wi, mp, mp, mp, mp, al, al, P("mp", "dp"), al, row),
        out_specs=(row, row, al, al, wi, wi, mp, mp, mp, mp, al, al, P("mp", "dp"), al),
        check_vma=False,
    )
```
